32 devices in a mesh: section: 2 (over x), dp: 16 (over z, y, core).
Axes of the slice: x: 2, y: 2, z: 4, core: 2. Of those that a mesh axis runs over, the one named last changes fastest.
Arguments:
- patches_in: bfloat16 [2, 4096, 768], P(None, 'dp'), may hold values from -6 to 6
- grid_rows: int32 [2, 16, 4], P(None, 'dp'), may hold values from 1 to 14, as said below
- grid_cols: int32 [2, 16, 4], P(None, 'dp'), may hold values from 1 to 14
- norm1_gain: float32 [2, 768], P('section'), may hold values from 0.25 to 1.75
- norm1_bias: float32 [2, 768], P('section'), may hold values from -3 to 3
- qkv_weight: bfloat16 [2, 768, 2304], P('section'), may hold values from -0.21875 to 0.21875
- q_bias: float32 [2, 768], P('section'), may hold values from -3 to 3
- v_bias: float32 [2, 768], P('section'), may hold values from -3 to 3
- rel_table: float32 [2, 729, 12], P('section'), may hold values from -6 to 6
- proj_weight: bfloat16 [2, 768, 768], P('section'), may hold values from -0.875 to 0.875
- proj_bias: float32 [2, 768], P('section'), may hold values from -3 to 3
- attn_scale: float32 [2, 768], P('section'), may hold values from 0.25 to 1.75
- norm2_gain: float32 [2, 768], P('section'), may hold values from 0.25 to 1.75
- norm2_bias: float32 [2, 768], P('section'), may hold values from -3 to 3
- fc1_weight: bfloat16 [2, 768, 3072], P('section'), may hold values from -0.21875 to 0.21875
- fc1_bias: float32 [2, 3072], P('section'), may hold values from -3 to 3
- fc2_weight: bfloat16 [2, 3072, 768], P('section'), may hold values from -0.109375 to 0.109375
- fc2_bias: float32 [2, 768], P('section'), may hold values from -3 to 3
- mlp_scale: float32 [2, 768], P('section'), may hold values from 0.25 to 1.75
- cotangent: bfloat16 [2, 4096, 768], P(None, 'dp'), may hold values from -6 to 6
Outputs:
- activations: bfloat16 [2, 2, 4096, 768], P('section', None, 'dp')
- input_grads: float32 [2, 2, 4096, 768], P('section', None, 'dp')
- grad_norm1_gain: float32 [2, 768], P('section')
- grad_norm1_bias: float32 [2, 768], P('section')
- grad_qkv_weight: float32 [2, 768, 2304], P('section', 'dp')
- grad_q_bias: float32 [2, 768], P('section')
- grad_v_bias: float32 [2, 768], P('section')
- grad_rel_table: float32 [2, 729, 12], P('section')
- grad_proj_weight: float32 [2, 768, 768], P('section', 'dp')
- grad_proj_bias: float32 [2, 768], P('section')
- grad_attn_scale: float32 [2, 768], P('section')
- grad_norm2_gain: float32 [2, 768], P('section')
- grad_norm2_bias: float32 [2, 768], P('section')
- grad_fc1_weight: float32 [2, 768, 3072], P('section', 'dp')
- grad_fc1_bias: float32 [2, 3072], P('section')
- grad_fc2_weight: float32 [2, 3072, 768], P('section', 'dp')
- grad_fc2_bias: float32 [2, 768], P('section')
- grad_mlp_scale: float32 [2, 768], P('section')
The draws below stay inside these ranges and needn't reach their ends.
Inputs may be any that keep to these rules, and one draw needn't show every extreme that they name: In every pack the patch counts grid_rows * grid_cols of its 4 images sum to at most 256; exactly one image of each pack has 14 rows, and some pack holds an image of 14 x 14 patches.
All inputs are finite; a program needn't handle non-finite values.
Results may differ from the reference program's by a relative error of at most 0.02.
Values may be sent and summed in bfloat16 or wider, within the bound.
No kernel may reach another device: no remote copies, remote signals or barrier semaphores. Data moves between devices by JAX's collectives and lax.ppermute only.
A program may use at most 256 MiB of HBM per device.

```python
import math
import jax
import jax.numpy as jnp
from jax import lax

D = 768
HEADS = 12
HEAD_DIM = 64
FF = 3072
MB = 2
PACK = 256
SLOTS = 4
GRID = 14
PACKS = 16
TOKENS = 4096
REL = 729


def pack_grids(key):
    pack_count = TOKENS // PACK
    side_most = max(1, math.isqrt((PACK - GRID * GRID) // (SLOTS - 1)))
    keys_all = jax.random.split(key, 5)
    small_rows = jax.random.randint(keys_all[0], (MB, pack_count, SLOTS), 1, side_most + 1, dtype=jnp.int32)
    small_cols = jax.random.randint(keys_all[1], (MB, pack_count, SLOTS), 1, side_most + 1, dtype=jnp.int32)
    big_cols = jax.random.randint(keys_all[2], (MB, pack_count, 1), max(1, GRID // 2), GRID + 1, dtype=jnp.int32)
    chosen = jax.random.randint(keys_all[3], (MB, pack_count, 1), 0, SLOTS, dtype=jnp.int32)
    widest = jax.random.randint(keys_all[4], (), 0, MB * pack_count, dtype=jnp.int32)
    pack_ids = jnp.arange(MB * pack_count, dtype=jnp.int32).reshape(MB, pack_count, 1)
    big_cols = jnp.where(pack_ids == widest, GRID, big_cols)
    slot_ids = jnp.arange(SLOTS, dtype=jnp.int32).reshape(1, 1, SLOTS)
    rows_out = jnp.where(slot_ids == chosen, GRID, small_rows)
    cols_out = jnp.where(slot_ids == chosen, big_cols, small_cols)
    return (rows_out.astype(jnp.int32), cols_out.astype(jnp.int32))


def draw_grid_rows(key, part):
    shared = pack_grids(key)
    return shared[0]


def draw_grid_cols(key, part):
    shared = pack_grids(key)
    return shared[1]


def with_spikes(array, rng, source, target, parts, factor):
    def block_of(axis_at):
        return (jnp.arange(array.shape[axis_at]) // (array.shape[axis_at] // parts)).reshape((-1,) + (1,) * (array.ndim - 1 - axis_at))

    first = jax.random.permutation(rng, parts)[block_of(target)]
    second = (block_of(target) + parts // 2) % parts
    return jnp.where((block_of(source) == first) | (block_of(source) == second), factor * array, array)


def levels(stream_key, dims, pieces, low, high):
    level = 1.0
    for axis_at, parts in pieces:
        steps = jax.random.uniform(jax.random.fold_in(jax.random.fold_in(stream_key, 6), axis_at), (parts,), jnp.float32, low / len(pieces), high / len(pieces))
        level = level * jnp.repeat(jnp.exp(steps), dims[axis_at] // parts).reshape((-1,) + (1,) * (len(dims) - 1 - axis_at))
    return level


def scatter_about(own_key, shape, scale, reach, cuts=(), held_as=jnp.bfloat16):
    loudness = levels(own_key, shape, cuts, -0.22, 0.18) if cuts else 1.0
    drawn = jax.random.normal(own_key, shape, jnp.float32) * scale * loudness
    return jnp.minimum(jnp.maximum(drawn, -reach), reach).astype(held_as)


def gaussian_with(own_key, extent, width, most, cuts, heavy, held_as=jnp.bfloat16):
    drawn = width * jax.random.normal(own_key, extent, jnp.float32)
    if cuts:
        drawn = drawn * levels(own_key, extent, cuts, -0.22, 0.18)
    return jnp.clip(with_spikes(drawn, jax.random.fold_in(own_key, 3), *heavy), -most, most).astype(held_as)


def setup_inputs(seed: int = 0) -> dict:
    key_list = jax.random.split(jax.random.key(seed), 21)
    return {
        "patches_in": gaussian_with(key_list[0], (MB, TOKENS, D), 1.0, 6.0, ((1, 16),), (1, 2, 16, 2.0)),
        "grid_rows": draw_grid_rows(jax.random.fold_in(key_list[20], 71), 0),
        "grid_cols": draw_grid_cols(jax.random.fold_in(key_list[20], 71), 0),
        "norm1_gain": jnp.clip(1.0 + 0.15 * jax.random.normal(key_list[3], (2, D), jnp.float32), 0.25, 1.75),
        "norm1_bias": scatter_about(key_list[4], (2, D), 0.5, 3.0, ((0, 2),), jnp.float32),
        "qkv_weight": scatter_about(key_list[5], (2, D, 3 * D), D ** -0.5, 0.21875, ((0, 2),)),
        "q_bias": scatter_about(key_list[6], (2, D), 0.5, 3.0, ((0, 2),), jnp.float32),
        "v_bias": scatter_about(key_list[7], (2, D), 0.5, 3.0, ((0, 2),), jnp.float32),
        "rel_table": scatter_about(key_list[8], (2, REL, HEADS), 1.0, 6.0, ((0, 2),), jnp.float32),
        "proj_weight": scatter_about(key_list[9], (2, D, D), (D // 16) ** -0.5, 0.875, ((0, 2),)),
        "proj_bias": scatter_about(key_list[10], (2, D), 0.5, 3.0, ((0, 2),), jnp.float32),
        "attn_scale": jnp.clip(1.0 + 0.15 * jax.random.normal(key_list[11], (2, D), jnp.float32), 0.25, 1.75),
        "norm2_gain": jnp.clip(1.0 + 0.15 * jax.random.normal(key_list[12], (2, D), jnp.float32), 0.25, 1.75),
        "norm2_bias": scatter_about(key_list[13], (2, D), 0.5, 3.0, ((0, 2),), jnp.float32),
        "fc1_weight": scatter_about(key_list[14], (2, D, FF), D ** -0.5, 0.21875, ((0, 2),)),
        "fc1_bias": scatter_about(key_list[15], (2, FF), 0.5, 3.0, ((0, 2),), jnp.float32),
        "fc2_weight": scatter_about(key_list[16], (2, FF, D), FF ** -0.5, 0.109375, ((0, 2),)),
        "fc2_bias": scatter_about(key_list[17], (2, D), 0.5, 3.0, ((0, 2),), jnp.float32),
        "mlp_scale": jnp.clip(1.0 + 0.15 * jax.random.normal(key_list[18], (2, D), jnp.float32), 0.25, 1.75),
        "cotangent": gaussian_with(key_list[19], (MB, TOKENS, D), 1.0, 6.0, ((1, 16),), (1, 2, 16, 2.0)),
    }


@jax.custom_vjp
def low(v):
    return lax.optimization_barrier(v.astype(jnp.bfloat16)).astype(jnp.float32)

@jax.custom_vjp
def low_back(v):
    return v

def low_keep(v):
    return (low(v), None)

def low_pass(kept, grad):
    return (grad,)

def back_keep(v):
    return (v, None)

def back_low(kept, grad):
    return (low(grad),)
low.defvjp(low_keep, low_pass)
low_back.defvjp(back_keep, back_low)
EPS = 1e-06
NEG = -1000000000.0

def matmul_hi(left_op, right_op):
    return jnp.dot(left_op, right_op, precision=lax.Precision.HIGHEST)

def pack_layout(rows_of, cols_of, length):
    patches = rows_of * cols_of
    image_end = jnp.cumsum(patches).astype(jnp.int32)
    image_start = image_end - patches
    places = jnp.arange(length, dtype=jnp.int32)
    owner_of = lax.optimization_barrier(jnp.sum((places[:, None] >= image_end[None, :]).astype(jnp.int32), axis=1))
    member = (owner_of[:, None] == jnp.arange(SLOTS, dtype=jnp.int32)[None, :]).astype(jnp.int32)
    start_of = lax.optimization_barrier(jnp.sum(member * image_start[None, :], axis=1))
    breadth = jnp.maximum(lax.optimization_barrier(jnp.sum(member * cols_of[None, :], axis=1)), 1)
    inside = owner_of < SLOTS
    offset = jnp.where(inside, places - start_of, 0)
    patch_row = offset // breadth
    patch_col = offset - patch_row * breadth
    stride_rel = 2 * GRID - 1
    rel_index = (patch_row[:, None] - patch_row[None, :] + GRID - 1) * stride_rel + (patch_col[:, None] - patch_col[None, :] + GRID - 1)
    same_image = owner_of[:, None] == owner_of[None, :]
    return (rel_index.astype(jnp.int32), same_image, inside)

def normed(values, gain, shift):
    center = values - lax.optimization_barrier(jnp.mean(values, axis=-1, keepdims=True))
    spread = lax.optimization_barrier(jnp.mean(center * center, axis=-1, keepdims=True))
    return center * lax.rsqrt(spread + EPS) * gain + shift

def layer(inputs, params, rel_index, same_image):
    n1_gain, n1_shift, qkv_w, query_bias, value_bias, bias_table, proj_w, proj_shift, attn_gain, n2_gain, n2_shift, up_w, up_shift, down_w, down_shift, mlp_gain = params
    length = inputs.shape[0]
    hidden = low(normed(inputs, n1_gain, n1_shift))
    packed = matmul_hi(hidden, qkv_w)
    queries = low_back(low(packed[:, :D] + query_bias)).reshape(length, HEADS, HEAD_DIM)
    keys_all = low_back(low(packed[:, D:2 * D])).reshape(length, HEADS, HEAD_DIM)
    values_all = low_back(low(packed[:, 2 * D:] + value_bias)).reshape(length, HEADS, HEAD_DIM)
    bias_all = jnp.transpose(jnp.take(bias_table, rel_index, axis=0), (2, 0, 1))
    scores = jnp.einsum('qhd,khd->hqk', queries, keys_all, precision=lax.Precision.HIGHEST) * HEAD_DIM ** (-0.5) + bias_all
    scores = low_back(jnp.where(same_image[None], scores, NEG))
    weights = low(jax.nn.softmax(scores, axis=-1))
    mixed_heads = jnp.einsum('hqk,khd->qhd', weights, values_all, precision=lax.Precision.HIGHEST)
    mixed_heads = low_back(low(mixed_heads.reshape(length, D)))
    branch = low_back(matmul_hi(mixed_heads, proj_w) + proj_shift)
    middle = inputs + attn_gain * branch
    second = low(normed(middle, n2_gain, n2_shift))
    upward = low_back(matmul_hi(second, up_w) + up_shift)
    activated = low(jax.nn.gelu(upward, approximate=False))
    downward = low_back(matmul_hi(activated, down_w) + down_shift)
    return middle + mlp_gain * downward

def add_up(first_term, second_term):
    return first_term + second_term

def reference(patches_in, grid_rows, grid_cols, norm1_gain, norm1_bias, qkv_weight, q_bias, v_bias, rel_table, proj_weight, proj_bias, attn_scale, norm2_gain, norm2_bias, fc1_weight, fc1_bias, fc2_weight, fc2_bias, mlp_scale, cotangent):
    params = tuple((entry.astype(jnp.float32) for entry in (norm1_gain, norm1_bias, qkv_weight, q_bias, v_bias, rel_table, proj_weight, proj_bias, attn_scale, norm2_gain, norm2_bias, fc1_weight, fc1_bias, fc2_weight, fc2_bias, mlp_scale)))
    pack_count = MB * PACKS
    inputs_all = patches_in.reshape(pack_count, PACK, D)
    cots_all = cotangent.reshape(pack_count, PACK, D)
    rows_all = grid_rows.reshape(pack_count, SLOTS)
    cols_all = grid_cols.reshape(pack_count, SLOTS)

    def visit_pack(totals, pack_item):
        block_in, block_cot, rows_of, cols_of = pack_item
        rel_index, same_image, inside = pack_layout(rows_of, cols_of, PACK)

        def forward(source, probe_zero, weights_all):
            first_layer = tuple((entry[0] for entry in weights_all))
            second_layer = tuple((entry[1] for entry in weights_all))
            mid_out = layer(source, first_layer, rel_index, same_image)
            final = layer(low_back(low(mid_out)) + probe_zero, second_layer, rel_index, same_image)
            return (mid_out, final)
        source = block_in.astype(jnp.float32)
        probe_zero = jnp.zeros((PACK, D), jnp.float32)
        (mid_out, final), pullback = jax.vjp(forward, source, probe_zero, params)
        out_grad = block_cot.astype(jnp.float32) * inside[:, None].astype(jnp.float32)
        grad_source, grad_probe, grad_params = pullback((jnp.zeros_like(mid_out), out_grad))
        totals = jax.tree.map(add_up, totals, grad_params)
        return (totals, (mid_out.astype(jnp.bfloat16), final.astype(jnp.bfloat16), grad_source, grad_probe))
    start = tuple((jnp.zeros_like(entry) for entry in params))
    totals, (mids, finals, grads_in, grads_mid) = lax.scan(visit_pack, start, (inputs_all, cots_all, rows_all, cols_all))
    activations = jnp.stack([mids.reshape(MB, TOKENS, D), finals.reshape(MB, TOKENS, D)])
    input_grads = jnp.stack([grads_in.reshape(MB, TOKENS, D), grads_mid.reshape(MB, TOKENS, D)])
    return (activations, input_grads, totals[0], totals[1], totals[2], totals[3], totals[4], totals[5], totals[6], totals[7], totals[8], totals[9], totals[10], totals[11], totals[12], totals[13], totals[14], totals[15])
```

```python
import functools

import jax
import jax.numpy as jnp
from jax import lax
from jax.experimental import pallas as pl
from jax.experimental.pallas import tpu as pltpu
from jax.sharding import PartitionSpec as P

SLOTS = 4
GRID = 14
SPAN = 2 * GRID - 1
CODE = 16
PLACES = GRID * CODE
WIDE = 512
EPS = 1e-06
NEG = -1000000000.0
F32 = jnp.float32
BF16 = jnp.bfloat16
VMEM_BYTES = 56 * 1024 * 1024

NN = (((1,), (0,)), ((), ()))
NT = (((1,), (1,)), ((), ()))
TN = (((0,), (0,)), ((), ()))


def mm(left, right, dims=NN):
    return lax.dot_general(left, right, dims, preferred_element_type=F32)


def ramp(shape, axis):
    return lax.broadcasted_iota(jnp.int32, shape, axis)


def pack_places(rows_ref, cols_ref, mb, shape, axis):
    places = ramp(shape, axis)
    owner = jnp.zeros(shape, jnp.int32)
    start = jnp.zeros(shape, jnp.int32)
    breadth = jnp.ones(shape, jnp.int32)
    end = jnp.int32(0)
    for slot in range(SLOTS):
        cols = cols_ref[mb, 0, slot]
        here = places >= end
        start = jnp.where(here, end, start)
        breadth = jnp.where(here, cols, breadth)
        end = end + rows_ref[mb, 0, slot] * cols
        owner = owner + (places >= end).astype(jnp.int32)
    inside = places < end
    offset = (places - start).astype(F32)
    row = jnp.floor((offset + 0.5) / breadth.astype(F32)).astype(jnp.int32)
    col = places - start - row * breadth
    code = jnp.where(inside, row * CODE + col, 0)
    return owner, code, inside


def onehot(ids, shape, axis):
    return jnp.where(ids == ramp(shape, axis), 1.0, 0.0).astype(BF16)


def unit_rows(values):
    center = values - jnp.mean(values, axis=-1, keepdims=True)
    inverse = lax.rsqrt(jnp.mean(center * center, axis=-1, keepdims=True) + EPS)
    return center * inverse, inverse


def norm_back(grad_hat, hat, inverse):
    centered = grad_hat - jnp.mean(grad_hat, axis=-1, keepdims=True)
    return inverse * (centered - hat * jnp.mean(grad_hat * hat, axis=-1, keepdims=True))


def normal_parts(u):
    t = 1.0 / (1.0 + (0.3275911 * 0.7071067811865476) * jnp.abs(u))
    falling = jnp.exp(-0.5 * u * u)
    poly = t * (
        0.254829592
        + t * (-0.284496736 + t * (1.421413741 + t * (-1.453152027 + t * 1.061405429)))
    )
    tail = 0.5 * poly * falling
    return jnp.where(u < 0.0, tail, 1.0 - tail), u * falling * 0.3989422804014327


def spread_map(shape, flat_axis, wide_axis):
    flat = ramp(shape, flat_axis)
    wide = ramp(shape, wide_axis)
    row = wide // CODE
    col = wide - row * CODE
    meets = (flat == row * SPAN + col) & (col < GRID) & (row < SPAN)
    return jnp.where(meets, 1.0, 0.0).astype(BF16)


def split_two(values):
    high = values.astype(BF16)
    return high, (values - high.astype(F32)).astype(BF16)


def table_kernel(rev_ref, out_ref, wide_ref):
    heads = out_ref.shape[1]
    rev = rev_ref[...]
    height, flat = rev.shape
    turned = jnp.concatenate(
        [pltpu.roll(rev, (c - (GRID - 1)) % flat, 1) for c in range(CODE)], axis=0
    )
    spread = spread_map((flat, WIDE), 0, 1)
    for part, piece in enumerate(split_two(turned)):
        wide = mm(piece, spread)
        for at in range(WIDE // 128):
            wide_ref[at] = wide[:, at * 128 : (at + 1) * 128]

        def one_head(h, carry):
            block = jnp.concatenate(
                [
                    wide_ref[at, pl.ds(h, CODE, stride=height), :]
                    for at in range(WIDE // 128)
                ],
                axis=1,
            )
            keep = ramp((CODE, 256), 1) < PLACES
            for r in range(GRID):
                moved = pltpu.roll(block, (WIDE - CODE * (GRID - 1 - r)) % WIDE, 1)
                out_ref[part, h, r * CODE : (r + 1) * CODE, :] = jnp.where(
                    keep, moved[:, :256], 0.0
                ).astype(BF16)
            return carry

        lax.fori_loop(0, heads, one_head, 0)


def table_matrices(rel_table):
    rel, heads = rel_table.shape
    flat = -(-rel // 128) * 128
    height = -(-heads // 8) * 8
    rev = jnp.pad(jnp.flip(rel_table, 0).T, ((0, height - heads), (0, flat - rel)))
    return pl.pallas_call(
        table_kernel,
        out_shape=jax.ShapeDtypeStruct((2, heads, PLACES, 256), BF16),
        scratch_shapes=[pltpu.VMEM((WIDE // 128, CODE * height, 128), F32)],
        compiler_params=pltpu.CompilerParams(vmem_limit_bytes=VMEM_BYTES),
        name="table_matrices",
    )(rev)


def table_grad_kernel(
    sec_ref, rows_ref, cols_ref, ds0_ref, ds1_ref, ds2_ref, out_ref, ds_scr, wide_ref, sem
):
    sec = sec_ref[0]
    heads, length, _ = ds0_ref.shape
    height, flat = out_ref.shape
    spread = spread_map((WIDE, flat), 1, 0)

    @pl.when(sec == 0)
    def _():
        pltpu.make_async_copy(ds2_ref, ds_scr.at[0], sem.at[0]).start()

    @pl.when(sec != 0)
    def _():
        pltpu.make_async_copy(ds0_ref, ds_scr.at[0], sem.at[0]).start()

    other = pltpu.make_async_copy(ds1_ref, ds_scr.at[1], sem.at[1])
    other.start()
    wide_ref[...] = jnp.zeros_like(wide_ref)
    sides = []
    for which in range(2):
        mb = sec if which == 0 else 1 - sec
        _, code_col, _ = pack_places(rows_ref, cols_ref, mb, (length, 1), 0)
        _, code_row, _ = pack_places(rows_ref, cols_ref, mb, (1, length), 1)
        sides.append(
            (onehot(code_col, (length, 256), 1), onehot(code_row, (256, length), 0))
        )
    pltpu.make_async_copy(ds0_ref, ds_scr.at[0], sem.at[0]).wait()
    other.wait()

    def one_head(h, carry):
        total = jnp.zeros((256, 256), F32)
        for which, (place_col, place_row) in enumerate(sides):
            keyed = mm(ds_scr[which, h], place_col).astype(BF16)
            total = total + mm(place_row, keyed)
        acc = jnp.zeros((CODE, WIDE), F32)
        for r in range(GRID):
            block = jnp.concatenate(
                [total[r * CODE : (r + 1) * CODE, :], jnp.zeros((CODE, WIDE - 256), F32)],
                axis=1,
            )
            acc = acc + pltpu.roll(block, CODE * (GRID - 1 - r), 1)
        for at in range(WIDE // 128):
            wide_ref[at, pl.ds(h, CODE, stride=height), :] = acc[:, at * 128 : (at + 1) * 128]
        return carry

    lax.fori_loop(0, heads, one_head, 0)
    high, rest = split_two(
        jnp.concatenate([wide_ref[at] for at in range(WIDE // 128)], axis=1)
    )
    turned = mm(high, spread) + mm(rest, spread)
    result = jnp.zeros((height, flat), F32)
    for c in range(GRID):
        result = result + pltpu.roll(
            turned[c * height : (c + 1) * height, :], GRID - 1 - c, 1
        )
    out_ref[...] = result


def table_grad(sec, grid_rows, grid_cols, score_grads, rel):
    heads, length, _ = score_grads[0].shape
    flat = -(-rel // 128) * 128
    height = -(-heads // 8) * 8
    smem = pl.BlockSpec(memory_space=pltpu.SMEM)
    hbm = pl.BlockSpec(memory_space=pl.ANY)
    rev = pl.pallas_call(
        table_grad_kernel,
        out_shape=jax.ShapeDtypeStruct((height, flat), F32),
        in_specs=[smem] * 3 + [hbm] * 3,
        scratch_shapes=[
            pltpu.VMEM((2, heads, length, length), BF16),
            pltpu.VMEM((WIDE // 128, CODE * height, 128), F32),
            pltpu.SemaphoreType.DMA((2,)),
        ],
        compiler_params=pltpu.CompilerParams(vmem_limit_bytes=VMEM_BYTES),
        name="table_grad",
    )(sec, grid_rows, grid_cols, *score_grads)
    return rev


def forward_kernel(
    slot,
    micro_count,
    sec_ref,
    rows_ref,
    cols_ref,
    own_ref,
    inc_ref,
    n1_gain,
    n1_shift,
    query_bias,
    value_bias,
    proj_shift,
    attn_gain,
    n2_gain,
    n2_shift,
    up_shift,
    down_shift,
    mlp_gain,
    table_hbm,
    qkv_hbm,
    proj_hbm,
    up_hbm,
    down_hbm,
    x_out,
    h_out,
    p_out,
    wt_out,
    o_out,
    br_out,
    m_out,
    h2_out,
    dg_out,
    z_out,
    fd_out,
    y_out,
    x_scr,
    table_scr,
    qkv_w,
    proj_w,
    up_w,
    down_w,
    h_scr,
    p_scr,
    wt_scr,
    o_scr,
    br_scr,
    m_scr,
    h2_scr,
    dg_scr,
    z_scr,
    fd_scr,
    y_scr,
    hi_scr,
    lo_scr,
    in_sem,
    out_sem,
):
    length, width = x_scr.shape
    heads = wt_scr.shape[0]
    hidden = z_scr.shape[1]
    head_dim = width // heads
    pair = 2 * head_dim
    sec = sec_ref[0]
    mb = jnp.clip(slot - sec, 0, micro_count - 1)

    x_copy = pltpu.make_async_copy(own_ref.at[mb], x_scr, in_sem.at[0])
    if slot == 0:
        x_copy.start()
    else:

        @pl.when(sec == 0)
        def _():
            x_copy.start()

        @pl.when(sec != 0)
        def _():
            pltpu.make_async_copy(inc_ref, x_scr, in_sem.at[0]).start()

    loads = []
    for place, (src, dst) in enumerate(
        (
            (qkv_hbm.at[0], qkv_w),
            (table_hbm, table_scr),
            (proj_hbm.at[0], proj_w),
            (up_hbm.at[0], up_w),
            (down_hbm.at[0], down_w),
        )
    ):
        load = pltpu.make_async_copy(src, dst, in_sem.at[1 + place])
        load.start()
        loads.append(load)
    stores = []

    def keep(src, dst):
        store = pltpu.make_async_copy(src, dst, out_sem.at[len(stores)])
        store.start()
        stores.append(store)

    owner_col, code_col, _ = pack_places(rows_ref, cols_ref, mb, (length, 1), 0)
    owner_row, code_row, _ = pack_places(rows_ref, cols_ref, mb, (1, length), 1)
    lanes = ramp((length, 256), 1)
    place_col = jnp.where(
        (lanes == code_col) | (lanes == owner_col + PLACES), 1.0, 0.0
    ).astype(BF16)
    place_row = onehot(code_row, (256, length), 0)
    spare = ramp((256 - PLACES, length), 0)
    hi_scr[:, PLACES:, :] = jnp.broadcast_to(
        jnp.where(spare == owner_row, 0.0, NEG).astype(BF16)[None],
        (2, 256 - PLACES, length),
    )
    lo_scr[:, PLACES:, :] = jnp.zeros((2, 256 - PLACES, length), BF16)

    x_copy.wait()
    keep(x_scr, x_out)
    inputs = x_scr[...].astype(F32)
    hat, _ = unit_rows(inputs)
    h_scr[...] = (hat * n1_gain[...] + n1_shift[...]).astype(BF16)
    keep(h_scr, h_out)

    loads[0].wait()
    scale = head_dim ** (-0.5)
    h_all = h_scr[...]
    p_scr[:, :width] = (
        (mm(h_all, qkv_w[:, :width]) + query_bias[...]).astype(BF16) * scale
    ).astype(BF16)
    p_scr[:, width : 2 * width] = mm(h_all, qkv_w[:, width : 2 * width]).astype(BF16)
    p_scr[:, 2 * width :] = (mm(h_all, qkv_w[:, 2 * width :]) + value_bias[...]).astype(BF16)
    keep(p_scr, p_out)

    loads[1].wait()
    first = ramp((length, pair), 1) < head_dim
    zero = jnp.zeros((length, pair), BF16)

    def attend(j, carry):
        at = pl.multiple_of(j * pair, pair)
        queries = p_scr[:, pl.ds(at, pair)]
        keys_all = p_scr[:, pl.ds(width + at, pair)]
        values_all = p_scr[:, pl.ds(2 * width + at, pair)]
        mixed = []
        for side in range(2):
            head = 2 * j + side
            hi_scr[side, :PLACES, :] = mm(table_scr[0, head], place_row).astype(BF16)
            lo_scr[side, :PLACES, :] = mm(table_scr[1, head], place_row).astype(BF16)
            own = jnp.where(first, queries, zero) if side == 0 else jnp.where(first, zero, queries)
            scores = (
                mm(own, keys_all, NT)
                + mm(place_col, hi_scr[side])
                + mm(place_col, lo_scr[side])
            )
            raised = jnp.exp(scores - jnp.max(scores, axis=-1, keepdims=True))
            share = 1.0 / jnp.sum(raised, axis=-1, keepdims=True)
            weights = (raised * share).astype(BF16)
            wt_scr[head] = weights
            mixed.append(mm(weights, values_all))
        o_scr[:, pl.ds(at, pair)] = jnp.where(first, mixed[0], mixed[1]).astype(BF16)
        return carry

    lax.fori_loop(0, heads // 2, attend, 0)
    keep(wt_scr, wt_out)
    keep(o_scr, o_out)

    loads[2].wait()
    branch = mm(o_scr[...], proj_w[...]) + proj_shift[...]
    br_scr[...] = branch.astype(BF16)
    keep(br_scr, br_out)
    middle = inputs + attn_gain[...] * branch
    m_scr[...] = middle
    keep(m_scr, m_out)
    hat, _ = unit_rows(middle)
    h2_scr[...] = (hat * n2_gain[...] + n2_shift[...]).astype(BF16)
    keep(h2_scr, h2_out)

    loads[3].wait()
    loads[4].wait()
    second = h2_scr[...]
    tile = width
    down = None
    for at in range(0, hidden, tile):
        upward = mm(second, up_w[:, at : at + tile]) + up_shift[:, at : at + tile]
        cdf, leaning = normal_parts(upward)
        z = (upward * cdf).astype(BF16)
        z_scr[:, at : at + tile] = z
        dg_scr[:, at : at + tile] = (cdf + leaning).astype(BF16)
        term = mm(z, down_w[at : at + tile, :])
        down = term if down is None else down + term
    keep(z_scr, z_out)
    keep(dg_scr, dg_out)
    downward = down + down_shift[...]
    y_scr[...] = (m_scr[...] + mlp_gain[...] * downward).astype(BF16)
    keep(y_scr, y_out)
    fd_scr[...] = downward.astype(BF16)
    keep(fd_scr, fd_out)
    for store in stores:
        store.wait()


def layer_forward(slot, micro_count, sec, grid_rows, grid_cols, own, incoming, vectors, table, weights):
    _, length, width = own.shape
    hidden = weights[2].shape[2]
    heads = table.shape[1]
    smem = pl.BlockSpec(memory_space=pltpu.SMEM)
    vmem = pl.BlockSpec(memory_space=pltpu.VMEM)
    hbm = pl.BlockSpec(memory_space=pl.ANY)
    results = (
        ((length, width), BF16),
        ((length, width), BF16),
        ((length, 3 * width), BF16),
        ((heads, length, length), BF16),
        ((length, width), BF16),
        ((length, width), BF16),
        ((length, width), F32),
        ((length, width), BF16),
        ((length, hidden), BF16),
        ((length, hidden), BF16),
        ((length, width), BF16),
        ((length, width), BF16),
    )
    scratch = [
        pltpu.VMEM((length, width), BF16),
        pltpu.VMEM(table.shape, BF16),
        pltpu.VMEM(weights[0].shape[1:], BF16),
        pltpu.VMEM(weights[1].shape[1:], BF16),
        pltpu.VMEM(weights[2].shape[1:], BF16),
        pltpu.VMEM(weights[3].shape[1:], BF16),
    ]
    scratch += [pltpu.VMEM(shape, dtype) for shape, dtype in results[1:]]
    scratch += [
        pltpu.VMEM((2, 256, length), BF16),
        pltpu.VMEM((2, 256, length), BF16),
        pltpu.SemaphoreType.DMA((6,)),
        pltpu.SemaphoreType.DMA((len(results),)),
    ]
    return pl.pallas_call(
        functools.partial(forward_kernel, slot, micro_count),
        out_shape=[jax.ShapeDtypeStruct(shape, dtype) for shape, dtype in results],
        in_specs=[smem] * 3 + [hbm] * 2 + [vmem] * len(vectors) + [hbm] * 5,
        out_specs=[hbm] * len(results),
        scratch_shapes=scratch,
        compiler_params=pltpu.CompilerParams(vmem_limit_bytes=VMEM_BYTES),
        name="layer_forward",
    )(sec, grid_rows, grid_cols, own, incoming, *vectors, table, *weights)


SUM_ROWS = 16


def backward_kernel(
    moment,
    micro_count,
    sec_ref,
    rows_ref,
    cols_ref,
    cot_ref,
    ret_ref,
    n1_gain,
    attn_gain,
    n2_gain,
    mlp_gain,
    prior_ref,
    down_hbm,
    up_hbm,
    proj_hbm,
    qkv_hbm,
    fd_hbm,
    dg_hbm,
    m_hbm,
    br_hbm,
    p_hbm,
    wt_hbm,
    x_hbm,
    df_out,
    du_out,
    db_out,
    ds_out,
    dp_out,
    dx_out,
    dxb_out,
    sums_out,
    g_scr,
    down_w,
    up_w,
    proj_w,
    qkv_w,
    fd_scr,
    dg_scr,
    m_scr,
    br_scr,
    p_scr,
    wt_scr,
    x_scr,
    df_scr,
    du_scr,
    db_scr,
    ds_scr,
    dp_scr,
    dx_scr,
    dxb_scr,
    do_scr,
    in_sem,
    out_sem,
):
    length, width = g_scr.shape
    heads = wt_scr.shape[0]
    hidden = dg_scr.shape[1]
    head_dim = width // heads
    pair = 2 * head_dim
    sec = sec_ref[0]
    order = micro_count - moment - sec
    mb = jnp.clip(order, 0, micro_count - 1)
    active = ((order >= 0) & (order < micro_count)).astype(F32)

    cot_copy = pltpu.make_async_copy(cot_ref.at[mb], g_scr, in_sem.at[0])
    if moment == 0:
        cot_copy.start()
    else:

        @pl.when(sec != 0)
        def _():
            cot_copy.start()

        @pl.when(sec == 0)
        def _():
            pltpu.make_async_copy(ret_ref, g_scr, in_sem.at[0]).start()

    loads = []
    for place, (src, dst) in enumerate(
        (
            (fd_hbm, fd_scr),
            (down_hbm.at[0], down_w),
            (dg_hbm, dg_scr),
            (up_hbm.at[0], up_w),
            (m_hbm, m_scr),
            (br_hbm, br_scr),
            (proj_hbm.at[0], proj_w),
            (p_hbm, p_scr),
            (wt_hbm, wt_scr),
            (qkv_hbm.at[0], qkv_w),
            (x_hbm, x_scr),
        )
    ):
        load = pltpu.make_async_copy(src, dst, in_sem.at[1 + place])
        load.start()
        loads.append(load)
    stores = []

    def keep(src, dst):
        store = pltpu.make_async_copy(src, dst, out_sem.at[len(stores)])
        store.start()
        stores.append(store)

    def total(values):
        return jnp.sum(values, axis=0, keepdims=True)

    def note(row, values):
        if moment == 0:
            sums_out[row : row + 1, :] = values
        else:
            sums_out[row : row + 1, :] = prior_ref[row : row + 1, :] + values

    _, _, inside = pack_places(rows_ref, cols_ref, mb, (length, 1), 0)
    kept = jnp.where(inside | (sec == 0), active, 0.0)

    cot_copy.wait()
    grad_out = g_scr[...].astype(F32) * kept
    loads[0].wait()
    note(9, total(grad_out * fd_scr[...].astype(F32)))
    df = (grad_out * mlp_gain[...]).astype(BF16)
    df_scr[...] = df
    keep(df_scr, df_out)
    note(8, total(df.astype(F32)))

    loads[1].wait()
    loads[2].wait()
    loads[3].wait()
    tile = width
    dh2 = None
    for at in range(0, hidden, tile):
        dz = mm(df_scr[...], down_w[at : at + tile, :], NT)
        du = (dz * dg_scr[:, at : at + tile].astype(F32)).astype(BF16)
        du_scr[:, at : at + tile] = du
        note(10 + at // tile, total(du.astype(F32)))
        term = mm(du, up_w[:, at : at + tile], NT)
        dh2 = term if dh2 is None else dh2 + term
    keep(du_scr, du_out)
    for row in range(10 + hidden // tile, SUM_ROWS):
        sums_out[row : row + 1, :] = jnp.zeros((1, width), F32)

    loads[4].wait()
    hat, inverse = unit_rows(m_scr[...])
    note(6, total(dh2 * hat))
    note(7, total(dh2))
    dm = g_scr[...].astype(F32) * kept + norm_back(dh2 * n2_gain[...], hat, inverse)
    dx_scr[...] = dm
    loads[5].wait()
    note(5, total(dm * br_scr[...].astype(F32)))
    db = (dm * attn_gain[...]).astype(BF16)
    db_scr[...] = db
    keep(db_scr, db_out)
    note(4, total(db.astype(F32)))
    loads[6].wait()
    do_scr[...] = mm(db, proj_w[...], NT).astype(BF16)

    loads[7].wait()
    loads[8].wait()
    first = ramp((length, pair), 1) < head_dim
    zero = jnp.zeros((length, pair), BF16)
    scale = head_dim ** (-0.5)

    def halves(block):
        return jnp.where(first, block, zero), jnp.where(first, zero, block)

    def attend(j, carry):
        at = pl.multiple_of(j * pair, pair)
        queries = p_scr[:, pl.ds(at, pair)]
        keys_all = p_scr[:, pl.ds(width + at, pair)]
        values_all = p_scr[:, pl.ds(2 * width + at, pair)]
        dout = do_scr[:, pl.ds(at, pair)]
        dq, dk, dv = [], [], []
        for side, own in enumerate(halves(dout)):
            head = 2 * j + side
            weights = wt_scr[head]
            dwt = mm(own, values_all, NT)
            probs = weights.astype(F32)
            inner = jnp.sum(probs * dwt, axis=-1, keepdims=True)
            ds = (probs * (dwt - inner)).astype(BF16)
            ds_scr[head] = ds
            dv.append(mm(weights, dout, TN))
            dq.append(mm(ds, keys_all))
            dk.append(mm(ds, queries, TN))
        dq_all = (jnp.where(first, dq[0], dq[1]) * scale).astype(BF16)
        dk_all = jnp.where(first, dk[0], dk[1]).astype(BF16)
        dv_all = jnp.where(first, dv[0], dv[1]).astype(BF16)
        dp_scr[:, pl.ds(at, pair)] = dq_all
        dp_scr[:, pl.ds(width + at, pair)] = dk_all
        dp_scr[:, pl.ds(2 * width + at, pair)] = dv_all
        return carry

    lax.fori_loop(0, heads // 2, attend, 0)
    keep(ds_scr, ds_out)
    keep(dp_scr, dp_out)

    loads[9].wait()
    dh = mm(dp_scr[...], qkv_w[...], NT)
    loads[10].wait()
    hat, inverse = unit_rows(x_scr[...].astype(F32))
    dx = dx_scr[...] + norm_back(dh * n1_gain[...], hat, inverse)
    dxb_scr[...] = dx.astype(BF16)
    keep(dxb_scr, dxb_out)
    dx_scr[...] = dx
    keep(dx_scr, dx_out)
    note(0, total(dh * hat))
    note(1, total(dh))
    note(2, total(dp_scr[:, :width].astype(F32)))
    note(3, total(dp_scr[:, 2 * width :].astype(F32)))
    for store in stores:
        store.wait()


def layer_backward(
    moment, micro_count, sec, grid_rows, grid_cols, cotangent, returning, vectors, prior, weights, cache
):
    x, _, p, wt, _, br, m, _, dg, _, fd, _ = cache
    length, width = x.shape
    hidden = dg.shape[1]
    heads = wt.shape[0]
    qkv_weight, proj_weight, up_weight, down_weight = weights
    smem = pl.BlockSpec(memory_space=pltpu.SMEM)
    vmem = pl.BlockSpec(memory_space=pltpu.VMEM)
    hbm = pl.BlockSpec(memory_space=pl.ANY)
    results = (
        ((length, width), BF16),
        ((length, hidden), BF16),
        ((length, width), BF16),
        ((heads, length, length), BF16),
        ((length, 3 * width), BF16),
        ((length, width), F32),
        ((length, width), BF16),
    )
    scratch = [
        pltpu.VMEM((length, width), BF16),
        pltpu.VMEM(down_weight.shape[1:], BF16),
        pltpu.VMEM(up_weight.shape[1:], BF16),
        pltpu.VMEM(proj_weight.shape[1:], BF16),
        pltpu.VMEM(qkv_weight.shape[1:], BF16),
    ]
    scratch += [pltpu.VMEM(entry.shape, entry.dtype) for entry in (fd, dg, m, br, p, wt, x)]
    scratch += [pltpu.VMEM(shape, dtype) for shape, dtype in results]
    scratch += [
        pltpu.VMEM((length, width), BF16),
        pltpu.SemaphoreType.DMA((12,)),
        pltpu.SemaphoreType.DMA((len(results),)),
    ]
    return pl.pallas_call(
        functools.partial(backward_kernel, moment, micro_count),
        out_shape=[jax.ShapeDtypeStruct(shape, dtype) for shape, dtype in results]
        + [jax.ShapeDtypeStruct((SUM_ROWS, width), F32)],
        in_specs=[smem] * 3 + [hbm] * 2 + [vmem] * 5 + [hbm] * 11,
        out_specs=[hbm] * len(results) + [vmem],
        scratch_shapes=scratch,
        compiler_params=pltpu.CompilerParams(vmem_limit_bytes=VMEM_BYTES),
        name="layer_backward",
    )(
        sec,
        grid_rows,
        grid_cols,
        cotangent,
        returning,
        *vectors,
        prior,
        down_weight,
        up_weight,
        proj_weight,
        qkv_weight,
        fd,
        dg,
        m,
        br,
        p,
        wt,
        x,
    )


def weight_kernel(parts, chunk_count, sec_ref, *refs):
    sec = sec_ref[0]
    core = sec_ref[1]
    operands, refs = refs[: 6 * parts], refs[6 * parts :]
    (send_out, keep_out), refs = refs[:2], refs[2:]
    lefts, refs = refs[:parts], refs[parts:]
    rights, refs = refs[:parts], refs[parts:]
    turned, refs = refs[:parts], refs[parts:]
    in_sem = refs[0]
    places, _, rows, _ = send_out.shape[0], *send_out.shape[1:]
    length = operands[0].shape[0]
    waits = []
    for part in range(parts):
        six = operands[6 * part : 6 * part + 6]
        for kind, (three, scr) in enumerate(
            ((six[:3], lefts[part]), (six[3:], rights[part]))
        ):
            sems = [in_sem.at[part, kind, which] for which in range(2)]
            top = scr.at[pl.ds(0, length)]
            low = scr.at[pl.ds(length, length)]
            early = pltpu.make_async_copy(three[0], top, sems[0])
            late = pltpu.make_async_copy(three[2], top, sems[0])
            pl.when(sec == 0)(early.start)
            pl.when(sec != 0)(late.start)
            shared = pltpu.make_async_copy(three[1], low, sems[1])
            shared.start()
            waits.append((early, shared))
    at_col = 0
    for part in range(parts):
        for both in waits[2 * part : 2 * part + 2]:
            for copy in both:
                copy.wait()
        depth, width = lefts[part].shape
        step = width // chunk_count
        strip = 256 if width % 256 == 0 else width
        flipped = jnp.concatenate(
            [lefts[part][:, at : at + strip].T for at in range(0, width, strip)], axis=0
        )
        for chunk in range(chunk_count):
            core_of, y, z = chunk % 2, (chunk // 2) % 2, chunk // 4
            to = (y * (chunk_count // 4) + z) * step
            turned[part][core_of, to : to + step, :] = flipped[
                chunk * step : (chunk + 1) * step, :
            ]
        cols = rights[part].shape[1]
        for out, half in ((send_out, 1 - core), (keep_out, core)):
            for y in range(2):
                rows_here = turned[part][half, pl.ds(y * (width // 4), width // 4), :]
                for at in range(0, cols, 768):
                    tile = min(768, cols - at)
                    term = mm(rows_here, rights[part][:, at : at + tile])
                    out[y, :, :, at_col + at : at_col + at + tile] = term.astype(
                        BF16
                    ).reshape(chunk_count // 4, step, tile)
        at_col += cols


def weight_terms(sec_core, chunk_count, pairs):
    hbm = pl.BlockSpec(memory_space=pl.ANY)
    vmem = pl.BlockSpec(memory_space=pltpu.VMEM)
    smem = pl.BlockSpec(memory_space=pltpu.SMEM)
    length, width = pairs[0][0][0].shape
    cols = [right[0].shape[1] for _, right in pairs]
    out = jax.ShapeDtypeStruct(
        (2, chunk_count // 4, width // chunk_count, sum(cols)), BF16
    )
    operands = []
    for left, right in pairs:
        operands += [*left, right[2], right[1], right[0]]
    return pl.pallas_call(
        functools.partial(weight_kernel, len(pairs), chunk_count),
        out_shape=[out, out],
        in_specs=[smem] + [hbm] * len(operands),
        out_specs=[vmem, vmem],
        scratch_shapes=[pltpu.VMEM((2 * length, width), BF16) for _ in pairs]
        + [pltpu.VMEM((2 * length, count), BF16) for count in cols]
        + [pltpu.VMEM((2, width // 2, 2 * length), BF16) for _ in pairs]
        + [pltpu.SemaphoreType.DMA((len(pairs), 2, 2))],
        compiler_params=pltpu.CompilerParams(vmem_limit_bytes=VMEM_BYTES),
        name="weight_terms",
    )(sec_core, *operands)


def swap(block, bit):
    devices = range(lax.axis_size("dp"))
    return lax.ppermute(block, "dp", [(i, i ^ bit) for i in devices])


def pick(block, index):
    return lax.dynamic_index_in_dim(block, index, 0, keepdims=False).astype(F32)


def scatter_sum(send, keep, rank):
    _, depth, rows, cols = send.shape
    y = (rank // 2) % 2
    z = rank // 4
    got = swap(send, 1)
    other = (pick(keep, 1 - y) + pick(got, 1 - y)).astype(BF16)
    crossed = swap(other, 2)
    mine = (pick(keep, y) + pick(got, y) + crossed.astype(F32)).astype(BF16)
    right = left = None
    for step in range(1, depth):
        up = pick(mine, jnp.clip(depth - step + z, 0, depth - 1))
        down = pick(mine, jnp.clip(step - depth + z, 0, depth - 1))
        if right is not None:
            up = up + right.astype(F32)
            down = down + left.astype(F32)
        rising = [
            (4 * at + low, 4 * at + 4 + low) for at in range(step) for low in range(4)
        ]
        falling = [
            (4 * at + low, 4 * at - 4 + low)
            for at in range(depth - step, depth)
            for low in range(4)
        ]
        right = lax.ppermute(up.astype(BF16), "dp", rising)
        left = lax.ppermute(down.astype(BF16), "dp", falling)
    total = pick(mine, z)
    if right is not None:
        total = total + right.astype(F32) + left.astype(F32)
    return total


def full_sum(values):
    size = lax.axis_size("dp")
    if size & (size - 1):
        return lax.psum(values, "dp")
    bit = 1
    while bit < size:
        values = values + swap(values, bit)
        bit *= 2
    return values


def shards(
    patches_in,
    grid_rows,
    grid_cols,
    norm1_gain,
    norm1_bias,
    qkv_weight,
    q_bias,
    v_bias,
    rel_table,
    proj_weight,
    proj_bias,
    attn_scale,
    norm2_gain,
    norm2_bias,
    fc1_weight,
    fc1_bias,
    fc2_weight,
    fc2_bias,
    mlp_scale,
    cotangent,
):
    section = lax.axis_index("section")
    rank = lax.axis_index("dp")
    dp_size = lax.axis_size("dp")
    micro_count, length, width = patches_in.shape
    hidden = fc1_bias.shape[1]
    rel, heads = rel_table.shape[1:]
    sec = jnp.stack([section, rank % 2]).astype(jnp.int32)
    weights = (qkv_weight, proj_weight, fc1_weight, fc2_weight)
    forward_vectors = (
        norm1_gain,
        norm1_bias,
        q_bias,
        v_bias,
        proj_bias,
        attn_scale,
        norm2_gain,
        norm2_bias,
        fc1_bias,
        fc2_bias,
        mlp_scale,
    )
    backward_vectors = (norm1_gain, attn_scale, norm2_gain, mlp_scale)
    table = table_matrices(rel_table[0])
    caches = []
    incoming = patches_in[0]
    for slot in range(micro_count + 1):
        cache = layer_forward(
            slot,
            micro_count,
            sec,
            grid_rows,
            grid_cols,
            patches_in,
            incoming,
            forward_vectors,
            table,
            weights,
        )
        caches.append(cache)
        if slot < micro_count:
            incoming = lax.ppermute(cache[11], "section", [(0, 1)])
    backs = []
    returning = cotangent[0]
    sums = jnp.zeros((SUM_ROWS, width), F32)
    for moment in range(micro_count + 1):
        back = layer_backward(
            moment,
            micro_count,
            sec,
            grid_rows,
            grid_cols,
            cotangent,
            returning,
            backward_vectors,
            sums,
            weights,
            caches[micro_count - moment],
        )
        backs.append(back)
        sums = back[7]
        if moment < micro_count:
            returning = lax.ppermute(back[6], "section", [(1, 0)])

    def sides(left_at, right_at):
        return ([cache[left_at] for cache in caches], [back[right_at] for back in backs])

    down_sides = sides(9, 0)
    up_sides = sides(7, 1)
    proj_sides = sides(4, 2)
    qkv_sides = sides(1, 4)
    if dp_size % 4 == 0 and width % (16 * dp_size) == 0 and micro_count == 2:
        groups = ([down_sides], [up_sides], [proj_sides, qkv_sides])
        down_grad, up_grad, attn_grad = [
            scatter_sum(*weight_terms(sec, dp_size, group), rank) for group in groups
        ]
        proj_grad, qkv_grad = attn_grad[:, :width], attn_grad[:, width:]
    else:

        def plain(pair):
            lefts, rights = pair
            left = jnp.concatenate(lefts, axis=0)
            right = jnp.concatenate(rights[::-1], axis=0)
            term = jnp.einsum("rk,rn->kn", left, right, preferred_element_type=F32)
            return lax.psum_scatter(term, "dp", scatter_dimension=0, tiled=True)

        down_grad, up_grad, proj_grad, qkv_grad = [
            plain(pair) for pair in (down_sides, up_sides, proj_sides, qkv_sides)
        ]
    rev = table_grad(sec, grid_rows, grid_cols, [back[3] for back in backs], rel)
    sums = full_sum(sums)
    rev = full_sum(rev)
    rel_grad = jnp.flip(rev[:heads, :rel].T, 0)
    wide = 10 + hidden // width
    up_shift_grad = sums[10:wide].reshape(1, hidden)

    results = [cache[11] for cache in caches]
    activations = jnp.stack(
        [jnp.where(section == 0, results[mb], results[mb + 1]) for mb in range(micro_count)]
    )
    grads_in = [back[5] for back in backs]
    input_grads = jnp.stack(
        [
            jnp.where(section == 1, grads_in[micro_count - 1 - mb], grads_in[micro_count - mb])
            for mb in range(micro_count)
        ]
    )
    small = [sums[row : row + 1] for row in range(10)]
    return (
        activations[None],
        input_grads[None],
        small[0],
        small[1],
        qkv_grad[None],
        small[2],
        small[3],
        rel_grad[None],
        proj_grad[None],
        small[4],
        small[5],
        small[6],
        small[7],
        up_grad[None],
        up_shift_grad,
        down_grad[None],
        small[8],
        small[9],
    )


def solution(mesh):
    layer_row = P("section", None)
    layer_matrix = P("section", None, None)
    packs = P(None, "dp", None)
    scattered = P("section", "dp", None)
    in_specs = (
        packs,
        packs,
        packs,
        layer_row,
        layer_row,
        layer_matrix,
        layer_row,
        layer_row,
        layer_matrix,
        layer_matrix,
        layer_row,
        layer_row,
        layer_row,
        layer_row,
        layer_matrix,
        layer_row,
        layer_matrix,
        layer_row,
        layer_row,
        packs,
    )
    out_specs = (
        P("section", None, "dp", None),
        P("section", None, "dp", None),
        layer_row,
        layer_row,
        scattered,
        layer_row,
        layer_row,
        layer_matrix,
        scattered,
        layer_row,
        layer_row,
        layer_row,
        layer_row,
        scattered,
        layer_row,
        scattered,
        layer_row,
        layer_row,
    )
    return jax.shard_map(
        shards, mesh=mesh, in_specs=in_specs, out_specs=out_specs, check_vma=False
    )
```

```python
import functools

import jax
import jax.numpy as jnp
from jax import lax
from jax.experimental import pallas as pl
from jax.experimental.pallas import tpu as pltpu
from jax.sharding import PartitionSpec as P

SLOTS = 4
GRID = 14
SPAN = 2 * GRID - 1
CODE = 16
PLACES = GRID * CODE
WIDE = 512
EPS = 1e-06
NEG = -1000000000.0
F32 = jnp.float32
BF16 = jnp.bfloat16
VMEM_BYTES = 56 * 1024 * 1024
BRIEF = pl.CostEstimate(flops=1, bytes_accessed=1, transcendentals=0)

NN = (((1,), (0,)), ((), ()))
NT = (((1,), (1,)), ((), ()))
TN = (((0,), (0,)), ((), ()))


def mm(left, right, dims=NN):
    return lax.dot_general(left, right, dims, preferred_element_type=F32)


def ramp(shape, axis):
    return lax.broadcasted_iota(jnp.int32, shape, axis)


def pack_places(rows_ref, cols_ref, mb, shape, axis):
    places = ramp(shape, axis)
    owner = jnp.zeros(shape, jnp.int32)
    start = jnp.zeros(shape, jnp.int32)
    breadth = jnp.ones(shape, jnp.int32)
    end = jnp.int32(0)
    for slot in range(SLOTS):
        cols = cols_ref[mb, 0, slot]
        here = places >= end
        start = jnp.where(here, end, start)
        breadth = jnp.where(here, cols, breadth)
        end = end + rows_ref[mb, 0, slot] * cols
        owner = owner + (places >= end).astype(jnp.int32)
    inside = places < end
    offset = (places - start).astype(F32)
    row = jnp.floor((offset + 0.5) / breadth.astype(F32)).astype(jnp.int32)
    col = places - start - row * breadth
    code = jnp.where(inside, row * CODE + col, 0)
    return owner, code, inside


def onehot(ids, shape, axis):
    return jnp.where(ids == ramp(shape, axis), 1.0, 0.0).astype(BF16)


def unit_rows(values):
    center = values - jnp.mean(values, axis=-1, keepdims=True)
    inverse = lax.rsqrt(jnp.mean(center * center, axis=-1, keepdims=True) + EPS)
    return center * inverse, inverse


def norm_back(grad_hat, hat, inverse):
    centered = grad_hat - jnp.mean(grad_hat, axis=-1, keepdims=True)
    return inverse * (centered - hat * jnp.mean(grad_hat * hat, axis=-1, keepdims=True))


def normal_parts(u):
    t = 1.0 / (1.0 + (0.3275911 * 0.7071067811865476) * jnp.abs(u))
    falling = jnp.exp(-0.5 * u * u)
    poly = t * (
        0.254829592
        + t * (-0.284496736 + t * (1.421413741 + t * (-1.453152027 + t * 1.061405429)))
    )
    tail = 0.5 * poly * falling
    return jnp.where(u < 0.0, tail, 1.0 - tail), u * falling * 0.3989422804014327


def spread_map(shape, flat_axis, wide_axis):
    flat = ramp(shape, flat_axis)
    wide = ramp(shape, wide_axis)
    row = wide // CODE
    col = wide - row * CODE
    meets = (flat == row * SPAN + col) & (col < GRID) & (row < SPAN)
    return jnp.where(meets, 1.0, 0.0).astype(BF16)


def split_two(values):
    high = values.astype(BF16)
    return high, (values - high.astype(F32)).astype(BF16)


def table_kernel(table_ref, out_ref, wide_ref):
    _, rel, heads = table_ref.shape
    height = wide_ref.shape[1] // CODE
    flat = -(-rel // 128) * 128
    table = table_ref[0]
    mirror = jnp.where(
        ramp((rel, flat), 0) + ramp((rel, flat), 1) == rel - 1, 1.0, 0.0
    ).astype(BF16)
    spread = spread_map((flat, WIDE), 0, 1)
    for part, piece in enumerate(split_two(table)):
        rev = mm(piece, mirror, TN)
        if height > heads:
            rev = jnp.concatenate([rev, jnp.zeros((height - heads, flat), F32)], axis=0)
        turned = jnp.concatenate(
            [pltpu.roll(rev, (c - (GRID - 1)) % flat, 1) for c in range(CODE)], axis=0
        )
        wide = mm(turned.astype(BF16), spread)
        for at in range(WIDE // 128):
            wide_ref[at] = wide[:, at * 128 : (at + 1) * 128]
        for h in range(heads):
            for at in range(WIDE // 128):
                out_ref[part, h, :, at * 128 : (at + 1) * 128] = wide_ref[
                    at, pl.ds(h, CODE, stride=height), :
                ].astype(BF16)


def table_spread(rel_table):
    _, rel, heads = rel_table.shape
    height = -(-heads // 8) * 8
    return pl.pallas_call(
        table_kernel,
        out_shape=jax.ShapeDtypeStruct((2, heads, CODE, WIDE), BF16),
        scratch_shapes=[pltpu.VMEM((WIDE // 128, CODE * height, 128), F32)],
        compiler_params=pltpu.CompilerParams(vmem_limit_bytes=VMEM_BYTES),
        cost_estimate=BRIEF,
        name="table_spread",
    )(rel_table)


def table_grad_kernel(rows_ref, cols_ref, ds_hbm, out_ref, ds_scr, wide_ref, sem):
    micro_count, heads, length, _ = ds_hbm.shape
    height, flat = out_ref.shape
    load = pltpu.make_async_copy(ds_hbm, ds_scr, sem.at[0])
    load.start()
    spread = spread_map((WIDE, flat), 1, 0)
    wide_ref[...] = jnp.zeros_like(wide_ref)
    sides = []
    for mb in range(micro_count):
        _, code_col, _ = pack_places(rows_ref, cols_ref, mb, (length, 1), 0)
        _, code_row, _ = pack_places(rows_ref, cols_ref, mb, (1, length), 1)
        sides.append(
            (onehot(code_col, (length, 256), 1), onehot(code_row, (256, length), 0))
        )
    load.wait()

    def one_head(h, carry):
        total = jnp.zeros((256, 256), F32)
        for mb, (place_col, place_row) in enumerate(sides):
            keyed = mm(ds_scr[mb, h], place_col).astype(BF16)
            total = total + mm(place_row, keyed)
        acc = jnp.zeros((CODE, WIDE), F32)
        for r in range(GRID):
            block = jnp.concatenate(
                [total[r * CODE : (r + 1) * CODE, :], jnp.zeros((CODE, WIDE - 256), F32)],
                axis=1,
            )
            acc = acc + pltpu.roll(block, CODE * (GRID - 1 - r), 1)
        for at in range(WIDE // 128):
            wide_ref[at, pl.ds(h, CODE, stride=height), :] = acc[:, at * 128 : (at + 1) * 128]
        return carry

    lax.fori_loop(0, heads, one_head, 0)
    high, rest = split_two(
        jnp.concatenate([wide_ref[at] for at in range(WIDE // 128)], axis=1)
    )
    turned = mm(high, spread) + mm(rest, spread)
    result = jnp.zeros((height, flat), F32)
    for c in range(GRID):
        result = result + pltpu.roll(
            turned[c * height : (c + 1) * height, :], GRID - 1 - c, 1
        )
    out_ref[...] = result


def table_grad(grid_rows, grid_cols, score_grads, rel):
    micro_count, heads, length, _ = score_grads.shape
    flat = -(-rel // 128) * 128
    height = -(-heads // 8) * 8
    return pl.pallas_call(
        table_grad_kernel,
        out_shape=jax.ShapeDtypeStruct((height, flat), F32),
        in_specs=[pl.BlockSpec(memory_space=pltpu.SMEM)] * 2
        + [pl.BlockSpec(memory_space=pl.ANY)],
        scratch_shapes=[
            pltpu.VMEM(score_grads.shape, BF16),
            pltpu.VMEM((WIDE // 128, CODE * height, 128), F32),
            pltpu.SemaphoreType.DMA((1,)),
        ],
        compiler_params=pltpu.CompilerParams(vmem_limit_bytes=VMEM_BYTES),
        cost_estimate=BRIEF,
        name="table_grad",
    )(grid_rows, grid_cols, score_grads)


KEPT = ("h", "p", "wt", "o", "br", "m", "h2", "dg", "z", "fd", "act")


def forward_shapes(micro_count, length, width, hidden, heads):
    row = (micro_count, length, width)
    return {
        "h": (row, BF16),
        "p": ((micro_count, length, 3 * width), BF16),
        "wt": ((micro_count, heads, length, length), BF16),
        "o": (row, BF16),
        "br": (row, BF16),
        "m": (row, F32),
        "h2": (row, BF16),
        "dg": ((micro_count, length, hidden), BF16),
        "z": ((micro_count, length, hidden), BF16),
        "fd": (row, BF16),
        "act": (row, BF16),
    }


def forward_kernel(section, mb, sends, prior_count, *refs):
    sec_ref, rows_ref, cols_ref, x_hbm = refs[:4]
    vectors, refs = refs[4:15], refs[15:]
    wide_hbm, qkv_hbm, proj_hbm, up_hbm, down_hbm = refs[:5]
    refs = refs[5 + prior_count :]
    outs, refs = dict(zip(KEPT, refs)), refs[len(KEPT) :]
    if sends:
        send_out, refs = refs[0], refs[1:]
    x_scr, wide_scr, qkv_w, proj_w, up_w, down_w = refs[:6]
    scr, refs = dict(zip(KEPT, refs[6:])), refs[6 + len(KEPT) :]
    bias_scr, ladder_scr, in_sem, out_sem = refs
    n1_gain, n1_shift, query_bias, value_bias, proj_shift, attn_gain = vectors[:6]
    n2_gain, n2_shift, up_shift, down_shift, mlp_gain = vectors[6:]
    length, width = x_scr.shape
    heads = scr["wt"].shape[0]
    hidden = scr["z"].shape[1]
    head_dim = width // heads
    pair = 2 * head_dim

    @pl.when(sec_ref[0] == section)
    def _():
        loads = []
        for place, (src, dst) in enumerate(
            (
                (wide_hbm, wide_scr),
                (x_hbm if section else x_hbm.at[mb], x_scr),
                (qkv_hbm.at[0], qkv_w),
                (proj_hbm.at[0], proj_w),
                (up_hbm.at[0], up_w),
                (down_hbm.at[0], down_w),
            )
        ):
            load = pltpu.make_async_copy(src, dst, in_sem.at[place])
            load.start()
            loads.append(load)
        stores = []

        def copy_out(src, dst):
            store = pltpu.make_async_copy(src, dst, out_sem.at[len(stores)])
            store.start()
            stores.append(store)

        def keep(name):
            copy_out(scr[name], outs[name].at[mb])

        owner_col, code_col, _ = pack_places(rows_ref, cols_ref, mb, (length, 1), 0)
        owner_row, code_row, _ = pack_places(rows_ref, cols_ref, mb, (1, length), 1)
        lanes = ramp((length, 256), 1)
        place_col = jnp.where(
            (lanes == code_col) | (lanes == owner_col + PLACES), 1.0, 0.0
        ).astype(BF16)
        place_col = jnp.concatenate([place_col, place_col], axis=1)
        reach = CODE * (GRID - 1)
        ladder_scr[...] = onehot(code_row + reach, ladder_scr.shape, 0)
        spare = ramp((256 - PLACES, length), 0)
        walls = jnp.where(spare == owner_row, 0.0, NEG).astype(BF16)
        blank = jnp.zeros((256 - PLACES, length), BF16)
        for h in range(heads):
            bias_scr[h, PLACES:256, :] = walls
            bias_scr[h, 256 + PLACES :, :] = blank
        loads[0].wait()
        for r in range(GRID):
            begin = CODE * (GRID - 1 - r)
            low = begin // 128 * 128
            high = -(-(begin + PLACES) // 128) * 128
            rung = ladder_scr[CODE * r + low : CODE * r + high, :]
            for part in range(2):
                block = mm(
                    wide_scr[part, :, :, low:high].reshape(heads * CODE, high - low), rung
                ).astype(BF16)
                at = 256 * part + CODE * r
                for h in range(heads):
                    bias_scr[h, at : at + CODE, :] = block[h * CODE : (h + 1) * CODE]

        loads[1].wait()
        inputs = x_scr[...].astype(F32)
        hat, _ = unit_rows(inputs)
        scr["h"][...] = (hat * n1_gain[...] + n1_shift[...]).astype(BF16)
        keep("h")

        loads[2].wait()
        scale = head_dim ** (-0.5)
        h_all = scr["h"][...]
        p_scr = scr["p"]
        p_scr[:, :width] = (
            (mm(h_all, qkv_w[:, :width]) + query_bias[...]).astype(BF16) * scale
        ).astype(BF16)
        p_scr[:, width : 2 * width] = mm(h_all, qkv_w[:, width : 2 * width]).astype(BF16)
        p_scr[:, 2 * width :] = (mm(h_all, qkv_w[:, 2 * width :]) + value_bias[...]).astype(
            BF16
        )
        keep("p")

        first = ramp((length, pair), 1) < head_dim
        zero = jnp.zeros((length, pair), BF16)
        for at in range(0, width, pair):
            queries = p_scr[:, at : at + pair]
            keys_all = p_scr[:, width + at : width + at + pair]
            values_all = p_scr[:, 2 * width + at : 2 * width + at + pair]
            mixed = []
            for side, own in enumerate(
                (jnp.where(first, queries, zero), jnp.where(first, zero, queries))
            ):
                head = at // head_dim + side
                scores = mm(own, keys_all, NT) + mm(place_col, bias_scr[head])
                raised = jnp.exp(scores - jnp.max(scores, axis=-1, keepdims=True))
                share = 1.0 / jnp.sum(raised, axis=-1, keepdims=True)
                weights = (raised * share).astype(BF16)
                scr["wt"][head] = weights
                mixed.append(mm(weights, values_all))
            scr["o"][:, at : at + pair] = jnp.where(first, mixed[0], mixed[1]).astype(BF16)
        keep("wt")
        keep("o")

        loads[3].wait()
        branch = mm(scr["o"][...], proj_w[...]) + proj_shift[...]
        scr["br"][...] = branch.astype(BF16)
        keep("br")
        middle = x_scr[...].astype(F32) + attn_gain[...] * branch
        scr["m"][...] = middle
        keep("m")
        hat, _ = unit_rows(middle)
        scr["h2"][...] = (hat * n2_gain[...] + n2_shift[...]).astype(BF16)
        keep("h2")

        loads[4].wait()
        loads[5].wait()
        second = scr["h2"][...]
        tile = width
        down = None
        for at in range(0, hidden, tile):
            upward = mm(second, up_w[:, at : at + tile]) + up_shift[:, at : at + tile]
            cdf, leaning = normal_parts(upward)
            z = (upward * cdf).astype(BF16)
            scr["z"][:, at : at + tile] = z
            scr["dg"][:, at : at + tile] = (cdf + leaning).astype(BF16)
            term = mm(z, down_w[at : at + tile, :])
            down = term if down is None else down + term
        keep("z")
        keep("dg")
        downward = down + down_shift[...]
        scr["act"][...] = (scr["m"][...] + mlp_gain[...] * downward).astype(BF16)
        if sends:
            copy_out(scr["act"], send_out)
        keep("act")
        scr["fd"][...] = downward.astype(BF16)
        keep("fd")
        for store in stores:
            store.wait()


def layer_forward(section, mb, sends, sec, grid_rows, grid_cols, source, vectors, wide, weights, prior):
    length, width = source.shape[-2:]
    hidden = weights[2].shape[2]
    heads = wide.shape[1]
    smem = pl.BlockSpec(memory_space=pltpu.SMEM)
    vmem = pl.BlockSpec(memory_space=pltpu.VMEM)
    hbm = pl.BlockSpec(memory_space=pl.ANY)
    shapes = forward_shapes(grid_rows.shape[0], length, width, hidden, heads)
    outs = [jax.ShapeDtypeStruct(*shapes[name]) for name in KEPT]
    if sends:
        outs.append(jax.ShapeDtypeStruct((length, width), BF16))
    scratch = [pltpu.VMEM((length, width), BF16), pltpu.VMEM(wide.shape, BF16)]
    scratch += [pltpu.VMEM(entry.shape[1:], BF16) for entry in weights]
    scratch += [pltpu.VMEM(shapes[name][0][1:], shapes[name][1]) for name in KEPT]
    scratch += [
        pltpu.VMEM((heads, 512, length), BF16),
        pltpu.VMEM((CODE * (GRID - 1) + WIDE, length), BF16),
        pltpu.SemaphoreType.DMA((6,)),
        pltpu.SemaphoreType.DMA((len(outs),)),
    ]
    before = 4 + len(vectors) + 5
    results = pl.pallas_call(
        functools.partial(forward_kernel, section, mb, sends, len(prior)),
        out_shape=outs,
        in_specs=[smem] * 3 + [hbm] + [vmem] * len(vectors) + [hbm] * (5 + len(prior)),
        out_specs=[hbm] * len(outs),
        scratch_shapes=scratch,
        input_output_aliases={before + at: at for at in range(len(prior))},
        compiler_params=pltpu.CompilerParams(vmem_limit_bytes=VMEM_BYTES),
        cost_estimate=BRIEF,
        name="layer_forward",
    )(sec, grid_rows, grid_cols, source, *vectors, wide, *weights, *prior)
    return list(results[: len(KEPT)]), (results[-1] if sends else None)


SUM_ROWS = 16
GRADS = ("df", "du", "db", "ds", "dp", "dx", "sums")
MLP_IN = ("fd", "dg", "m", "br")
ATTN_IN = ("p", "wt")


def backward_kernel(section, mb, mlp, attn, sends, adds, prior_names, *refs):
    sec_ref, rows_ref, cols_ref, g_hbm, x_hbm = refs[:5]
    n1_gain, attn_gain, n2_gain, mlp_gain = refs[5:9]
    qkv_hbm, proj_hbm, up_hbm, down_hbm = refs[9:13]
    cache, refs = dict(zip(MLP_IN + ATTN_IN, refs[13:19])), refs[19:]
    if not mlp:
        dm_in, refs = refs[0], refs[1:]
    refs = refs[len(prior_names) :]
    outs, refs = dict(zip(GRADS, refs)), refs[len(GRADS) :]
    if not attn:
        dm_out, refs = refs[0], refs[1:]
    if sends:
        send_out, refs = refs[0], refs[1:]
    g_scr, x_scr, qkv_w, proj_w, up_w, down_w = refs[:6]
    got, refs = dict(zip(MLP_IN + ATTN_IN, refs[6:12])), refs[12:]
    scr, refs = dict(zip(GRADS, refs)), refs[len(GRADS) :]
    do_scr, send_scr, in_sem, out_sem = refs
    length, width = g_scr.shape
    heads = got["wt"].shape[0]
    hidden = got["dg"].shape[1]
    head_dim = width // heads
    pair = 2 * head_dim

    @pl.when(sec_ref[0] == section)
    def _():
        wanted = []
        if adds or not mlp:
            wanted.append(("sums", outs["sums"], scr["sums"]))
        if mlp:
            wanted += [
                ("g", g_hbm.at[mb] if section else g_hbm, g_scr),
                ("fd", cache["fd"].at[mb], got["fd"]),
                ("down", down_hbm.at[0], down_w),
                ("dg", cache["dg"].at[mb], got["dg"]),
                ("up", up_hbm.at[0], up_w),
                ("m", cache["m"].at[mb], got["m"]),
                ("br", cache["br"].at[mb], got["br"]),
            ]
        else:
            wanted += [
                ("db", outs["db"].at[mb], scr["db"]),
                ("dm", dm_in, scr["dx"]),
            ]
        if attn:
            wanted += [
                ("proj", proj_hbm.at[0], proj_w),
                ("p", cache["p"].at[mb], got["p"]),
                ("wt", cache["wt"].at[mb], got["wt"]),
                ("qkv", qkv_hbm.at[0], qkv_w),
                ("x", x_hbm if section else x_hbm.at[mb], x_scr),
            ]
        loads = {}
        for name, src, dst in wanted:
            loads[name] = pltpu.make_async_copy(src, dst, in_sem.at[len(loads)])
            loads[name].start()
        stores = []

        def copy_out(src, dst):
            store = pltpu.make_async_copy(src, dst, out_sem.at[len(stores)])
            store.start()
            stores.append(store)

        def keep(name):
            copy_out(scr[name], outs[name].at[mb])

        def total(values):
            return jnp.sum(values, axis=0, keepdims=True)

        sums = scr["sums"]

        def note(row, values):
            if adds:
                values = values + sums[row : row + 1, :]
            sums[row : row + 1, :] = values

        if "sums" in loads:
            loads["sums"].wait()
        if mlp:
            if section:
                _, _, inside = pack_places(rows_ref, cols_ref, mb, (length, 1), 0)
                kept = jnp.where(inside, 1.0, 0.0)
            else:
                kept = 1.0
            loads["g"].wait()
            grad_out = g_scr[...].astype(F32) * kept
            loads["fd"].wait()
            note(9, total(grad_out * got["fd"][...].astype(F32)))
            df = (grad_out * mlp_gain[...]).astype(BF16)
            scr["df"][...] = df
            if attn:
                keep("df")
            note(8, total(df.astype(F32)))

            loads["down"].wait()
            loads["dg"].wait()
            loads["up"].wait()
            tile = width
            dh2 = None
            for at in range(0, hidden, tile):
                dz = mm(scr["df"][...], down_w[at : at + tile, :], NT)
                du = (dz * got["dg"][:, at : at + tile].astype(F32)).astype(BF16)
                scr["du"][:, at : at + tile] = du
                note(10 + at // tile, total(du.astype(F32)))
                term = mm(du, up_w[:, at : at + tile], NT)
                dh2 = term if dh2 is None else dh2 + term
            keep("du")
            for row in range(10 + hidden // tile, SUM_ROWS):
                sums[row : row + 1, :] = jnp.zeros((1, width), F32)

            loads["m"].wait()
            hat, inverse = unit_rows(got["m"][...])
            note(6, total(dh2 * hat))
            note(7, total(dh2))
            dm = g_scr[...].astype(F32) * kept + norm_back(dh2 * n2_gain[...], hat, inverse)
            scr["dx"][...] = dm
            if not attn:
                copy_out(scr["dx"], dm_out)
            loads["br"].wait()
            note(5, total(dm * got["br"][...].astype(F32)))
            db = (dm * attn_gain[...]).astype(BF16)
            scr["db"][...] = db
            keep("db")
            note(4, total(db.astype(F32)))
        else:
            loads["db"].wait()
            loads["dm"].wait()

        if attn:
            loads["proj"].wait()
            do_scr[...] = mm(scr["db"][...], proj_w[...], NT).astype(BF16)
            loads["p"].wait()
            loads["wt"].wait()
            first = ramp((length, pair), 1) < head_dim
            zero = jnp.zeros((length, pair), BF16)
            scale = head_dim ** (-0.5)
            p_scr, dp_scr = got["p"], scr["dp"]
            for at in range(0, width, pair):
                queries = p_scr[:, at : at + pair]
                keys_all = p_scr[:, width + at : width + at + pair]
                values_all = p_scr[:, 2 * width + at : 2 * width + at + pair]
                dout = do_scr[:, at : at + pair]
                dq, dk, dv = [], [], []
                for side, own in enumerate(
                    (jnp.where(first, dout, zero), jnp.where(first, zero, dout))
                ):
                    head = at // head_dim + side
                    weights = got["wt"][head]
                    dwt = mm(own, values_all, NT)
                    probs = weights.astype(F32)
                    inner = jnp.sum(probs * dwt, axis=-1, keepdims=True)
                    ds = (probs * (dwt - inner)).astype(BF16)
                    scr["ds"][head] = ds
                    dv.append(mm(weights, dout, TN))
                    dq.append(mm(ds, keys_all))
                    dk.append(mm(ds, queries, TN))
                for part, both in enumerate((dq, dk, dv)):
                    merged = jnp.where(first, both[0], both[1])
                    if part == 0:
                        merged = merged * scale
                    dp_scr[:, part * width + at : part * width + at + pair] = merged.astype(BF16)
            keep("ds")
            keep("dp")

            loads["qkv"].wait()
            dh = mm(dp_scr[...], qkv_w[...], NT)
            loads["x"].wait()
            hat, inverse = unit_rows(x_scr[...].astype(F32))
            dx = scr["dx"][...] + norm_back(dh * n1_gain[...], hat, inverse)
            if sends:
                send_scr[...] = dx.astype(BF16)
                copy_out(send_scr, send_out)
            scr["dx"][...] = dx
            keep("dx")
            note(0, total(dh * hat))
            note(1, total(dh))
            note(2, total(dp_scr[:, :width].astype(F32)))
            note(3, total(dp_scr[:, 2 * width :].astype(F32)))
        copy_out(sums, outs["sums"])
        for store in stores:
            store.wait()


def layer_backward(
    section, mb, mlp, attn, sends, adds, sec, grid_rows, grid_cols, grad, source, vectors, weights, cache, middle, prior
):
    length, width = source.shape[-2:]
    hidden = cache["dg"].shape[-1]
    heads = cache["wt"].shape[1]
    micro_count = grid_rows.shape[0]
    smem = pl.BlockSpec(memory_space=pltpu.SMEM)
    vmem = pl.BlockSpec(memory_space=pltpu.VMEM)
    hbm = pl.BlockSpec(memory_space=pl.ANY)
    row = (micro_count, length, width)
    shapes = {
        "df": (row, BF16),
        "du": ((micro_count, length, hidden), BF16),
        "db": (row, BF16),
        "ds": ((micro_count, heads, length, length), BF16),
        "dp": ((micro_count, length, 3 * width), BF16),
        "dx": (row, F32),
    }
    scratch = [pltpu.VMEM((length, width), BF16)] * 2
    scratch += [pltpu.VMEM(entry.shape[1:], BF16) for entry in weights]
    saved = [cache[name] for name in MLP_IN + ATTN_IN]
    scratch += [pltpu.VMEM(entry.shape[1:], entry.dtype) for entry in saved]
    scratch += [pltpu.VMEM(shape[1:], dtype) for shape, dtype in shapes.values()]
    shapes["sums"] = ((SUM_ROWS, width), F32)
    outs = [jax.ShapeDtypeStruct(*shapes[name]) for name in GRADS]
    if not attn:
        outs.append(jax.ShapeDtypeStruct((length, width), F32))
    if sends:
        outs.append(jax.ShapeDtypeStruct((length, width), BF16))
    scratch += [
        pltpu.VMEM((SUM_ROWS, width), F32),
        pltpu.VMEM((length, width), BF16),
        pltpu.VMEM((length, width), BF16),
        pltpu.SemaphoreType.DMA((13,)),
        pltpu.SemaphoreType.DMA((len(GRADS) + 2,)),
    ]
    extra = [] if mlp else [middle]
    operands = [sec, grid_rows, grid_cols, grad, source, *vectors, *weights, *saved, *extra]
    results = pl.pallas_call(
        functools.partial(backward_kernel, section, mb, mlp, attn, sends, adds, GRADS[: len(prior)]),
        out_shape=outs,
        in_specs=[smem] * 3
        + [hbm] * 2
        + [vmem] * len(vectors)
        + [hbm] * (len(operands) - 5 - len(vectors) + len(prior)),
        out_specs=[hbm] * len(outs),
        scratch_shapes=scratch,
        input_output_aliases={len(operands) + at: at for at in range(len(prior))},
        compiler_params=pltpu.CompilerParams(vmem_limit_bytes=VMEM_BYTES),
        cost_estimate=BRIEF,
        name="layer_backward",
    )(*operands, *prior)
    return list(results[: len(GRADS)]), (results[-1] if len(outs) > len(GRADS) else None)


def turn_kernel(chunk_count, *refs):
    count = len(refs) // 4
    sources, outs, refs = refs[:count], refs[count : 2 * count], refs[2 * count :]
    lefts, turned, refs = refs[:count], refs[count : 2 * count], refs[2 * count :]
    in_sem, out_sem = refs
    loads = [
        pltpu.make_async_copy(src, dst, in_sem.at[at])
        for at, (src, dst) in enumerate(zip(sources, lefts))
    ]
    stores = [
        pltpu.make_async_copy(src, dst, out_sem.at[at])
        for at, (src, dst) in enumerate(zip(turned, outs))
    ]
    for load in loads:
        load.start()
    for left, out, load, store in zip(lefts, turned, loads, stores):
        load.wait()
        micro_count, length, width = left.shape
        step = width // chunk_count
        strip = 256 if width % 256 == 0 else width
        for mb in range(micro_count):
            flipped = jnp.concatenate(
                [left[mb, :, at : at + strip].T for at in range(0, width, strip)], axis=0
            )
            for chunk in range(chunk_count):
                core_of, to = chunk % 2, chunk // 2 * step
                out[core_of, to : to + step, mb * length : (mb + 1) * length] = flipped[
                    chunk * step : (chunk + 1) * step, :
                ]
        store.start()
    for store in stores:
        store.wait()


def turn_lefts(chunk_count, lefts):
    hbm = pl.BlockSpec(memory_space=pl.ANY)
    shapes = [(2, left.shape[2] // 2, left.shape[0] * left.shape[1]) for left in lefts]
    return pl.pallas_call(
        functools.partial(turn_kernel, chunk_count),
        out_shape=[jax.ShapeDtypeStruct(shape, BF16) for shape in shapes],
        in_specs=[hbm] * len(lefts),
        out_specs=[hbm] * len(lefts),
        scratch_shapes=[pltpu.VMEM(left.shape, BF16) for left in lefts]
        + [pltpu.VMEM(shape, BF16) for shape in shapes]
        + [pltpu.SemaphoreType.DMA((len(lefts),))] * 2,
        compiler_params=pltpu.CompilerParams(vmem_limit_bytes=VMEM_BYTES),
        cost_estimate=BRIEF,
        name="turn_lefts",
    )(*lefts)


def placed(chunk, order):
    place = 0
    for bit in order:
        place = 2 * place + (chunk >> (bit - 1) & 1)
    return place


def weight_kernel(parts, fresh, sends, orders, sec_ref, *refs):
    cuts = len(orders)
    half = 1 - sec_ref[1] if sends else sec_ref[1]
    operands, refs = refs[: 2 * parts], refs[2 * parts :]
    if fresh:
        (grad_hbm, gain_ref), refs = refs[:2], refs[2:]
    outs, refs = refs[:cuts], refs[cuts:]
    lefts, rights, refs = refs[:parts], refs[parts : 2 * parts], refs[2 * parts :]
    out_scr, in_sem, out_sem = refs[:3]
    loads = []
    for part in range(parts):
        pairs = (
            (operands[2 * part].at[half], lefts[part]),
            (operands[2 * part + 1], rights[part]),
        )
        for kind, (src, dst) in enumerate(pairs):
            load = pltpu.make_async_copy(src, dst, in_sem.at[part, kind])
            load.start()
            loads.append(load)
    if fresh:
        grad_scr = refs[3]
        grad_copy = pltpu.make_async_copy(grad_hbm, grad_scr, in_sem.at[parts, 0])
        grad_copy.start()
    stores = []
    at_col = 0
    unit = out_scr.shape[2]
    for part in range(parts):
        loads[2 * part].wait()
        loads[2 * part + 1].wait()
        if fresh:
            grad_copy.wait()

            @pl.when(sec_ref[0] == 0)
            def _():
                rights[part][0] = (grad_scr[...].astype(F32) * gain_ref[...]).astype(BF16)

        micro_count, length, cols = rights[part].shape
        height = lefts[part].shape[0]
        tile = min(768, unit)
        for at in range(0, cols, tile):
            right = rights[part][:, :, at : at + tile].reshape(micro_count * length, tile)
            which, place = divmod(at_col + at, unit)
            step = height >> len(orders[which])
            for low in range(0, height, 384):
                rows = min(384, height - low)
                block = mm(lefts[part][low : low + rows], right).astype(BF16)
                for top in range(0, rows, step):
                    to = step * placed((low + top) // step, orders[which])
                    out_scr[which, to : to + step, place : place + tile] = block[
                        top : top + step
                    ]
            piece = (slice(None), pl.ds(place, tile))
            store = pltpu.make_async_copy(
                out_scr.at[which].at[piece], outs[which].at[piece], out_sem.at[len(stores)]
            )
            store.start()
            stores.append(store)
        at_col += cols
    for store in stores:
        store.wait()


def weight_terms(sends, orders, sec, pairs, fresh=()):
    hbm = pl.BlockSpec(memory_space=pl.ANY)
    vmem = pl.BlockSpec(memory_space=pltpu.VMEM)
    smem = pl.BlockSpec(memory_space=pltpu.SMEM)
    height = pairs[0][0].shape[1]
    cuts = len(orders)
    unit = sum(right.shape[2] for _, right in pairs) // cuts
    tiles = -(-unit // min(768, unit)) * cuts
    operands = [side for pair in pairs for side in pair]
    scratch = [pltpu.VMEM(left.shape[1:], BF16) for left, _ in pairs]
    scratch += [pltpu.VMEM(right.shape, BF16) for _, right in pairs]
    scratch += [
        pltpu.VMEM((cuts, height, unit), BF16),
        pltpu.SemaphoreType.DMA((len(pairs) + 1, 2)),
        pltpu.SemaphoreType.DMA((tiles,)),
    ]
    if fresh:
        scratch.append(pltpu.VMEM(fresh[0].shape, BF16))
    terms = pl.pallas_call(
        functools.partial(weight_kernel, len(pairs), bool(fresh), sends, orders),
        out_shape=[jax.ShapeDtypeStruct((height, unit), BF16)] * cuts,
        in_specs=[smem] + [hbm] * len(operands) + ([hbm, vmem] if fresh else []),
        out_specs=[hbm] * cuts,
        scratch_shapes=scratch,
        compiler_params=pltpu.CompilerParams(vmem_limit_bytes=VMEM_BYTES),
        cost_estimate=BRIEF,
        name="weight_terms",
    )(sec, *operands, *fresh)
    return [term.reshape(2, height // 2, unit) for term in terms]


def swap(block, bit):
    devices = range(lax.axis_size("dp"))
    return lax.ppermute(block, "dp", [(i, i ^ bit) for i in devices])


def after(value, *others):
    return lax.optimization_barrier((value, *others))[0]


def half_of(block, side):
    return lax.dynamic_index_in_dim(block, side, 0, keepdims=False).astype(F32)


def begin_sum(keep, got, rank, order):
    side = (rank >> order[0]) & 1
    sent = (half_of(keep, 1 - side) + half_of(got, 1 - side)).astype(BF16)
    mine = half_of(keep, side) + half_of(got, side)
    return sent, swap(sent, 1 << order[0]), mine, order[1:]


def next_sum(begun, rank, *before):
    _, crossed, mine, order = begun
    block = mine + after(crossed, *before).astype(F32)
    if not order:
        return block
    block = block.astype(BF16).reshape(2, block.shape[0] // 2, block.shape[1])
    side = (rank >> order[0]) & 1
    sent = half_of(block, 1 - side).astype(BF16)
    return sent, swap(sent, 1 << order[0]), half_of(block, side), order[1:]


def full_sum(values):
    size = lax.axis_size("dp")
    if size & (size - 1):
        return lax.psum(values, "dp")
    bit = 1
    while bit < size:
        values = values + swap(values, bit)
        bit *= 2
    return values


def shards(
    patches_in,
    grid_rows,
    grid_cols,
    norm1_gain,
    norm1_bias,
    qkv_weight,
    q_bias,
    v_bias,
    rel_table,
    proj_weight,
    proj_bias,
    attn_scale,
    norm2_gain,
    norm2_bias,
    fc1_weight,
    fc1_bias,
    fc2_weight,
    fc2_bias,
    mlp_scale,
    cotangent,
):
    rank = lax.axis_index("dp")
    dp_size = lax.axis_size("dp")
    micro_count, length, width = patches_in.shape
    hidden = fc1_bias.shape[1]
    rel, heads = rel_table.shape[1:]
    sec = jnp.stack([lax.axis_index("section"), rank % 2]).astype(jnp.int32)
    weights = (qkv_weight, proj_weight, fc1_weight, fc2_weight)
    forward_vectors = (
        norm1_gain,
        norm1_bias,
        q_bias,
        v_bias,
        proj_bias,
        attn_scale,
        norm2_gain,
        norm2_bias,
        fc1_bias,
        fc2_bias,
        mlp_scale,
    )
    backward_vectors = (norm1_gain, attn_scale, norm2_gain, mlp_scale)
    wide = table_spread(rel_table)

    kept = []
    moved = []
    for mb in range(micro_count):
        kept, sent = layer_forward(
            0, mb, True, sec, grid_rows, grid_cols, patches_in, forward_vectors, wide, weights, kept
        )
        moved.append(lax.ppermute(sent, "section", [(0, 1)]))
    for mb in range(micro_count):
        kept, _ = layer_forward(
            1, mb, False, sec, grid_rows, grid_cols, moved[mb], forward_vectors, wide, weights, kept
        )
    cache = dict(zip(KEPT, kept))

    def backward(section, mb, grad, source, prior, middle=None, mlp=True, attn=True):
        return layer_backward(
            section,
            mb,
            mlp,
            attn,
            section == 1,
            mb != micro_count - 1,
            sec,
            grid_rows,
            grid_cols,
            grad,
            source,
            backward_vectors,
            weights,
            cache,
            middle,
            prior,
        )

    grads = []
    returned = [None] * micro_count
    for mb in range(micro_count - 1, -1, -1):
        grads, sent = backward(1, mb, cotangent, moved[mb], grads)
        returned[mb] = lax.ppermute(sent, "section", [(1, 0)])
    spread_out = dp_size == 16 and width % (16 * dp_size) == 0
    if spread_out:
        lefts = [after(cache[name], grads[5]) for name in ("z", "h2", "o", "h")]
        z_turned, h2_turned, o_turned, h_turned = turn_lefts(dp_size, lefts)
    for mb in range(micro_count - 1, 0, -1):
        grads, _ = backward(0, mb, returned[mb], patches_in, grads)
    named = dict(zip(GRADS, grads))
    last = returned[0]
    if spread_out:
        one, two = (1, 2, 3), (2, 1, 3)

        def core_terms(orders, *operands):
            send = weight_terms(True, orders, sec, *operands)
            return send, [swap(block, 1) for block in send]

        def begin(orders, sent, got, hold, *operands):
            keep = weight_terms(False, orders, after(sec, *sent, *hold), *operands)
            return [
                begin_sum(mine, other, rank, order)
                for mine, other, order in zip(keep, got, orders)
            ]

        def follow(begun, *before):
            return [next_sum(each, rank, *before) for each in begun]

        def moving(begun):
            return [each[0] for each in begun]

        down_orders = up_orders = attn_orders = (one, two)
        operands = ([(z_turned, named["df"])], (last, mlp_scale))
        sent, got = core_terms(down_orders, *operands)
        down = begin(down_orders, sent, got, [], *operands)
        grads, middle = backward(
            0, 0, after(last, *moving(down)), patches_in, grads, attn=False
        )
        named = dict(zip(GRADS, grads))
        operands = ([(h2_turned, named["du"])],)
        sent, got = core_terms(up_orders, *operands)
        down = follow(down, *sent)
        up = begin(up_orders, sent, got, moving(down), *operands)
        grads, _ = backward(
            0, 0, last, patches_in, grads, middle=after(middle, *moving(up)), mlp=False
        )
        named = dict(zip(GRADS, grads))
        operands = ([(o_turned, named["db"]), (h_turned, named["dp"])],)
        sent, got = core_terms(attn_orders, *operands)
        down = follow(down, *sent)
        up = follow(up, *sent)
        attn = begin(attn_orders, sent, got, moving(down) + moving(up), *operands)
        rev = table_grad(grid_rows, grid_cols, after(named["ds"], *moving(attn)), rel)
        down_grad = follow(down, rev)
        up = follow(up, rev)
        attn = follow(attn, *moving(up))
        small = full_sum(
            jnp.concatenate([after(named["sums"], *moving(attn)), rev], axis=0)
        )
        up_grad = follow(up)
        attn_grad = follow(follow(attn))
        down_grad, up_grad, attn_grad = [
            jnp.concatenate(grad, axis=1) for grad in (down_grad, up_grad, attn_grad)
        ]
        proj_grad, qkv_grad = attn_grad[:, :width], attn_grad[:, width:]
        sums, rev = small[:SUM_ROWS], small[SUM_ROWS:]
    else:
        grads, _ = backward(0, 0, last, patches_in, grads)
        named = dict(zip(GRADS, grads))

        def plain(left, right):
            term = jnp.einsum("mrk,mrn->kn", left, right, preferred_element_type=F32)
            return lax.psum_scatter(term, "dp", scatter_dimension=0, tiled=True)

        down_grad = plain(cache["z"], named["df"])
        up_grad = plain(cache["h2"], named["du"])
        proj_grad = plain(cache["o"], named["db"])
        qkv_grad = plain(cache["h"], named["dp"])
        rev = full_sum(table_grad(grid_rows, grid_cols, named["ds"], rel))
        sums = full_sum(named["sums"])
    rel_grad = jnp.flip(rev[:heads, :rel].T, 0)
    up_shift_grad = sums[10 : 10 + hidden // width].reshape(1, hidden)
    small = [sums[row : row + 1] for row in range(10)]
    return (
        cache["act"][None],
        named["dx"][None],
        small[0],
        small[1],
        qkv_grad[None],
        small[2],
        small[3],
        rel_grad[None],
        proj_grad[None],
        small[4],
        small[5],
        small[6],
        small[7],
        up_grad[None],
        up_shift_grad,
        down_grad[None],
        small[8],
        small[9],
    )


def solution(mesh):
    layer_row = P("section", None)
    layer_matrix = P("section", None, None)
    packs = P(None, "dp", None)
    scattered = P("section", "dp", None)
    in_specs = (
        packs,
        packs,
        packs,
        layer_row,
        layer_row,
        layer_matrix,
        layer_row,
        layer_row,
        layer_matrix,
        layer_matrix,
        layer_row,
        layer_row,
        layer_row,
        layer_row,
        layer_matrix,
        layer_row,
        layer_matrix,
        layer_row,
        layer_row,
        packs,
    )
    out_specs = (
        P("section", None, "dp", None),
        P("section", None, "dp", None),
        layer_row,
        layer_row,
        scattered,
        layer_row,
        layer_row,
        layer_matrix,
        scattered,
        layer_row,
        layer_row,
        layer_row,
        layer_row,
        scattered,
        layer_row,
        scattered,
        layer_row,
        layer_row,
    )
    return jax.shard_map(
        shards, mesh=mesh, in_specs=in_specs, out_specs=out_specs, check_vma=False
    )
```

```python
import functools

import jax
import jax.numpy as jnp
from jax import lax
from jax.experimental import pallas as pl
from jax.experimental.pallas import tpu as pltpu
from jax.sharding import PartitionSpec as P

SLOTS = 4
GRID = 14
SPAN = 2 * GRID - 1
CODE = 16
PLACES = GRID * CODE
WIDE = 512
EPS = 1e-06
NEG = -1000000000.0
F32 = jnp.float32
BF16 = jnp.bfloat16
VMEM_BYTES = 56 * 1024 * 1024
BRIEF = pl.CostEstimate(flops=1, bytes_accessed=1, transcendentals=0)

NN = (((1,), (0,)), ((), ()))
NT = (((1,), (1,)), ((), ()))
TN = (((0,), (0,)), ((), ()))


def mm(left, right, dims=NN):
    return lax.dot_general(left, right, dims, preferred_element_type=F32)


def ramp(shape, axis):
    return lax.broadcasted_iota(jnp.int32, shape, axis)


def pack_places(rows_ref, cols_ref, mb, shape, axis):
    places = ramp(shape, axis)
    owner = jnp.zeros(shape, jnp.int32)
    start = jnp.zeros(shape, jnp.int32)
    breadth = jnp.ones(shape, jnp.int32)
    end = jnp.int32(0)
    for slot in range(SLOTS):
        cols = cols_ref[mb, 0, slot]
        here = places >= end
        start = jnp.where(here, end, start)
        breadth = jnp.where(here, cols, breadth)
        end = end + rows_ref[mb, 0, slot] * cols
        owner = owner + (places >= end).astype(jnp.int32)
    inside = places < end
    offset = (places - start).astype(F32)
    row = jnp.floor((offset + 0.5) / breadth.astype(F32)).astype(jnp.int32)
    col = places - start - row * breadth
    code = jnp.where(inside, row * CODE + col, 0)
    return owner, code, inside


def onehot(ids, shape, axis):
    return jnp.where(ids == ramp(shape, axis), 1.0, 0.0).astype(BF16)


def unit_rows(values):
    center = values - jnp.mean(values, axis=-1, keepdims=True)
    inverse = lax.rsqrt(jnp.mean(center * center, axis=-1, keepdims=True) + EPS)
    return center * inverse, inverse


def norm_back(grad_hat, hat, inverse):
    centered = grad_hat - jnp.mean(grad_hat, axis=-1, keepdims=True)
    return inverse * (centered - hat * jnp.mean(grad_hat * hat, axis=-1, keepdims=True))


def normal_parts(u):
    t = 1.0 / (1.0 + (0.3275911 * 0.7071067811865476) * jnp.abs(u))
    falling = jnp.exp(-0.5 * u * u)
    poly = t * (
        0.254829592
        + t * (-0.284496736 + t * (1.421413741 + t * (-1.453152027 + t * 1.061405429)))
    )
    tail = 0.5 * poly * falling
    return jnp.where(u < 0.0, tail, 1.0 - tail), u * falling * 0.3989422804014327


def spread_map(shape, flat_axis, wide_axis):
    flat = ramp(shape, flat_axis)
    wide = ramp(shape, wide_axis)
    row = wide // CODE
    col = wide - row * CODE
    meets = (flat == row * SPAN + col) & (col < GRID) & (row < SPAN)
    return jnp.where(meets, 1.0, 0.0).astype(BF16)


def split_two(values):
    high = values.astype(BF16)
    return high, (values - high.astype(F32)).astype(BF16)


def table_kernel(table_ref, out_ref, wide_ref):
    heads, rel = table_ref.shape
    height = wide_ref.shape[1] // CODE
    flat = -(-rel // 128) * 128
    table = table_ref[...]
    mirror = jnp.where(
        ramp((rel, flat), 0) + ramp((rel, flat), 1) == rel - 1, 1.0, 0.0
    ).astype(BF16)
    spread = spread_map((flat, WIDE), 0, 1)
    for part, piece in enumerate(split_two(table)):
        rev = mm(piece, mirror)
        if height > heads:
            rev = jnp.concatenate([rev, jnp.zeros((height - heads, flat), F32)], axis=0)
        turned = jnp.concatenate(
            [pltpu.roll(rev, (c - (GRID - 1)) % flat, 1) for c in range(CODE)], axis=0
        )
        wide = mm(turned.astype(BF16), spread)
        for at in range(WIDE // 128):
            wide_ref[at] = wide[:, at * 128 : (at + 1) * 128]
        for h in range(heads):
            for at in range(WIDE // 128):
                out_ref[part, h, :, at * 128 : (at + 1) * 128] = wide_ref[
                    at, pl.ds(h, CODE, stride=height), :
                ].astype(BF16)


def table_spread(rel_table):
    _, rel, heads = rel_table.shape
    height = -(-heads // 8) * 8
    return pl.pallas_call(
        table_kernel,
        out_shape=jax.ShapeDtypeStruct((2, heads, CODE, WIDE), BF16),
        scratch_shapes=[pltpu.VMEM((WIDE // 128, CODE * height, 128), F32)],
        compiler_params=pltpu.CompilerParams(vmem_limit_bytes=VMEM_BYTES),
        cost_estimate=BRIEF,
        name="table_spread",
    )(rel_table[0].T)


def table_grad_kernel(rows_ref, cols_ref, ds_hbm, out_ref, ds_scr, dw_scr, wide_ref, sem):
    micro_count, heads, length, _ = ds_hbm.shape
    height, flat = out_ref.shape
    loads = [
        pltpu.make_async_copy(ds_hbm.at[mb], ds_scr.at[mb], sem.at[mb])
        for mb in range(micro_count)
    ]
    for load in loads:
        load.start()
    spread = spread_map((WIDE, flat), 1, 0)
    wide_ref[...] = jnp.zeros_like(wide_ref)
    total = jnp.zeros((heads * CODE, WIDE), F32)
    for mb in range(micro_count):
        _, code_row, _ = pack_places(rows_ref, cols_ref, mb, (1, length), 1)
        place_row = onehot(code_row, (256, length), 0)
        reach = CODE * (GRID - 1)
        ladder = onehot(code_row + reach, (reach + WIDE, length), 0)
        loads[mb].wait()
        for h in range(heads):
            dw_scr[h] = mm(place_row, ds_scr[mb, h]).astype(BF16)
        for r in range(GRID):
            block = jnp.concatenate(
                [dw_scr[h, CODE * r : CODE * (r + 1)] for h in range(heads)], axis=0
            )
            total = total + mm(block, ladder[CODE * r : CODE * r + WIDE], NT)
    for h in range(heads):
        for at in range(WIDE // 128):
            wide_ref[at, pl.ds(h, CODE, stride=height), :] = total[
                h * CODE : (h + 1) * CODE, at * 128 : (at + 1) * 128
            ]
    high, rest = split_two(
        jnp.concatenate([wide_ref[at] for at in range(WIDE // 128)], axis=1)
    )
    turned = mm(high, spread) + mm(rest, spread)
    result = jnp.zeros((height, flat), F32)
    for c in range(GRID):
        result = result + pltpu.roll(
            turned[c * height : (c + 1) * height, :], GRID - 1 - c, 1
        )
    out_ref[...] = result


def table_grad(grid_rows, grid_cols, score_grads, rel):
    micro_count, heads, length, _ = score_grads.shape
    flat = -(-rel // 128) * 128
    height = -(-heads // 8) * 8
    return pl.pallas_call(
        table_grad_kernel,
        out_shape=jax.ShapeDtypeStruct((height, flat), F32),
        in_specs=[pl.BlockSpec(memory_space=pltpu.SMEM)] * 2
        + [pl.BlockSpec(memory_space=pl.ANY)],
        scratch_shapes=[
            pltpu.VMEM(score_grads.shape, BF16),
            pltpu.VMEM((heads, 256, length), BF16),
            pltpu.VMEM((WIDE // 128, CODE * height, 128), F32),
            pltpu.SemaphoreType.DMA((micro_count,)),
        ],
        compiler_params=pltpu.CompilerParams(vmem_limit_bytes=VMEM_BYTES),
        cost_estimate=BRIEF,
        name="table_grad",
    )(grid_rows, grid_cols, score_grads)


SIDES = ("h", "o", "h2", "z", "act")
HELD = ("p", "wt", "br", "m", "dg", "fd")
GRADS = ("df", "du", "db", "ds", "dp", "dx", "sums")
WEIGHTS = ("qkv", "proj", "up", "down")
VECTORS = (
    "n1_gain",
    "n1_shift",
    "query_bias",
    "value_bias",
    "proj_shift",
    "attn_gain",
    "n2_gain",
    "n2_shift",
    "up_shift",
    "down_shift",
    "mlp_gain",
)
SUM_ROWS = 16


def layer_shapes(micro_count, length, width, hidden, heads):
    row = (micro_count, length, width)
    return {
        "h": (row, BF16),
        "p": ((micro_count, length, 3 * width), BF16),
        "wt": ((micro_count, heads, length, length), BF16),
        "o": (row, BF16),
        "br": (row, BF16),
        "m": (row, F32),
        "h2": (row, BF16),
        "dg": ((micro_count, length, hidden), BF16),
        "z": ((micro_count, length, hidden), BF16),
        "fd": (row, BF16),
        "act": (row, BF16),
        "df": (row, BF16),
        "du": ((micro_count, length, hidden), BF16),
        "db": (row, BF16),
        "ds": ((micro_count, heads, length, length), BF16),
        "dp": ((micro_count, length, 3 * width), BF16),
        "dx": (row, F32),
        "sums": ((SUM_ROWS, width), F32),
    }


def forward_body(mb, rows_ref, cols_ref, vec, wide_scr, x_scr, w, scr, tools, wait, keep):
    bias_scr, ladder_scr, score_scr = tools
    length, width = x_scr.shape
    heads = scr["wt"].shape[0]
    hidden = scr["z"].shape[1]
    head_dim = width // heads
    pair = 2 * head_dim
    owner_col, code_col, _ = pack_places(rows_ref, cols_ref, mb, (length, 1), 0)
    owner_row, code_row, _ = pack_places(rows_ref, cols_ref, mb, (1, length), 1)
    lanes = ramp((length, 256), 1)
    place_col = jnp.where(
        (lanes == code_col) | (lanes == owner_col + PLACES), 1.0, 0.0
    ).astype(BF16)
    place_col = jnp.concatenate([place_col, place_col], axis=1)
    reach = CODE * (GRID - 1)
    ladder_scr[...] = onehot(code_row + reach, ladder_scr.shape, 0)
    spare = ramp((256 - PLACES, length), 0)
    walls = jnp.where(spare == owner_row, 0.0, NEG).astype(BF16)
    blank = jnp.zeros((256 - PLACES, length), BF16)
    for h in range(heads):
        bias_scr[h, PLACES:256, :] = walls
        bias_scr[h, 256 + PLACES :, :] = blank
    wait("wide")
    for r in range(GRID):
        begin = CODE * (GRID - 1 - r)
        low = begin // 128 * 128
        high = -(-(begin + PLACES) // 128) * 128
        rung = ladder_scr[CODE * r + low : CODE * r + high, :]
        for part in range(2):
            block = mm(
                wide_scr[part, :, :, low:high].reshape(heads * CODE, high - low), rung
            ).astype(BF16)
            at = 256 * part + CODE * r
            for h in range(heads):
                bias_scr[h, at : at + CODE, :] = block[h * CODE : (h + 1) * CODE]

    wait("x")
    hat, _ = unit_rows(x_scr[...].astype(F32))
    scr["h"][...] = (hat * vec["n1_gain"][...] + vec["n1_shift"][...]).astype(BF16)
    keep("h")

    scale = head_dim ** (-0.5)
    h_all = scr["h"][...]
    p_scr = scr["p"]
    wait("qkv")
    p_scr[:, :width] = (
        (mm(h_all, w["qkv"][:, :width]) + vec["query_bias"][...]).astype(BF16) * scale
    ).astype(BF16)
    p_scr[:, width : 2 * width] = mm(h_all, w["qkv"][:, width : 2 * width]).astype(BF16)
    p_scr[:, 2 * width :] = (
        mm(h_all, w["qkv"][:, 2 * width :]) + vec["value_bias"][...]
    ).astype(BF16)
    keep("p")

    first = ramp((length, pair), 1) < head_dim
    zero = jnp.zeros((length, pair), BF16)
    for head in range(heads):
        at = head // 2 * pair
        queries = p_scr[:, at : at + pair]
        keys_all = p_scr[:, width + at : width + at + pair]
        own = jnp.where(first == (head % 2 == 0), queries, zero)
        score_scr[head] = mm(own, keys_all, NT) + mm(place_col, bias_scr[head])
    for head in range(heads):
        for at in range(0, length, 64):
            scores = score_scr[head, at : at + 64]
            raised = jnp.exp(scores - jnp.max(scores, axis=-1, keepdims=True))
            share = 1.0 / jnp.sum(raised, axis=-1, keepdims=True)
            scr["wt"][head, at : at + 64] = (raised * share).astype(BF16)
    keep("wt")
    for head in range(0, heads, 2):
        at = head // 2 * pair
        values_all = p_scr[:, 2 * width + at : 2 * width + at + pair]
        mixed = [mm(scr["wt"][head + side], values_all) for side in range(2)]
        scr["o"][:, at : at + pair] = jnp.where(first, mixed[0], mixed[1]).astype(BF16)
    keep("o")

    wait("proj")
    branch = mm(scr["o"][...], w["proj"][...]) + vec["proj_shift"][...]
    scr["br"][...] = branch.astype(BF16)
    keep("br")
    middle = x_scr[...].astype(F32) + vec["attn_gain"][...] * branch
    scr["m"][...] = middle
    keep("m")
    hat, _ = unit_rows(middle)
    scr["h2"][...] = (hat * vec["n2_gain"][...] + vec["n2_shift"][...]).astype(BF16)
    keep("h2")

    wait("up")
    wait("down")
    second = scr["h2"][...]
    tile = width
    down = None
    for at in range(0, hidden, tile):
        upward = mm(second, w["up"][:, at : at + tile]) + vec["up_shift"][:, at : at + tile]
        cdf, leaning = normal_parts(upward)
        z = (upward * cdf).astype(BF16)
        scr["z"][:, at : at + tile] = z
        scr["dg"][:, at : at + tile] = (cdf + leaning).astype(BF16)
        for name in ("z", "dg"):
            keep(name, slice(None), pl.ds(at, tile))
        term = mm(z, w["down"][at : at + tile, :])
        down = term if down is None else down + term
    downward = down + vec["down_shift"][...]
    scr["act"][...] = (scr["m"][...] + vec["mlp_gain"][...] * downward).astype(BF16)
    keep("send")
    keep("act")
    scr["fd"][...] = downward.astype(BF16)
    keep("fd")


def backward_body(adds, kept, vec, g_scr, x_scr, w, got, scr, tools, wait, keep):
    do_scr, dwt_scr, send_scr = tools
    length, width = x_scr.shape
    heads = got["wt"].shape[0]
    hidden = got["dg"].shape[1]
    head_dim = width // heads
    pair = 2 * head_dim

    def total(values):
        return jnp.sum(values, axis=0, keepdims=True)

    sums = scr["sums"]

    def note(row, values):
        if adds:
            values = values + sums[row : row + 1, :]
        sums[row : row + 1, :] = values

    wait("sums")
    wait("g")
    grad_out = g_scr[...].astype(F32) * kept
    wait("fd")
    note(9, total(grad_out * got["fd"][...].astype(F32)))
    df = (grad_out * vec["mlp_gain"][...]).astype(BF16)
    scr["df"][...] = df
    keep("df")
    note(8, total(df.astype(F32)))

    tile = width
    dh2 = None
    for at in range(0, hidden, tile):
        wait("down%d" % at)
        wait("dg%d" % at)
        wait("up%d" % at)
        dz = mm(scr["df"][...], w["down"][at : at + tile, :], NT)
        du = (dz * got["dg"][:, at : at + tile].astype(F32)).astype(BF16)
        scr["du"][:, at : at + tile] = du
        keep("du", slice(None), pl.ds(at, tile))
        note(10 + at // tile, total(du.astype(F32)))
        term = mm(du, w["up"][:, at : at + tile], NT)
        dh2 = term if dh2 is None else dh2 + term
    for row in range(10 + hidden // tile, SUM_ROWS):
        sums[row : row + 1, :] = jnp.zeros((1, width), F32)

    wait("m")
    hat, inverse = unit_rows(got["m"][...])
    note(6, total(dh2 * hat))
    note(7, total(dh2))
    dm = g_scr[...].astype(F32) * kept + norm_back(dh2 * vec["n2_gain"][...], hat, inverse)
    scr["dx"][...] = dm
    wait("br")
    note(5, total(dm * got["br"][...].astype(F32)))
    db = (dm * vec["attn_gain"][...]).astype(BF16)
    scr["db"][...] = db
    keep("db")
    note(4, total(db.astype(F32)))

    wait("proj")
    do_scr[...] = mm(scr["db"][...], w["proj"][...], NT).astype(BF16)
    wait("p")
    wait("wt")
    first = ramp((length, pair), 1) < head_dim
    zero = jnp.zeros((length, pair), BF16)
    scale = head_dim ** (-0.5)
    p_scr, dp_scr = got["p"], scr["dp"]
    for head in range(heads):
        at = head // 2 * pair
        own = jnp.where(first == (head % 2 == 0), do_scr[:, at : at + pair], zero)
        dwt_scr[head] = mm(own, p_scr[:, 2 * width + at : 2 * width + at + pair], NT)
    for head in range(heads):
        for at in range(0, length, 64):
            dwt = dwt_scr[head, at : at + 64]
            probs = got["wt"][head, at : at + 64].astype(F32)
            inner = jnp.sum(probs * dwt, axis=-1, keepdims=True)
            scr["ds"][head, at : at + 64] = (probs * (dwt - inner)).astype(BF16)
    keep("ds")
    for head in range(0, heads, 2):
        at = head // 2 * pair
        queries = p_scr[:, at : at + pair]
        keys_all = p_scr[:, width + at : width + at + pair]
        dout = do_scr[:, at : at + pair]
        both = []
        for here in (head, head + 1):
            ds = scr["ds"][here]
            both.append(
                (
                    mm(ds, keys_all) * scale,
                    mm(ds, queries, TN),
                    mm(got["wt"][here], dout, TN),
                )
            )
        for part, (even, odd) in enumerate(zip(*both)):
            dp_scr[:, part * width + at : part * width + at + pair] = jnp.where(
                first, even, odd
            ).astype(BF16)
    keep("dp")

    wait("qkv")
    dh = mm(dp_scr[...], w["qkv"][...], NT)
    wait("x")
    hat, inverse = unit_rows(x_scr[...].astype(F32))
    dx = scr["dx"][...] + norm_back(dh * vec["n1_gain"][...], hat, inverse)
    send_scr[...] = dx.astype(BF16)
    keep("send")
    scr["dx"][...] = dx
    keep("dx")
    note(0, total(dh * hat))
    note(1, total(dh))
    note(2, total(dp_scr[:, :width].astype(F32)))
    note(3, total(dp_scr[:, 2 * width :].astype(F32)))
    keep("sums")


def layer_kernel(section, mb, kind, adds, layout, *refs):
    named = [dict() for _ in layout]
    for group, names in zip(named, layout):
        group.update(zip(names, refs))
        refs = refs[len(names) :]
    given, outs, own = named
    sec_ref, rows_ref, cols_ref = [given[name] for name in ("sec", "rows", "cols")]
    length, width = own["x"].shape

    @pl.when(sec_ref[0] == section)
    def _():
        loads, stores = {}, []

        def wait(name):
            if name in loads:
                loads.pop(name).wait()

        def keep(name, *piece):
            if name not in outs:
                return
            dst = outs[name]
            if name == "send":
                src = own["send"] if kind != "forward" else own["act"]
            else:
                src = own[name]
                dst = dst if name == "sums" else dst.at[mb]
            if piece:
                src, dst = src.at[piece], dst.at[piece]
            store = pltpu.make_async_copy(src, dst, own["out_sem"].at[len(stores)])
            store.start()
            stores.append(store)

        order = []
        x_src = given["x"] if section else given["x"].at[mb]
        hidden = own["dg"].shape[1]
        if kind != "backward":
            order += [("wide", given["wide"], own["wide"]), ("x", x_src, own["x"])]
            order += [(name, given[name].at[0], own[name]) for name in WEIGHTS]
        if kind != "forward":
            if adds:
                order.append(("sums", outs["sums"], own["sums"]))
            order.append(("g", given["g"].at[mb] if section else given["g"], own["g"]))
        if kind == "backward":
            order.append(("fd", given["fd"].at[mb], own["fd"]))
            for at in range(0, hidden, width):
                strip, piece = pl.ds(at, width), (slice(None), pl.ds(at, width))
                order += [
                    ("down%d" % at, given["down"].at[0].at[strip], own["down"].at[strip]),
                    ("dg%d" % at, given["dg"].at[mb].at[piece], own["dg"].at[piece]),
                    ("up%d" % at, given["up"].at[0].at[piece], own["up"].at[piece]),
                ]
            order += [
                ("m", given["m"].at[mb], own["m"]),
                ("br", given["br"].at[mb], own["br"]),
                ("proj", given["proj"].at[0], own["proj"]),
                ("p", given["p"].at[mb], own["p"]),
                ("wt", given["wt"].at[mb], own["wt"]),
                ("qkv", given["qkv"].at[0], own["qkv"]),
                ("x", x_src, own["x"]),
            ]
        for place, (name, src, dst) in enumerate(order):
            loads[name] = pltpu.make_async_copy(src, dst, own["in_sem"].at[place])
            loads[name].start()
        if kind != "backward":
            tools = (own["bias"], own["ladder"], own["score"])
            forward_body(
                mb, rows_ref, cols_ref, given, own["wide"], own["x"], own, own, tools, wait, keep
            )
        if kind != "forward":
            kept = 1.0
            if section:
                _, _, inside = pack_places(rows_ref, cols_ref, mb, (length, 1), 0)
                kept = jnp.where(inside, 1.0, 0.0)
            tools = (own["do"], own["score"], own["send"])
            backward_body(
                adds, kept, given, own["g"], own["x"], own, own, own, tools, wait, keep
            )
        for store in stores:
            store.wait()


def run_layer(section, mb, kind, adds, inputs, vectors, weights, prior):
    smem = pl.BlockSpec(memory_space=pltpu.SMEM)
    vmem = pl.BlockSpec(memory_space=pltpu.VMEM)
    hbm = pl.BlockSpec(memory_space=pl.ANY)
    length, width = inputs["x"].shape[-2:]
    micro_count = inputs["rows"].shape[0]
    hidden = weights["up"].shape[2]
    heads = inputs["heads"]
    inputs = {name: array for name, array in inputs.items() if name != "heads"}
    shapes = layer_shapes(micro_count, length, width, hidden, heads)
    results = []
    if kind != "backward":
        results += SIDES
    if kind == "forward":
        results += HELD
    if kind != "forward":
        results += GRADS
    out_shape = [jax.ShapeDtypeStruct(*shapes[name]) for name in results]
    sends = kind == "forward" or section == 1
    if sends:
        results.append("send")
        out_shape.append(jax.ShapeDtypeStruct((length, width), BF16))
    operands = {**inputs, **vectors, **weights}
    specs = []
    for name in operands:
        specs.append(smem if name in ("sec", "rows", "cols") else vmem if name in VECTORS else hbm)
    held = [name for name in results if name in prior]
    operands_all = {**operands, **{"prior " + name: prior[name] for name in held}}
    block = lambda name: pltpu.VMEM(shapes[name][0][1:], shapes[name][1])
    scratch = {"x": pltpu.VMEM((length, width), BF16)}
    for name in WEIGHTS:
        scratch[name] = pltpu.VMEM(weights[name].shape[1:], BF16)
    for name in HELD:
        scratch[name] = block(name)
    scratch["score"] = pltpu.VMEM((heads, length, length), F32)
    if kind != "backward":
        for name in SIDES:
            scratch[name] = block(name)
        scratch["wide"] = pltpu.VMEM(inputs["wide"].shape, BF16)
        scratch["bias"] = pltpu.VMEM((heads, 512, length), BF16)
        scratch["ladder"] = pltpu.VMEM((CODE * (GRID - 1) + WIDE, length), BF16)
    if kind != "forward":
        for name in GRADS[:-1]:
            scratch[name] = block(name)
        scratch["sums"] = pltpu.VMEM((SUM_ROWS, width), F32)
        for name in ("g", "do", "send"):
            scratch[name] = pltpu.VMEM((length, width), BF16)
    scratch["in_sem"] = pltpu.SemaphoreType.DMA((10 + 3 * (hidden // width),))
    scratch["out_sem"] = pltpu.SemaphoreType.DMA((len(results) + 2 * (hidden // width),))
    layout = (list(operands_all), results, list(scratch))
    made = pl.pallas_call(
        functools.partial(layer_kernel, section, mb, kind, adds, layout),
        out_shape=out_shape,
        in_specs=specs + [hbm] * len(held),
        out_specs=[hbm] * len(results),
        scratch_shapes=list(scratch.values()),
        input_output_aliases={
            len(operands) + at: results.index(name) for at, name in enumerate(held)
        },
        compiler_params=pltpu.CompilerParams(vmem_limit_bytes=VMEM_BYTES),
        cost_estimate=BRIEF,
        name="layer_" + kind,
    )(*operands_all.values())
    return dict(zip(results, made))


def turn_kernel(chunk_count, *refs):
    count = len(refs) // 4
    sources, outs, refs = refs[:count], refs[count : 2 * count], refs[2 * count :]
    lefts, turned, refs = refs[:count], refs[count : 2 * count], refs[2 * count :]
    in_sem, out_sem = refs
    loads = [
        pltpu.make_async_copy(src, dst, in_sem.at[at])
        for at, (src, dst) in enumerate(zip(sources, lefts))
    ]
    stores = [
        pltpu.make_async_copy(src, dst, out_sem.at[at])
        for at, (src, dst) in enumerate(zip(turned, outs))
    ]
    for load in loads:
        load.start()
    for left, out, load, store in zip(lefts, turned, loads, stores):
        load.wait()
        micro_count, length, width = left.shape
        step = width // chunk_count
        strip = 256 if width % 256 == 0 else width
        for mb in range(micro_count):
            flipped = jnp.concatenate(
                [left[mb, :, at : at + strip].T for at in range(0, width, strip)], axis=0
            )
            for chunk in range(chunk_count):
                core_of, to = chunk % 2, chunk // 2 * step
                out[core_of, to : to + step, mb * length : (mb + 1) * length] = flipped[
                    chunk * step : (chunk + 1) * step, :
                ]
        store.start()
    for store in stores:
        store.wait()


def turn_lefts(chunk_count, lefts):
    hbm = pl.BlockSpec(memory_space=pl.ANY)
    shapes = [(2, left.shape[2] // 2, left.shape[0] * left.shape[1]) for left in lefts]
    return pl.pallas_call(
        functools.partial(turn_kernel, chunk_count),
        out_shape=[jax.ShapeDtypeStruct(shape, BF16) for shape in shapes],
        in_specs=[hbm] * len(lefts),
        out_specs=[hbm] * len(lefts),
        scratch_shapes=[pltpu.VMEM(left.shape, BF16) for left in lefts]
        + [pltpu.VMEM(shape, BF16) for shape in shapes]
        + [pltpu.SemaphoreType.DMA((len(lefts),))] * 2,
        compiler_params=pltpu.CompilerParams(vmem_limit_bytes=VMEM_BYTES),
        cost_estimate=BRIEF,
        name="turn_lefts",
    )(*lefts)


def placed(chunk, order):
    place = 0
    for bit in order:
        place = 2 * place + (chunk >> (bit - 1) & 1)
    return place


def weight_kernel(parts, fresh, orders, sides, sec_ref, *refs):
    operands, refs = refs[: 2 * parts], refs[2 * parts :]
    if fresh:
        (grad_hbm, gain_ref), refs = refs[:2], refs[2:]
    count = len(sides)
    outs, refs = refs[:count], refs[count:]
    lefts, rights, refs = refs[:parts], refs[parts : 2 * parts], refs[2 * parts :]
    scrs, (in_sem, out_sem), refs = refs[:count], refs[count : count + 2], refs[count + 2 :]
    halves = [sec_ref[1] if side else 1 - sec_ref[1] for side in sides]
    strip = 384
    loads = []
    for part in range(parts):
        pairs = [(operands[2 * part + 1], rights[part])]
        for which, half in enumerate(halves):
            for low in range(0, lefts[part].shape[1], strip):
                rows = pl.ds(low, strip)
                pairs.append(
                    (operands[2 * part].at[half].at[rows], lefts[part].at[which].at[rows])
                )
        loads.append([])
        for kind, (src, dst) in enumerate(pairs):
            load = pltpu.make_async_copy(src, dst, in_sem.at[part, kind])
            load.start()
            loads[part].append(load)
    if fresh:
        grad_scr = refs[0]
        grad_copy = pltpu.make_async_copy(grad_hbm, grad_scr, in_sem.at[parts, 0])
        grad_copy.start()
        grad_copy.wait()
        loads[0][0].wait()

        @pl.when(sec_ref[0] == 0)
        def _():
            rights[0][rights[0].shape[0] - 1] = (grad_scr[...].astype(F32) * gain_ref[...]).astype(BF16)

    stores = []
    unit = scrs[0].shape[2]
    tile = min(768, unit)
    for which in range(count):
        at_col = 0
        for part in range(parts):
            if which == 0 and not fresh:
                loads[part][0].wait()
            micro_count, length, cols = rights[part].shape
            height = lefts[part].shape[1]
            pieces = height // strip
            for at in range(0, cols, tile):
                right = rights[part][:, :, at : at + tile].reshape(micro_count * length, tile)
                cut, place = divmod(at_col + at, unit)
                step = height >> len(orders[cut])
                for low in range(0, height, strip):
                    if at == 0:
                        loads[part][1 + which * pieces + low // strip].wait()
                    block = mm(lefts[part][which, low : low + strip], right).astype(BF16)
                    for top in range(0, strip, step):
                        to = step * placed((low + top) // step, orders[cut])
                        scrs[which][cut, to : to + step, place : place + tile] = block[
                            top : top + step
                        ]
                piece = (slice(None), pl.ds(place, tile))
                store = pltpu.make_async_copy(
                    scrs[which].at[cut].at[piece],
                    outs[which].at[cut].at[piece],
                    out_sem.at[len(stores)],
                )
                store.start()
                stores.append(store)
            at_col += cols
    for store in stores:
        store.wait()


def weight_terms(orders, sides, sec, pairs, fresh=()):
    hbm = pl.BlockSpec(memory_space=pl.ANY)
    vmem = pl.BlockSpec(memory_space=pltpu.VMEM)
    smem = pl.BlockSpec(memory_space=pltpu.SMEM)
    height = pairs[0][0].shape[1]
    cuts = len(orders)
    unit = sum(right.shape[2] for _, right in pairs) // cuts
    tiles = -(-unit // min(768, unit)) * cuts * len(sides)
    operands = [side for pair in pairs for side in pair]
    scratch = [pltpu.VMEM((len(sides), *left.shape[1:]), BF16) for left, _ in pairs]
    scratch += [pltpu.VMEM(right.shape, BF16) for _, right in pairs]
    scratch += [pltpu.VMEM((cuts, height, unit), BF16) for _ in sides]
    scratch += [
        pltpu.SemaphoreType.DMA((len(pairs) + 1, 1 + 2 * (height // 384))),
        pltpu.SemaphoreType.DMA((tiles,)),
    ]
    if fresh:
        scratch.append(pltpu.VMEM(fresh[0].shape, BF16))
    return pl.pallas_call(
        functools.partial(weight_kernel, len(pairs), bool(fresh), orders, sides),
        out_shape=[jax.ShapeDtypeStruct((cuts, height, unit), BF16) for _ in sides],
        in_specs=[smem] + [hbm] * len(operands) + ([hbm, vmem] if fresh else []),
        out_specs=[hbm] * len(sides),
        scratch_shapes=scratch,
        compiler_params=pltpu.CompilerParams(vmem_limit_bytes=VMEM_BYTES),
        cost_estimate=BRIEF,
        name="weight_terms",
    )(sec, *operands, *fresh)


def swap(block, bit):
    devices = range(lax.axis_size("dp"))
    return lax.ppermute(block, "dp", [(i, i ^ bit) for i in devices])


def after(value, *others):
    return lax.optimization_barrier((value, *others))[0]


def half_of(block, side):
    block = block.reshape(2, block.shape[0] // 2, block.shape[1])
    return lax.dynamic_index_in_dim(block, side, 0, keepdims=False)


def total_of(blocks):
    return functools.reduce(jnp.add, [block.astype(F32) for block in blocks])


def next_sum(mine, come, order, rank):
    side = (rank >> order[0]) & 1
    sent = total_of([half_of(mine, 1 - side), half_of(come, 1 - side)]).astype(BF16)
    kept = total_of([half_of(mine, side), half_of(come, side)]).astype(BF16)
    come = swap(sent, 1 << order[0])
    return lax.optimization_barrier(kept), come, order[1:], sent


def full_sum(values):
    size = lax.axis_size("dp")
    if size & (size - 1):
        return lax.psum(values, "dp")
    bit = 1
    while bit < size:
        values = values + swap(values, bit)
        bit *= 2
    return values


def shards(
    patches_in,
    grid_rows,
    grid_cols,
    norm1_gain,
    norm1_bias,
    qkv_weight,
    q_bias,
    v_bias,
    rel_table,
    proj_weight,
    proj_bias,
    attn_scale,
    norm2_gain,
    norm2_bias,
    fc1_weight,
    fc1_bias,
    fc2_weight,
    fc2_bias,
    mlp_scale,
    cotangent,
):
    rank = lax.axis_index("dp")
    dp_size = lax.axis_size("dp")
    micro_count, length, width = patches_in.shape
    hidden = fc1_bias.shape[1]
    rel, heads = rel_table.shape[1:]
    sec = jnp.stack([lax.axis_index("section"), rank % 2]).astype(jnp.int32)
    weights = dict(zip(WEIGHTS, (qkv_weight, proj_weight, fc1_weight, fc2_weight)))
    vectors = dict(
        zip(
            VECTORS,
            (
                norm1_gain,
                norm1_bias,
                q_bias,
                v_bias,
                proj_bias,
                attn_scale,
                norm2_gain,
                norm2_bias,
                fc1_bias,
                fc2_bias,
                mlp_scale,
            ),
        )
    )
    common = {"sec": sec, "rows": grid_rows, "cols": grid_cols, "heads": heads}
    wide = table_spread(rel_table)

    cache, grads = {}, {}
    moved, returned = [], []
    for mb in range(micro_count):
        inputs = {**common, "x": patches_in, "wide": wide}
        cache = run_layer(0, mb, "forward", False, inputs, vectors, weights, cache)
        moved.append(lax.ppermute(cache.pop("send"), "section", [(0, 1)]))
    for mb in range(micro_count):
        inputs = {**common, "x": moved[mb], "wide": wide, "g": cotangent}
        made = run_layer(1, mb, "both", mb > 0, inputs, vectors, weights, {**cache, **grads})
        returned.append(lax.ppermute(made.pop("send"), "section", [(1, 0)]))
        cache.update({name: made[name] for name in SIDES})
        grads = {name: made[name] for name in GRADS}

    def backward(mb, grad, prior):
        inputs = {**common, "x": patches_in, "g": grad}
        inputs.update({name: cache[name] for name in HELD})
        return run_layer(0, mb, "backward", mb > 0, inputs, vectors, weights, prior)

    spread_out = dp_size == 16 and width % (16 * dp_size) == 0
    if spread_out:
        lefts = [after(cache[name], grads["dx"]) for name in ("z", "h2", "o", "h")]
        z_turned, h2_turned, o_turned, h_turned = turn_lefts(dp_size, lefts)
    for mb in range(micro_count - 1):
        grads = backward(mb, returned[mb], grads)
    last = returned[-1]
    if spread_out:
        one, two = (1, 2, 3), (2, 1, 3)

        def paired(send, keep, orders):
            got = swap(send, 1)
            return [(keep[cut], got[cut], order, None) for cut, order in enumerate(orders)]

        def follow(units, *before):
            done = []
            for mine, come, order, _ in units:
                done.append(next_sum(mine, after(come, *before), order, rank))
            return done

        def moving(units):
            return [sent for _, _, _, sent in units]

        def ended(units, *before):
            return jnp.concatenate(
                [total_of([mine, after(come, *before)]) for mine, come, _, _ in units], axis=1
            )

        orders = (one, two)
        operands = ([(z_turned, grads["df"])], (last, mlp_scale))
        (send,) = weight_terms(orders, (0,), sec, *operands)
        (keep,) = weight_terms(orders, (1,), after(sec, send), *operands)
        down = follow(paired(send, keep, orders))
        grads = backward(micro_count - 1, after(last, *moving(down)), grads)
        down = follow(down, grads["sums"])
        send, keep = weight_terms(
            orders,
            (0, 1),
            sec,
            [(after(o_turned, *moving(down)), grads["db"]), (h_turned, grads["dp"])],
        )
        attn = paired(send, keep, orders)
        send, keep = weight_terms(
            orders, (0, 1), sec, [(after(h2_turned, send), grads["du"])]
        )
        up = paired(send, keep, orders)
        attn = follow(attn, send)
        down = follow(down, *moving(attn))
        up = follow(up, *moving(down))
        rev = table_grad(grid_rows, grid_cols, after(grads["ds"], *moving(up)), rel)
        small = jnp.concatenate([grads["sums"], rev], axis=0)
        small = small + swap(small, 1)
        attn = follow(attn, small)
        small = small + swap(after(small, *moving(attn)), 2)
        down_grad = ended(down, small)
        up = follow(up, down_grad)
        small = small + swap(after(small, *moving(up)), 4)
        attn = follow(attn, small)
        small = small + swap(after(small, *moving(attn)), 8)
        up = follow(up, small)
        attn_grad = ended(attn, *moving(up))
        up_grad = ended(up, attn_grad)
        proj_grad, qkv_grad = attn_grad[:, :width], attn_grad[:, width:]
        sums, rev = small[:SUM_ROWS], small[SUM_ROWS:]
    else:
        grads = backward(micro_count - 1, last, grads)

        def plain(left, right):
            term = jnp.einsum("mrk,mrn->kn", left, right, preferred_element_type=F32)
            return lax.psum_scatter(term, "dp", scatter_dimension=0, tiled=True)

        down_grad = plain(cache["z"], grads["df"])
        up_grad = plain(cache["h2"], grads["du"])
        proj_grad = plain(cache["o"], grads["db"])
        qkv_grad = plain(cache["h"], grads["dp"])
        rev = full_sum(table_grad(grid_rows, grid_cols, grads["ds"], rel))
        sums = full_sum(grads["sums"])
    rel_grad = jnp.flip(rev[:heads, :rel].T, 0)
    up_shift_grad = sums[10 : 10 + hidden // width].reshape(1, hidden)
    small = [sums[row : row + 1] for row in range(10)]
    return (
        cache["act"][None],
        grads["dx"][None],
        small[0],
        small[1],
        qkv_grad[None],
        small[2],
        small[3],
        rel_grad[None],
        proj_grad[None],
        small[4],
        small[5],
        small[6],
        small[7],
        up_grad[None],
        up_shift_grad,
        down_grad[None],
        small[8],
        small[9],
    )


def solution(mesh):
    layer_row = P("section", None)
    layer_matrix = P("section", None, None)
    packs = P(None, "dp", None)
    scattered = P("section", "dp", None)
    in_specs = (
        packs,
        packs,
        packs,
        layer_row,
        layer_row,
        layer_matrix,
        layer_row,
        layer_row,
        layer_matrix,
        layer_matrix,
        layer_row,
        layer_row,
        layer_row,
        layer_row,
        layer_matrix,
        layer_row,
        layer_matrix,
        layer_row,
        layer_row,
        packs,
    )
    out_specs = (
        P("section", None, "dp", None),
        P("section", None, "dp", None),
        layer_row,
        layer_row,
        scattered,
        layer_row,
        layer_row,
        layer_matrix,
        scattered,
        layer_row,
        layer_row,
        layer_row,
        layer_row,
        scattered,
        layer_row,
        scattered,
        layer_row,
        layer_row,
    )
    return jax.shard_map(
        shards, mesh=mesh, in_specs=in_specs, out_specs=out_specs, check_vma=False
    )
```

```python
import functools
import types

import jax
import jax.numpy as jnp
from jax import lax
from jax.experimental import pallas as pl
from jax.experimental.pallas import tpu as pltpu
from jax.sharding import PartitionSpec as P

SLOTS = 4
GRID = 14
SPAN = 2 * GRID - 1
CODE = 16
PLACES = GRID * CODE
WIDE = 512
EPS = 1e-06
NEG = -1000000000.0
F32 = jnp.float32
BF16 = jnp.bfloat16
VMEM_BYTES = 56 * 1024 * 1024
BRIEF = pl.CostEstimate(flops=1, bytes_accessed=1, transcendentals=0)

NN = (((1,), (0,)), ((), ()))
NT = (((1,), (1,)), ((), ()))
TN = (((0,), (0,)), ((), ()))


def mm(left, right, dims=NN):
    return lax.dot_general(left, right, dims, preferred_element_type=F32)


def ramp(shape, axis):
    return lax.broadcasted_iota(jnp.int32, shape, axis)


def pack_places(rows_ref, cols_ref, mb, shape, axis):
    places = ramp(shape, axis)
    owner = jnp.zeros(shape, jnp.int32)
    start = jnp.zeros(shape, jnp.int32)
    breadth = jnp.ones(shape, jnp.int32)
    end = jnp.int32(0)
    for slot in range(SLOTS):
        cols = cols_ref[mb, 0, slot]
        here = places >= end
        start = jnp.where(here, end, start)
        breadth = jnp.where(here, cols, breadth)
        end = end + rows_ref[mb, 0, slot] * cols
        owner = owner + (places >= end).astype(jnp.int32)
    inside = places < end
    offset = (places - start).astype(F32)
    row = jnp.floor((offset + 0.5) / breadth.astype(F32)).astype(jnp.int32)
    col = places - start - row * breadth
    code = jnp.where(inside, row * CODE + col, 0)
    return owner, code, inside


def onehot(ids, shape, axis):
    return jnp.where(ids == ramp(shape, axis), 1.0, 0.0).astype(BF16)


def unit_rows(values):
    center = values - jnp.mean(values, axis=-1, keepdims=True)
    inverse = lax.rsqrt(jnp.mean(center * center, axis=-1, keepdims=True) + EPS)
    return center * inverse, inverse


def norm_back(grad_hat, hat, inverse):
    centered = grad_hat - jnp.mean(grad_hat, axis=-1, keepdims=True)
    return inverse * (centered - hat * jnp.mean(grad_hat * hat, axis=-1, keepdims=True))


def normal_parts(u):
    t = 1.0 / (1.0 + (0.3275911 * 0.7071067811865476) * jnp.abs(u))
    falling = jnp.exp(-0.5 * u * u)
    poly = t * (
        0.254829592
        + t * (-0.284496736 + t * (1.421413741 + t * (-1.453152027 + t * 1.061405429)))
    )
    tail = 0.5 * poly * falling
    return jnp.where(u < 0.0, tail, 1.0 - tail), u * falling * 0.3989422804014327


def spread_map(shape, flat_axis, wide_axis):
    flat = ramp(shape, flat_axis)
    wide = ramp(shape, wide_axis)
    row = wide // CODE
    col = wide - row * CODE
    meets = (flat == row * SPAN + col) & (col < GRID) & (row < SPAN)
    return jnp.where(meets, 1.0, 0.0).astype(BF16)


def split_two(values):
    high = values.astype(BF16)
    return high, (values - high.astype(F32)).astype(BF16)


def table_kernel(table_ref, out_ref, wide_ref):
    heads, _, rel = table_ref.shape
    height = wide_ref.shape[1] // CODE
    flat = -(-rel // 128) * 128
    table = table_ref[:, 0, :]
    mirror = jnp.where(
        ramp((rel, flat), 0) + ramp((rel, flat), 1) == rel - 1, 1.0, 0.0
    ).astype(BF16)
    spread = spread_map((flat, WIDE), 0, 1)
    for part, piece in enumerate(split_two(table)):
        rev = mm(piece, mirror)
        if height > heads:
            rev = jnp.concatenate([rev, jnp.zeros((height - heads, flat), F32)], axis=0)
        turned = jnp.concatenate(
            [pltpu.roll(rev, (c - (GRID - 1)) % flat, 1) for c in range(CODE)], axis=0
        )
        wide = mm(turned.astype(BF16), spread)
        for at in range(WIDE // 128):
            wide_ref[at] = wide[:, at * 128 : (at + 1) * 128]
        for h in range(heads):
            for at in range(WIDE // 128):
                out_ref[part, h, :, at * 128 : (at + 1) * 128] = wide_ref[
                    at, pl.ds(h, CODE, stride=height), :
                ].astype(BF16)


def table_spread(rel_table):
    _, rel, heads = rel_table.shape
    height = -(-heads // 8) * 8
    return pl.pallas_call(
        table_kernel,
        out_shape=jax.ShapeDtypeStruct((2, heads, CODE, WIDE), BF16),
        scratch_shapes=[pltpu.VMEM((WIDE // 128, CODE * height, 128), F32)],
        compiler_params=pltpu.CompilerParams(vmem_limit_bytes=VMEM_BYTES),
        cost_estimate=BRIEF,
        name="table_spread",
    )(jnp.transpose(rel_table, (2, 0, 1)))


def table_grad_kernel(rows_ref, cols_ref, ds_hbm, out_ref, ds_scr, dw_scr, wide_ref, sem):
    micro_count, heads, length, _ = ds_hbm.shape
    height, flat = out_ref.shape
    loads = [
        pltpu.make_async_copy(ds_hbm.at[mb], ds_scr.at[mb], sem.at[mb])
        for mb in range(micro_count)
    ]
    for load in loads:
        load.start()
    spread = spread_map((WIDE, flat), 1, 0)
    wide_ref[...] = jnp.zeros_like(wide_ref)
    total = jnp.zeros((heads * CODE, WIDE), F32)
    for mb in range(micro_count):
        _, code_row, _ = pack_places(rows_ref, cols_ref, mb, (1, length), 1)
        place_row = onehot(code_row, (256, length), 0)
        reach = CODE * (GRID - 1)
        ladder = onehot(code_row + reach, (reach + WIDE, length), 0)
        loads[mb].wait()
        for h in range(heads):
            dw_scr[h] = mm(place_row, ds_scr[mb, h]).astype(BF16)
        for r in range(GRID):
            block = jnp.concatenate(
                [dw_scr[h, CODE * r : CODE * (r + 1)] for h in range(heads)], axis=0
            )
            total = total + mm(block, ladder[CODE * r : CODE * r + WIDE], NT)
    for h in range(heads):
        for at in range(WIDE // 128):
            wide_ref[at, pl.ds(h, CODE, stride=height), :] = total[
                h * CODE : (h + 1) * CODE, at * 128 : (at + 1) * 128
            ]
    high, rest = split_two(
        jnp.concatenate([wide_ref[at] for at in range(WIDE // 128)], axis=1)
    )
    turned = mm(high, spread) + mm(rest, spread)
    result = jnp.zeros((height, flat), F32)
    for c in range(GRID):
        result = result + pltpu.roll(
            turned[c * height : (c + 1) * height, :], GRID - 1 - c, 1
        )
    out_ref[...] = result


def table_grad(grid_rows, grid_cols, score_grads, rel):
    micro_count, heads, length, _ = score_grads.shape
    flat = -(-rel // 128) * 128
    height = -(-heads // 8) * 8
    return pl.pallas_call(
        table_grad_kernel,
        out_shape=jax.ShapeDtypeStruct((height, flat), F32),
        in_specs=[pl.BlockSpec(memory_space=pltpu.SMEM)] * 2
        + [pl.BlockSpec(memory_space=pl.ANY)],
        scratch_shapes=[
            pltpu.VMEM(score_grads.shape, BF16),
            pltpu.VMEM((heads, 256, length), BF16),
            pltpu.VMEM((WIDE // 128, CODE * height, 128), F32),
            pltpu.SemaphoreType.DMA((micro_count,)),
        ],
        compiler_params=pltpu.CompilerParams(vmem_limit_bytes=VMEM_BYTES),
        cost_estimate=BRIEF,
        name="table_grad",
    )(grid_rows, grid_cols, score_grads)


SIDES = ("h", "o", "h2", "z", "act")
HELD = ("p", "wt", "br", "m", "dg", "fd")
GRADS = ("df", "du", "db", "ds", "dp", "dx", "sums")
WEIGHTS = ("qkv", "proj", "up", "down")
VECTORS = (
    "n1_gain",
    "n1_shift",
    "query_bias",
    "value_bias",
    "proj_shift",
    "attn_gain",
    "n2_gain",
    "n2_shift",
    "up_shift",
    "down_shift",
    "mlp_gain",
)
SUM_ROWS = 16
FORWARD, BACKWARD, BOTH = "forward", "backward", "both"


def layer_shapes(micro_count, length, width, hidden, heads):
    row = (micro_count, length, width)
    return {
        "h": (row, BF16),
        "p": ((micro_count, length, 3 * width), BF16),
        "wt": ((micro_count, heads, length, length), BF16),
        "o": (row, BF16),
        "br": (row, BF16),
        "m": (row, F32),
        "h2": (row, BF16),
        "dg": ((micro_count, length, hidden), BF16),
        "z": ((micro_count, length, hidden), BF16),
        "fd": (row, BF16),
        "act": (row, BF16),
        "df": (row, BF16),
        "du": ((micro_count, length, hidden), BF16),
        "db": (row, BF16),
        "ds": ((micro_count, heads, length, length), BF16),
        "dp": ((micro_count, length, 3 * width), BF16),
        "dx": (row, F32),
        "sums": ((SUM_ROWS, width), F32),
    }


def named(vec):
    return types.SimpleNamespace(**{name: vec[name] for name in VECTORS if name in vec})


def forward_body(mb, rows_ref, cols_ref, vec, wide_scr, x_scr, w, scr, tools, wait, keep):
    bias_scr, ladder_scr, score_scr = tools
    vec = named(vec)
    length, width = x_scr.shape
    heads = scr["wt"].shape[0]
    hidden = scr["z"].shape[1]
    head_dim = width // heads
    pair = 2 * head_dim
    owner_col, code_col, _ = pack_places(rows_ref, cols_ref, mb, (length, 1), 0)
    owner_row, code_row, _ = pack_places(rows_ref, cols_ref, mb, (1, length), 1)
    lanes = ramp((length, 256), 1)
    place_col = jnp.where(
        (lanes == code_col) | (lanes == owner_col + PLACES), 1.0, 0.0
    ).astype(BF16)
    place_col = jnp.concatenate([place_col, place_col], axis=1)
    reach = CODE * (GRID - 1)
    ladder_scr[...] = onehot(code_row + reach, ladder_scr.shape, 0)
    spare = ramp((256 - PLACES, length), 0)
    walls = jnp.where(spare == owner_row, 0.0, NEG).astype(BF16)
    blank = jnp.zeros((256 - PLACES, length), BF16)
    for h in range(heads):
        bias_scr[h, PLACES:256, :] = walls
        bias_scr[h, 256 + PLACES :, :] = blank
    wait("wide")
    for r in range(GRID):
        begin = CODE * (GRID - 1 - r)
        low = begin // 128 * 128
        high = -(-(begin + PLACES) // 128) * 128
        rung = ladder_scr[CODE * r + low : CODE * r + high, :]
        for part in range(2):
            block = mm(
                wide_scr[part, :, :, low:high].reshape(heads * CODE, high - low), rung
            ).astype(BF16)
            at = 256 * part + CODE * r
            for h in range(heads):
                bias_scr[h, at : at + CODE, :] = block[h * CODE : (h + 1) * CODE]

    wait("x")
    hat, _ = unit_rows(x_scr[...].astype(F32))
    scr["h"][...] = (hat * vec.n1_gain[...] + vec.n1_shift[...]).astype(BF16)
    keep("h")

    scale = head_dim ** (-0.5)
    h_all = scr["h"][...]
    p_scr = scr["p"]
    wait("qkv")
    p_scr[:, :width] = (
        (mm(h_all, w["qkv"][:, :width]) + vec.query_bias[...]).astype(BF16) * scale
    ).astype(BF16)
    p_scr[:, width : 2 * width] = mm(h_all, w["qkv"][:, width : 2 * width]).astype(BF16)
    p_scr[:, 2 * width :] = (
        mm(h_all, w["qkv"][:, 2 * width :]) + vec.value_bias[...]
    ).astype(BF16)
    keep("p")

    first = ramp((length, pair), 1) < head_dim
    zero = jnp.zeros((length, pair), BF16)
    for head in range(heads):
        at = head // 2 * pair
        queries = p_scr[:, at : at + pair]
        keys_all = p_scr[:, width + at : width + at + pair]
        own = jnp.where(first == (head % 2 == 0), queries, zero)
        score_scr[head] = mm(own, keys_all, NT) + mm(place_col, bias_scr[head])
    for head in range(heads):
        for at in range(0, length, 64):
            scores = score_scr[head, at : at + 64]
            raised = jnp.exp(scores - jnp.max(scores, axis=-1, keepdims=True))
            share = 1.0 / jnp.sum(raised, axis=-1, keepdims=True)
            scr["wt"][head, at : at + 64] = (raised * share).astype(BF16)
    keep("wt")
    for head in range(0, heads, 2):
        at = head // 2 * pair
        values_all = p_scr[:, 2 * width + at : 2 * width + at + pair]
        mixed = [mm(scr["wt"][head + side], values_all) for side in range(2)]
        scr["o"][:, at : at + pair] = jnp.where(first, mixed[0], mixed[1]).astype(BF16)
    keep("o")

    wait("proj")
    branch = mm(scr["o"][...], w["proj"][...]) + vec.proj_shift[...]
    scr["br"][...] = branch.astype(BF16)
    keep("br")
    middle = x_scr[...].astype(F32) + vec.attn_gain[...] * branch
    scr["m"][...] = middle
    keep("m")
    hat, _ = unit_rows(middle)
    scr["h2"][...] = (hat * vec.n2_gain[...] + vec.n2_shift[...]).astype(BF16)
    keep("h2")

    wait("up")
    wait("down")
    second = scr["h2"][...]
    tile = width
    down = None
    for at in range(0, hidden, tile):
        upward = mm(second, w["up"][:, at : at + tile]) + vec.up_shift[:, at : at + tile]
        cdf, leaning = normal_parts(upward)
        z = (upward * cdf).astype(BF16)
        scr["z"][:, at : at + tile] = z
        scr["dg"][:, at : at + tile] = (cdf + leaning).astype(BF16)
        for name in ("z", "dg"):
            keep(name, slice(None), pl.ds(at, tile))
        term = mm(z, w["down"][at : at + tile, :])
        down = term if down is None else down + term
    downward = down + vec.down_shift[...]
    scr["act"][...] = (scr["m"][...] + vec.mlp_gain[...] * downward).astype(BF16)
    keep("send")
    keep("act")
    scr["fd"][...] = downward.astype(BF16)
    keep("fd")


def backward_body(adds, kept, vec, g_scr, x_scr, w, got, scr, tools, wait, keep):
    do_scr, dwt_scr, send_scr = tools
    vec = named(vec)
    length, width = x_scr.shape
    heads = got["wt"].shape[0]
    hidden = got["dg"].shape[1]
    head_dim = width // heads
    pair = 2 * head_dim

    def total(values):
        return jnp.sum(values, axis=0, keepdims=True)

    sums = scr["sums"]

    def note(row, values):
        if adds:
            values = values + sums[row : row + 1, :]
        sums[row : row + 1, :] = values

    wait("sums")
    wait("g")
    grad_out = g_scr[...].astype(F32) * kept
    wait("fd")
    note(9, total(grad_out * got["fd"][...].astype(F32)))
    df = (grad_out * vec.mlp_gain[...]).astype(BF16)
    scr["df"][...] = df
    keep("df")
    note(8, total(df.astype(F32)))

    tile = width
    dh2 = None
    for at in range(0, hidden, tile):
        wait("down%d" % at)
        wait("dg%d" % at)
        wait("up%d" % at)
        dz = mm(scr["df"][...], w["down"][at : at + tile, :], NT)
        du = (dz * got["dg"][:, at : at + tile].astype(F32)).astype(BF16)
        scr["du"][:, at : at + tile] = du
        keep("du", slice(None), pl.ds(at, tile))
        note(10 + at // tile, total(du.astype(F32)))
        term = mm(du, w["up"][:, at : at + tile], NT)
        dh2 = term if dh2 is None else dh2 + term
    for row in range(10 + hidden // tile, SUM_ROWS):
        sums[row : row + 1, :] = jnp.zeros((1, width), F32)

    wait("m")
    hat, inverse = unit_rows(got["m"][...])
    note(6, total(dh2 * hat))
    note(7, total(dh2))
    dm = g_scr[...].astype(F32) * kept + norm_back(dh2 * vec.n2_gain[...], hat, inverse)
    scr["dx"][...] = dm
    wait("br")
    note(5, total(dm * got["br"][...].astype(F32)))
    db = (dm * vec.attn_gain[...]).astype(BF16)
    scr["db"][...] = db
    keep("db")
    note(4, total(db.astype(F32)))

    wait("proj")
    do_scr[...] = mm(scr["db"][...], w["proj"][...], NT).astype(BF16)
    wait("p")
    wait("wt")
    first = ramp((length, pair), 1) < head_dim
    zero = jnp.zeros((length, pair), BF16)
    scale = head_dim ** (-0.5)
    p_scr, dp_scr = got["p"], scr["dp"]
    for head in range(heads):
        at = head // 2 * pair
        own = jnp.where(first == (head % 2 == 0), do_scr[:, at : at + pair], zero)
        dwt_scr[head] = mm(own, p_scr[:, 2 * width + at : 2 * width + at + pair], NT)
    for head in range(heads):
        for at in range(0, length, 64):
            dwt = dwt_scr[head, at : at + 64]
            probs = got["wt"][head, at : at + 64].astype(F32)
            inner = jnp.sum(probs * dwt, axis=-1, keepdims=True)
            scr["ds"][head, at : at + 64] = (probs * (dwt - inner)).astype(BF16)
    keep("ds")
    for head in range(0, heads, 2):
        at = head // 2 * pair
        queries = p_scr[:, at : at + pair]
        keys_all = p_scr[:, width + at : width + at + pair]
        dout = do_scr[:, at : at + pair]
        both = []
        for here in (head, head + 1):
            ds = scr["ds"][here]
            both.append(
                (
                    mm(ds, keys_all) * scale,
                    mm(ds, queries, TN),
                    mm(got["wt"][here], dout, TN),
                )
            )
        for part, (even, odd) in enumerate(zip(*both)):
            dp_scr[:, part * width + at : part * width + at + pair] = jnp.where(
                first, even, odd
            ).astype(BF16)
    keep("dp")

    wait("qkv")
    dh = mm(dp_scr[...], w["qkv"][...], NT)
    wait("x")
    hat, inverse = unit_rows(x_scr[...].astype(F32))
    dx = scr["dx"][...] + norm_back(dh * vec.n1_gain[...], hat, inverse)
    send_scr[...] = dx.astype(BF16)
    keep("send")
    scr["dx"][...] = dx
    keep("dx")
    note(0, total(dh * hat))
    note(1, total(dh))
    note(2, total(dp_scr[:, :width].astype(F32)))
    note(3, total(dp_scr[:, 2 * width :].astype(F32)))
    keep("sums")


def layer_kernel(section, mb, kind, adds, layout, *refs):
    groups = [dict() for _ in layout]
    for group, names in zip(groups, layout):
        group.update(zip(names, refs))
        refs = refs[len(names) :]
    given, outs, own = groups
    sec_ref, rows_ref, cols_ref = [given[name] for name in ("sec", "rows", "cols")]
    length, width = own["x"].shape

    @pl.when(sec_ref[0] == section)
    def _():
        loads, stores = {}, []

        def wait(name):
            if name in loads:
                loads.pop(name).wait()

        def keep(name, *piece):
            if name not in outs:
                return
            dst = outs[name]
            if name == "send":
                src = own["send"] if kind != FORWARD else own["act"]
            else:
                src = own[name]
                dst = dst if name == "sums" else dst.at[mb]
            if piece:
                src, dst = src.at[piece], dst.at[piece]
            store = pltpu.make_async_copy(src, dst, own["out_sem"].at[len(stores)])
            store.start()
            stores.append(store)

        order = []
        x_src = given["x"] if section else given["x"].at[mb]
        hidden = own["dg"].shape[1]
        if kind != BACKWARD:
            order += [("wide", given["wide"], own["wide"]), ("x", x_src, own["x"])]
            order += [(name, given[name].at[0], own[name]) for name in WEIGHTS]
        if kind != FORWARD:
            if adds:
                order.append(("sums", outs["sums"], own["sums"]))
            order.append(("g", given["g"].at[mb] if section else given["g"], own["g"]))
        if kind == BACKWARD:
            order.append(("fd", given["fd"].at[mb], own["fd"]))
            for at in range(0, hidden, width):
                strip, piece = pl.ds(at, width), (slice(None), pl.ds(at, width))
                order += [
                    ("down%d" % at, given["down"].at[0].at[strip], own["down"].at[strip]),
                    ("dg%d" % at, given["dg"].at[mb].at[piece], own["dg"].at[piece]),
                    ("up%d" % at, given["up"].at[0].at[piece], own["up"].at[piece]),
                ]
            order += [
                ("m", given["m"].at[mb], own["m"]),
                ("br", given["br"].at[mb], own["br"]),
                ("proj", given["proj"].at[0], own["proj"]),
                ("p", given["p"].at[mb], own["p"]),
                ("wt", given["wt"].at[mb], own["wt"]),
                ("qkv", given["qkv"].at[0], own["qkv"]),
                ("x", x_src, own["x"]),
            ]
        for place, (name, src, dst) in enumerate(order):
            loads[name] = pltpu.make_async_copy(src, dst, own["in_sem"].at[place])
            loads[name].start()
        if kind != BACKWARD:
            tools = (own["bias"], own["ladder"], own["score"])
            forward_body(
                mb, rows_ref, cols_ref, given, own["wide"], own["x"], own, own, tools, wait, keep
            )
        if kind != FORWARD:
            kept = 1.0
            if section:
                _, _, inside = pack_places(rows_ref, cols_ref, mb, (length, 1), 0)
                kept = jnp.where(inside, 1.0, 0.0)
            tools = (own["do"], own["score"], own["send"])
            backward_body(
                adds, kept, given, own["g"], own["x"], own, own, own, tools, wait, keep
            )
        for store in stores:
            store.wait()


def run_layer(section, mb, kind, adds, inputs, vectors, weights, prior):
    smem = pl.BlockSpec(memory_space=pltpu.SMEM)
    vmem = pl.BlockSpec(memory_space=pltpu.VMEM)
    hbm = pl.BlockSpec(memory_space=pl.ANY)
    length, width = inputs["x"].shape[-2:]
    micro_count = inputs["rows"].shape[0]
    hidden = weights["up"].shape[2]
    heads = inputs["heads"]
    inputs = {name: array for name, array in inputs.items() if name != "heads"}
    shapes = layer_shapes(micro_count, length, width, hidden, heads)
    results = []
    if kind != BACKWARD:
        results += SIDES
    if kind == FORWARD:
        results += HELD
    if kind != FORWARD:
        results += GRADS
    out_shape = [jax.ShapeDtypeStruct(*shapes[name]) for name in results]
    sends = kind == FORWARD or section == 1
    if sends:
        results.append("send")
        out_shape.append(jax.ShapeDtypeStruct((length, width), BF16))
    operands = {**inputs, **vectors, **weights}
    specs = []
    for name in operands:
        specs.append(smem if name in ("sec", "rows", "cols") else vmem if name in VECTORS else hbm)
    held = [name for name in results if name in prior]
    operands_all = {**operands, **{"prior " + name: prior[name] for name in held}}
    block = lambda name: pltpu.VMEM(shapes[name][0][1:], shapes[name][1])
    scratch = {"x": pltpu.VMEM((length, width), BF16)}
    for name in WEIGHTS:
        scratch[name] = pltpu.VMEM(weights[name].shape[1:], BF16)
    for name in HELD:
        scratch[name] = block(name)
    scratch["score"] = pltpu.VMEM((heads, length, length), F32)
    if kind != BACKWARD:
        for name in SIDES:
            scratch[name] = block(name)
        scratch["wide"] = pltpu.VMEM(inputs["wide"].shape, BF16)
        scratch["bias"] = pltpu.VMEM((heads, 512, length), BF16)
        scratch["ladder"] = pltpu.VMEM((CODE * (GRID - 1) + WIDE, length), BF16)
    if kind != FORWARD:
        for name in GRADS[:-1]:
            scratch[name] = block(name)
        scratch["sums"] = pltpu.VMEM((SUM_ROWS, width), F32)
        for name in ("g", "do", "send"):
            scratch[name] = pltpu.VMEM((length, width), BF16)
    scratch["in_sem"] = pltpu.SemaphoreType.DMA((10 + 3 * (hidden // width),))
    scratch["out_sem"] = pltpu.SemaphoreType.DMA((len(results) + 2 * (hidden // width),))
    layout = (list(operands_all), results, list(scratch))
    made = pl.pallas_call(
        functools.partial(layer_kernel, section, mb, kind, adds, layout),
        out_shape=out_shape,
        in_specs=specs + [hbm] * len(held),
        out_specs=[hbm] * len(results),
        scratch_shapes=list(scratch.values()),
        input_output_aliases={
            len(operands) + at: results.index(name) for at, name in enumerate(held)
        },
        compiler_params=pltpu.CompilerParams(vmem_limit_bytes=VMEM_BYTES),
        cost_estimate=BRIEF,
        name="layer_" + kind,
    )(*operands_all.values())
    return dict(zip(results, made))


def turn_kernel(chunk_count, *refs):
    count = len(refs) // 4
    sources, outs, refs = refs[:count], refs[count : 2 * count], refs[2 * count :]
    lefts, turned, refs = refs[:count], refs[count : 2 * count], refs[2 * count :]
    in_sem, out_sem = refs
    loads = [
        pltpu.make_async_copy(src, dst, in_sem.at[at])
        for at, (src, dst) in enumerate(zip(sources, lefts))
    ]
    stores = [
        pltpu.make_async_copy(src, dst, out_sem.at[at])
        for at, (src, dst) in enumerate(zip(turned, outs))
    ]
    for load in loads:
        load.start()
    for left, out, load, store in zip(lefts, turned, loads, stores):
        load.wait()
        micro_count, length, width = left.shape
        step = width // chunk_count
        strip = 256 if width % 256 == 0 else width
        for mb in range(micro_count):
            flipped = jnp.concatenate(
                [left[mb, :, at : at + strip].T for at in range(0, width, strip)], axis=0
            )
            for chunk in range(chunk_count):
                core_of, to = chunk % 2, chunk // 2 * step
                out[core_of, to : to + step, mb * length : (mb + 1) * length] = flipped[
                    chunk * step : (chunk + 1) * step, :
                ]
        store.start()
    for store in stores:
        store.wait()


def turn_lefts(chunk_count, lefts):
    hbm = pl.BlockSpec(memory_space=pl.ANY)
    shapes = [(2, left.shape[2] // 2, left.shape[0] * left.shape[1]) for left in lefts]
    return pl.pallas_call(
        functools.partial(turn_kernel, chunk_count),
        out_shape=[jax.ShapeDtypeStruct(shape, BF16) for shape in shapes],
        in_specs=[hbm] * len(lefts),
        out_specs=[hbm] * len(lefts),
        scratch_shapes=[pltpu.VMEM(left.shape, BF16) for left in lefts]
        + [pltpu.VMEM(shape, BF16) for shape in shapes]
        + [pltpu.SemaphoreType.DMA((len(lefts),))] * 2,
        compiler_params=pltpu.CompilerParams(vmem_limit_bytes=VMEM_BYTES),
        cost_estimate=BRIEF,
        name="turn_lefts",
    )(*lefts)


def placed(chunk, order):
    place = 0
    for bit in order:
        place = 2 * place + (chunk >> (bit - 1) & 1)
    return place


def weight_kernel(parts, fresh, orders, sides, sec_ref, *refs):
    operands, refs = refs[: 2 * parts], refs[2 * parts :]
    if fresh:
        (grad_hbm, gain_ref), refs = refs[:2], refs[2:]
    count = len(sides)
    outs, refs = refs[:count], refs[count:]
    lefts, rights, refs = refs[:parts], refs[parts : 2 * parts], refs[2 * parts :]
    scrs, (in_sem, out_sem), refs = refs[:count], refs[count : count + 2], refs[count + 2 :]
    halves = [sec_ref[1] if side else 1 - sec_ref[1] for side in sides]
    strip = 384
    loads = []
    for part in range(parts):
        pairs = [(operands[2 * part + 1], rights[part])]
        for which, half in enumerate(halves):
            for low in range(0, lefts[part].shape[1], strip):
                rows = pl.ds(low, strip)
                pairs.append(
                    (operands[2 * part].at[half].at[rows], lefts[part].at[which].at[rows])
                )
        loads.append([])
        for kind, (src, dst) in enumerate(pairs):
            load = pltpu.make_async_copy(src, dst, in_sem.at[part, kind])
            load.start()
            loads[part].append(load)
    if fresh:
        grad_scr = refs[0]
        grad_copy = pltpu.make_async_copy(grad_hbm, grad_scr, in_sem.at[parts, 0])
        grad_copy.start()
        grad_copy.wait()
        loads[0][0].wait()

        @pl.when(sec_ref[0] == 0)
        def _():
            rights[0][rights[0].shape[0] - 1] = (grad_scr[...].astype(F32) * gain_ref[...]).astype(BF16)

    stores = []
    unit = scrs[0].shape[2]
    tile = min(768, unit)
    for which in range(count):
        at_col = 0
        for part in range(parts):
            if which == 0 and not fresh:
                loads[part][0].wait()
            micro_count, length, cols = rights[part].shape
            height = lefts[part].shape[1]
            pieces = height // strip
            for at in range(0, cols, tile):
                right = rights[part][:, :, at : at + tile].reshape(micro_count * length, tile)
                cut, place = divmod(at_col + at, unit)
                step = height >> len(orders[cut])
                for low in range(0, height, strip):
                    if at == 0:
                        loads[part][1 + which * pieces + low // strip].wait()
                    block = mm(lefts[part][which, low : low + strip], right).astype(BF16)
                    for top in range(0, strip, step):
                        to = step * placed((low + top) // step, orders[cut])
                        scrs[which][cut, to : to + step, place : place + tile] = block[
                            top : top + step
                        ]
                piece = (slice(None), pl.ds(place, tile))
                store = pltpu.make_async_copy(
                    scrs[which].at[cut].at[piece],
                    outs[which].at[cut].at[piece],
                    out_sem.at[len(stores)],
                )
                store.start()
                stores.append(store)
            at_col += cols
    for store in stores:
        store.wait()


def weight_terms(orders, sides, sec, pairs, fresh=()):
    hbm = pl.BlockSpec(memory_space=pl.ANY)
    vmem = pl.BlockSpec(memory_space=pltpu.VMEM)
    smem = pl.BlockSpec(memory_space=pltpu.SMEM)
    height = pairs[0][0].shape[1]
    cuts = len(orders)
    unit = sum(right.shape[2] for _, right in pairs) // cuts
    tiles = -(-unit // min(768, unit)) * cuts * len(sides)
    operands = [side for pair in pairs for side in pair]
    scratch = [pltpu.VMEM((len(sides), *left.shape[1:]), BF16) for left, _ in pairs]
    scratch += [pltpu.VMEM(right.shape, BF16) for _, right in pairs]
    scratch += [pltpu.VMEM((cuts, height, unit), BF16) for _ in sides]
    scratch += [
        pltpu.SemaphoreType.DMA((len(pairs) + 1, 1 + 2 * (height // 384))),
        pltpu.SemaphoreType.DMA((tiles,)),
    ]
    if fresh:
        scratch.append(pltpu.VMEM(fresh[0].shape, BF16))
    return pl.pallas_call(
        functools.partial(weight_kernel, len(pairs), bool(fresh), orders, sides),
        out_shape=[jax.ShapeDtypeStruct((cuts, height, unit), BF16) for _ in sides],
        in_specs=[smem] + [hbm] * len(operands) + ([hbm, vmem] if fresh else []),
        out_specs=[hbm] * len(sides),
        scratch_shapes=scratch,
        compiler_params=pltpu.CompilerParams(vmem_limit_bytes=VMEM_BYTES),
        cost_estimate=BRIEF,
        name="weight_terms",
    )(sec, *operands, *fresh)


def swap(block, bit):
    devices = range(lax.axis_size("dp"))
    return lax.ppermute(block, "dp", [(i, i ^ bit) for i in devices])


def after(value, *others):
    return lax.optimization_barrier((value, *others))[0]


def half_of(block, side):
    block = block.reshape(2, block.shape[0] // 2, block.shape[1])
    return lax.dynamic_index_in_dim(block, side, 0, keepdims=False)


def total_of(blocks):
    return functools.reduce(jnp.add, [block.astype(F32) for block in blocks])


def next_sum(mine, come, order, rank):
    side = (rank >> order[0]) & 1
    sent = total_of([half_of(mine, 1 - side), half_of(come, 1 - side)]).astype(BF16)
    kept = total_of([half_of(mine, side), half_of(come, side)]).astype(BF16)
    come = swap(sent, 1 << order[0])
    return lax.optimization_barrier(kept), come, order[1:], sent


def full_sum(values):
    size = lax.axis_size("dp")
    if size & (size - 1):
        return lax.psum(values, "dp")
    bit = 1
    while bit < size:
        values = values + swap(values, bit)
        bit *= 2
    return values


def shards(
    patches_in,
    grid_rows,
    grid_cols,
    norm1_gain,
    norm1_bias,
    qkv_weight,
    q_bias,
    v_bias,
    rel_table,
    proj_weight,
    proj_bias,
    attn_scale,
    norm2_gain,
    norm2_bias,
    fc1_weight,
    fc1_bias,
    fc2_weight,
    fc2_bias,
    mlp_scale,
    cotangent,
):
    rank = lax.axis_index("dp")
    dp_size = lax.axis_size("dp")
    micro_count, length, width = patches_in.shape
    hidden = fc1_bias.shape[1]
    rel, heads = rel_table.shape[1:]
    sec = jnp.stack([lax.axis_index("section"), rank % 2]).astype(jnp.int32)
    weights = dict(zip(WEIGHTS, (qkv_weight, proj_weight, fc1_weight, fc2_weight)))
    vectors = dict(
        zip(
            VECTORS,
            (
                norm1_gain,
                norm1_bias,
                q_bias,
                v_bias,
                proj_bias,
                attn_scale,
                norm2_gain,
                norm2_bias,
                fc1_bias,
                fc2_bias,
                mlp_scale,
            ),
        )
    )
    common = {"sec": sec, "rows": grid_rows, "cols": grid_cols, "heads": heads}
    wide = table_spread(rel_table)

    cache, grads = {}, {}
    moved, returned = [], []
    for mb in range(micro_count):
        inputs = {**common, "x": patches_in, "wide": wide}
        cache = run_layer(0, mb, FORWARD, False, inputs, vectors, weights, cache)
        moved.append(lax.ppermute(cache.pop("send"), "section", [(0, 1)]))
    for mb in range(micro_count):
        inputs = {**common, "x": moved[mb], "wide": wide, "g": cotangent}
        made = run_layer(1, mb, BOTH, mb > 0, inputs, vectors, weights, {**cache, **grads})
        returned.append(lax.ppermute(made.pop("send"), "section", [(1, 0)]))
        cache.update({name: made[name] for name in SIDES})
        grads = {name: made[name] for name in GRADS}

    def backward(mb, grad, prior):
        inputs = {**common, "x": patches_in, "g": grad}
        inputs.update({name: cache[name] for name in HELD})
        return run_layer(0, mb, BACKWARD, mb > 0, inputs, vectors, weights, prior)

    spread_out = dp_size == 16 and width % (16 * dp_size) == 0
    if spread_out:
        lefts = [after(cache[name], grads["dx"]) for name in ("z", "h2", "o", "h")]
        z_turned, h2_turned, o_turned, h_turned = turn_lefts(dp_size, lefts)
    for mb in range(micro_count - 1):
        grads = backward(mb, returned[mb], grads)
    last = returned[-1]
    if spread_out:
        one, two = (1, 2, 3), (2, 1, 3)

        def paired(send, keep, orders):
            got = swap(send, 1)
            return [(keep[cut], got[cut], order, None) for cut, order in enumerate(orders)]

        def follow(units, *before):
            done = []
            for mine, come, order, _ in units:
                done.append(next_sum(mine, after(come, *before), order, rank))
            return done

        def moving(units):
            return [sent for _, _, _, sent in units]

        def ended(units, *before):
            return jnp.concatenate(
                [total_of([mine, after(come, *before)]) for mine, come, _, _ in units], axis=1
            )

        down_orders, attn_orders, up_orders = ((one, two), (one, two), (one, two))
        operands = ([(z_turned, grads["df"])], (last, mlp_scale))
        (send,) = weight_terms(down_orders, (0,), sec, *operands)
        (keep,) = weight_terms(down_orders, (1,), after(sec, send), *operands)
        down = follow(paired(send, keep, down_orders))
        grads = backward(micro_count - 1, after(last, *moving(down)), grads)
        down = follow(down, grads["sums"])
        send, keep = weight_terms(
            attn_orders,
            (0, 1),
            sec,
            [(after(o_turned, *moving(down)), grads["db"]), (h_turned, grads["dp"])],
        )
        attn = paired(send, keep, attn_orders)
        send, keep = weight_terms(
            up_orders, (0, 1), sec, [(after(h2_turned, send), grads["du"])]
        )
        up = paired(send, keep, up_orders)
        attn = follow(attn, send)
        down = follow(down, *moving(attn))
        up = follow(up, *moving(down))
        rev = table_grad(grid_rows, grid_cols, after(grads["ds"], *moving(up)), rel)
        small = jnp.concatenate([grads["sums"], rev], axis=0)
        small = small + swap(small, 1)
        attn = follow(attn, small)
        small = small + swap(after(small, *moving(attn)), 2)
        down_grad = ended(down, small)
        up = follow(up, down_grad)
        small = small + swap(after(small, *moving(up)), 4)
        attn = follow(attn, small)
        small = small + swap(after(small, *moving(attn)), 8)
        up = follow(up, small)
        attn_grad = ended(attn, *moving(up))
        up_grad = ended(up, attn_grad)
        proj_grad, qkv_grad = attn_grad[:, :width], attn_grad[:, width:]
        sums, rev = small[:SUM_ROWS], small[SUM_ROWS:]
    else:
        grads = backward(micro_count - 1, last, grads)

        def plain(left, right):
            term = jnp.einsum("mrk,mrn->kn", left, right, preferred_element_type=F32)
            return lax.psum_scatter(term, "dp", scatter_dimension=0, tiled=True)

        down_grad = plain(cache["z"], grads["df"])
        up_grad = plain(cache["h2"], grads["du"])
        proj_grad = plain(cache["o"], grads["db"])
        qkv_grad = plain(cache["h"], grads["dp"])
        rev = full_sum(table_grad(grid_rows, grid_cols, grads["ds"], rel))
        sums = full_sum(grads["sums"])
    rel_grad = jnp.flip(rev[:heads, :rel].T, 0)
    up_shift_grad = sums[10 : 10 + hidden // width].reshape(1, hidden)
    small = [sums[row : row + 1] for row in range(10)]
    return (
        cache["act"][None],
        grads["dx"][None],
        small[0],
        small[1],
        qkv_grad[None],
        small[2],
        small[3],
        rel_grad[None],
        proj_grad[None],
        small[4],
        small[5],
        small[6],
        small[7],
        up_grad[None],
        up_shift_grad,
        down_grad[None],
        small[8],
        small[9],
    )


def solution(mesh):
    layer_row = P("section", None)
    layer_matrix = P("section", None, None)
    packs = P(None, "dp", None)
    scattered = P("section", "dp", None)
    in_specs = (
        packs,
        packs,
        packs,
        layer_row,
        layer_row,
        layer_matrix,
        layer_row,
        layer_row,
        layer_matrix,
        layer_matrix,
        layer_row,
        layer_row,
        layer_row,
        layer_row,
        layer_matrix,
        layer_row,
        layer_matrix,
        layer_row,
        layer_row,
        packs,
    )
    out_specs = (
        P("section", None, "dp", None),
        P("section", None, "dp", None),
        layer_row,
        layer_row,
        scattered,
        layer_row,
        layer_row,
        layer_matrix,
        scattered,
        layer_row,
        layer_row,
        layer_row,
        layer_row,
        scattered,
        layer_row,
        scattered,
        layer_row,
        layer_row,
    )
    return jax.shard_map(
        shards, mesh=mesh, in_specs=in_specs, out_specs=out_specs, check_vma=False
    )
```

```python
import functools
import types

import jax
import jax.numpy as jnp
from jax import lax
from jax.experimental import pallas as pl
from jax.experimental.pallas import tpu as pltpu
from jax.sharding import PartitionSpec as P

SLOTS = 4
GRID = 14
SPAN = 2 * GRID - 1
CODE = 16
PLACES = GRID * CODE
WIDE = 512
EPS = 1e-06
NEG = -1000000000.0
F32 = jnp.float32
BF16 = jnp.bfloat16
VMEM_BYTES = 56 * 1024 * 1024
BRIEF = pl.CostEstimate(flops=1, bytes_accessed=1, transcendentals=0)

NN = (((1,), (0,)), ((), ()))
NT = (((1,), (1,)), ((), ()))
TN = (((0,), (0,)), ((), ()))


def mm(left, right, dims=NN):
    return lax.dot_general(left, right, dims, preferred_element_type=F32)


def ramp(shape, axis):
    return lax.broadcasted_iota(jnp.int32, shape, axis)


def pack_places(rows_ref, cols_ref, mb, shape, axis):
    places = ramp(shape, axis)
    owner = jnp.zeros(shape, jnp.int32)
    start = jnp.zeros(shape, jnp.int32)
    breadth = jnp.ones(shape, jnp.int32)
    end = jnp.int32(0)
    for slot in range(SLOTS):
        cols = cols_ref[mb, 0, slot]
        here = places >= end
        start = jnp.where(here, end, start)
        breadth = jnp.where(here, cols, breadth)
        end = end + rows_ref[mb, 0, slot] * cols
        owner = owner + (places >= end).astype(jnp.int32)
    inside = places < end
    offset = (places - start).astype(F32)
    row = jnp.floor((offset + 0.5) / breadth.astype(F32)).astype(jnp.int32)
    col = places - start - row * breadth
    code = jnp.where(inside, row * CODE + col, 0)
    return owner, code, inside


def onehot(ids, shape, axis):
    return jnp.where(ids == ramp(shape, axis), 1.0, 0.0).astype(BF16)


def unit_rows(values):
    center = values - jnp.mean(values, axis=-1, keepdims=True)
    inverse = lax.rsqrt(jnp.mean(center * center, axis=-1, keepdims=True) + EPS)
    return center * inverse, inverse


def norm_back(grad_hat, hat, inverse):
    centered = grad_hat - jnp.mean(grad_hat, axis=-1, keepdims=True)
    return inverse * (centered - hat * jnp.mean(grad_hat * hat, axis=-1, keepdims=True))


def normal_parts(u):
    t = 1.0 / (1.0 + (0.3275911 * 0.7071067811865476) * jnp.abs(u))
    falling = jnp.exp(-0.5 * u * u)
    poly = t * (
        0.254829592
        + t * (-0.284496736 + t * (1.421413741 + t * (-1.453152027 + t * 1.061405429)))
    )
    tail = 0.5 * poly * falling
    return jnp.where(u < 0.0, tail, 1.0 - tail), u * falling * 0.3989422804014327


def spread_map(shape, flat_axis, wide_axis):
    flat = ramp(shape, flat_axis)
    wide = ramp(shape, wide_axis)
    row = wide // CODE
    col = wide - row * CODE
    meets = (flat == row * SPAN + col) & (col < GRID) & (row < SPAN)
    return jnp.where(meets, 1.0, 0.0).astype(BF16)


def split_two(values):
    high = values.astype(BF16)
    return high, (values - high.astype(F32)).astype(BF16)


def table_kernel(table_ref, out_ref, wide_ref):
    heads, _, rel = table_ref.shape
    height = wide_ref.shape[1] // CODE
    flat = -(-rel // 128) * 128
    table = table_ref[:, 0, :]
    mirror = jnp.where(
        ramp((rel, flat), 0) + ramp((rel, flat), 1) == rel - 1, 1.0, 0.0
    ).astype(BF16)
    spread = spread_map((flat, WIDE), 0, 1)
    for part, piece in enumerate(split_two(table)):
        rev = mm(piece, mirror)
        if height > heads:
            rev = jnp.concatenate([rev, jnp.zeros((height - heads, flat), F32)], axis=0)
        turned = jnp.concatenate(
            [pltpu.roll(rev, (c - (GRID - 1)) % flat, 1) for c in range(CODE)], axis=0
        )
        wide = mm(turned.astype(BF16), spread)
        for at in range(WIDE // 128):
            wide_ref[at] = wide[:, at * 128 : (at + 1) * 128]
        for h in range(heads):
            for at in range(WIDE // 128):
                out_ref[part, h, :, at * 128 : (at + 1) * 128] = wide_ref[
                    at, pl.ds(h, CODE, stride=height), :
                ].astype(BF16)


def table_spread(rel_table):
    _, rel, heads = rel_table.shape
    height = -(-heads // 8) * 8
    return pl.pallas_call(
        table_kernel,
        out_shape=jax.ShapeDtypeStruct((2, heads, CODE, WIDE), BF16),
        scratch_shapes=[pltpu.VMEM((WIDE // 128, CODE * height, 128), F32)],
        compiler_params=pltpu.CompilerParams(vmem_limit_bytes=VMEM_BYTES),
        cost_estimate=BRIEF,
        name="table_spread",
    )(jnp.transpose(rel_table, (2, 0, 1)))


def table_grad_kernel(rows_ref, cols_ref, ds_hbm, out_ref, ds_scr, dw_scr, wide_ref, sem):
    micro_count, heads, length, _ = ds_hbm.shape
    height, flat = out_ref.shape
    loads = [
        pltpu.make_async_copy(ds_hbm.at[mb], ds_scr.at[mb], sem.at[mb])
        for mb in range(micro_count)
    ]
    for load in loads:
        load.start()
    spread = spread_map((WIDE, flat), 1, 0)
    wide_ref[...] = jnp.zeros_like(wide_ref)
    total = jnp.zeros((heads * CODE, WIDE), F32)
    for mb in range(micro_count):
        _, code_row, _ = pack_places(rows_ref, cols_ref, mb, (1, length), 1)
        place_row = onehot(code_row, (256, length), 0)
        reach = CODE * (GRID - 1)
        ladder = onehot(code_row + reach, (reach + WIDE, length), 0)
        loads[mb].wait()
        for h in range(heads):
            dw_scr[h] = mm(place_row, ds_scr[mb, h]).astype(BF16)
        for r in range(GRID):
            block = jnp.concatenate(
                [dw_scr[h, CODE * r : CODE * (r + 1)] for h in range(heads)], axis=0
            )
            total = total + mm(block, ladder[CODE * r : CODE * r + WIDE], NT)
    for h in range(heads):
        for at in range(WIDE // 128):
            wide_ref[at, pl.ds(h, CODE, stride=height), :] = total[
                h * CODE : (h + 1) * CODE, at * 128 : (at + 1) * 128
            ]
    high, rest = split_two(
        jnp.concatenate([wide_ref[at] for at in range(WIDE // 128)], axis=1)
    )
    turned = mm(high, spread) + mm(rest, spread)
    result = jnp.zeros((height, flat), F32)
    for c in range(GRID):
        result = result + pltpu.roll(
            turned[c * height : (c + 1) * height, :], GRID - 1 - c, 1
        )
    out_ref[...] = result


def table_grad(grid_rows, grid_cols, score_grads, rel):
    micro_count, heads, length, _ = score_grads.shape
    flat = -(-rel // 128) * 128
    height = -(-heads // 8) * 8
    return pl.pallas_call(
        table_grad_kernel,
        out_shape=jax.ShapeDtypeStruct((height, flat), F32),
        in_specs=[pl.BlockSpec(memory_space=pltpu.SMEM)] * 2
        + [pl.BlockSpec(memory_space=pl.ANY)],
        scratch_shapes=[
            pltpu.VMEM(score_grads.shape, BF16),
            pltpu.VMEM((heads, 256, length), BF16),
            pltpu.VMEM((WIDE // 128, CODE * height, 128), F32),
            pltpu.SemaphoreType.DMA((micro_count,)),
        ],
        compiler_params=pltpu.CompilerParams(vmem_limit_bytes=VMEM_BYTES),
        cost_estimate=BRIEF,
        name="table_grad",
    )(grid_rows, grid_cols, score_grads)


SIDES = ("h", "o", "h2", "z", "act")
HELD = ("p", "wt", "br", "m", "dg", "fd")
GRADS = ("df", "du", "db", "ds", "dp", "dx", "sums")
WEIGHTS = ("qkv", "proj", "up", "down")
VECTORS = (
    "n1_gain",
    "n1_shift",
    "query_bias",
    "value_bias",
    "proj_shift",
    "attn_gain",
    "n2_gain",
    "n2_shift",
    "up_shift",
    "down_shift",
    "mlp_gain",
)
SUM_ROWS = 16
FORWARD, BACKWARD, BOTH = "forward", "backward", "both"


def layer_shapes(micro_count, length, width, hidden, heads):
    row = (micro_count, length, width)
    return {
        "h": (row, BF16),
        "p": ((micro_count, length, 3 * width), BF16),
        "wt": ((micro_count, heads, length, length), BF16),
        "o": (row, BF16),
        "br": (row, BF16),
        "m": (row, F32),
        "h2": (row, BF16),
        "dg": ((micro_count, length, hidden), BF16),
        "z": ((micro_count, length, hidden), BF16),
        "fd": (row, BF16),
        "act": (row, BF16),
        "df": (row, BF16),
        "du": ((micro_count, length, hidden), BF16),
        "db": (row, BF16),
        "ds": ((micro_count, heads, length, length), BF16),
        "dp": ((micro_count, length, 3 * width), BF16),
        "dx": (row, F32),
        "sums": ((SUM_ROWS, width), F32),
    }


def named(vec):
    return types.SimpleNamespace(**{name: vec[name] for name in VECTORS if name in vec})


def forward_body(mb, rows_ref, cols_ref, vec, wide_scr, x_scr, w, scr, tools, wait, keep):
    bias_scr, ladder_scr, score_scr = tools
    vec = named(vec)
    length, width = x_scr.shape
    heads = scr["wt"].shape[0]
    hidden = scr["z"].shape[1]
    head_dim = width // heads
    pair = 2 * head_dim
    owner_col, code_col, _ = pack_places(rows_ref, cols_ref, mb, (length, 1), 0)
    owner_row, code_row, _ = pack_places(rows_ref, cols_ref, mb, (1, length), 1)
    lanes = ramp((length, 256), 1)
    place_col = jnp.where(
        (lanes == code_col) | (lanes == owner_col + PLACES), 1.0, 0.0
    ).astype(BF16)
    place_col = jnp.concatenate([place_col, place_col], axis=1)
    reach = CODE * (GRID - 1)
    ladder_scr[...] = onehot(code_row + reach, ladder_scr.shape, 0)
    spare = ramp((256 - PLACES, length), 0)
    walls = jnp.where(spare == owner_row, 0.0, NEG).astype(BF16)
    blank = jnp.zeros((256 - PLACES, length), BF16)
    for h in range(heads):
        bias_scr[h, PLACES:256, :] = walls
        bias_scr[h, 256 + PLACES :, :] = blank
    wait("wide")
    for r in range(GRID):
        begin = CODE * (GRID - 1 - r)
        low = begin // 128 * 128
        high = -(-(begin + PLACES) // 128) * 128
        rung = ladder_scr[CODE * r + low : CODE * r + high, :]
        block = mm(
            wide_scr[:, :, :, low:high].reshape(2 * heads * CODE, high - low), rung
        ).astype(BF16)
        for part in range(2):
            at = 256 * part + CODE * r
            for h in range(heads):
                top = (part * heads + h) * CODE
                bias_scr[h, at : at + CODE, :] = block[top : top + CODE]

    wait("x")
    hat, _ = unit_rows(x_scr[...].astype(F32))
    scr["h"][...] = (hat * vec.n1_gain[...] + vec.n1_shift[...]).astype(BF16)
    keep("h")

    scale = head_dim ** (-0.5)
    h_all = scr["h"][...]
    p_scr = scr["p"]
    wait("qkv")
    p_scr[:, :width] = (
        (mm(h_all, w["qkv"][:, :width]) + vec.query_bias[...]).astype(BF16) * scale
    ).astype(BF16)
    p_scr[:, width : 2 * width] = mm(h_all, w["qkv"][:, width : 2 * width]).astype(BF16)
    p_scr[:, 2 * width :] = (
        mm(h_all, w["qkv"][:, 2 * width :]) + vec.value_bias[...]
    ).astype(BF16)
    keep("p")

    first = ramp((length, pair), 1) < head_dim
    zero = jnp.zeros((length, pair), BF16)
    for head in range(heads):
        at = head // 2 * pair
        queries = p_scr[:, at : at + pair]
        keys_all = p_scr[:, width + at : width + at + pair]
        own = jnp.where(first == (head % 2 == 0), queries, zero)
        score_scr[head] = mm(own, keys_all, NT) + mm(place_col, bias_scr[head])
    for head in range(heads):
        for at in range(0, length, 64):
            scores = score_scr[head, at : at + 64]
            raised = jnp.exp(scores - jnp.max(scores, axis=-1, keepdims=True))
            share = 1.0 / jnp.sum(raised, axis=-1, keepdims=True)
            scr["wt"][head, at : at + 64] = (raised * share).astype(BF16)
    keep("wt")
    for head in range(0, heads, 2):
        at = head // 2 * pair
        values_all = p_scr[:, 2 * width + at : 2 * width + at + pair]
        even, odd = jnp.where(first, values_all, zero), jnp.where(first, zero, values_all)
        mixed = mm(scr["wt"][head], even) + mm(scr["wt"][head + 1], odd)
        scr["o"][:, at : at + pair] = mixed.astype(BF16)
    keep("o")

    wait("proj")
    branch = mm(scr["o"][...], w["proj"][...]) + vec.proj_shift[...]
    scr["br"][...] = branch.astype(BF16)
    keep("br")
    middle = x_scr[...].astype(F32) + vec.attn_gain[...] * branch
    scr["m"][...] = middle
    keep("m")
    hat, _ = unit_rows(middle)
    scr["h2"][...] = (hat * vec.n2_gain[...] + vec.n2_shift[...]).astype(BF16)
    keep("h2")

    wait("up")
    wait("down")
    second = scr["h2"][...]
    tile = width
    down = None
    for at in range(0, hidden, tile):
        upward = mm(second, w["up"][:, at : at + tile]) + vec.up_shift[:, at : at + tile]
        cdf, leaning = normal_parts(upward)
        z = (upward * cdf).astype(BF16)
        scr["z"][:, at : at + tile] = z
        scr["dg"][:, at : at + tile] = (cdf + leaning).astype(BF16)
        for name in ("z", "dg"):
            keep(name, slice(None), pl.ds(at, tile))
        term = mm(z, w["down"][at : at + tile, :])
        down = term if down is None else down + term
    downward = down + vec.down_shift[...]
    scr["act"][...] = (scr["m"][...] + vec.mlp_gain[...] * downward).astype(BF16)
    keep("send")
    keep("act")
    scr["fd"][...] = downward.astype(BF16)
    keep("fd")


def backward_body(adds, kept, vec, g_scr, x_scr, w, got, scr, tools, wait, keep):
    do_scr, dwt_scr, send_scr = tools
    vec = named(vec)
    length, width = x_scr.shape
    heads = got["wt"].shape[0]
    hidden = got["dg"].shape[1]
    head_dim = width // heads
    pair = 2 * head_dim

    def total(values):
        return jnp.sum(values, axis=0, keepdims=True)

    sums = scr["sums"]

    def note(row, values):
        if adds:
            values = values + sums[row : row + 1, :]
        sums[row : row + 1, :] = values

    wait("sums")
    wait("g")
    grad_out = g_scr[...].astype(F32) * kept
    wait("fd")
    note(9, total(grad_out * got["fd"][...].astype(F32)))
    df = (grad_out * vec.mlp_gain[...]).astype(BF16)
    scr["df"][...] = df
    keep("df")
    note(8, total(df.astype(F32)))

    tile = width
    dh2 = None
    for at in range(0, hidden, tile):
        wait("down%d" % at)
        wait("dg%d" % at)
        wait("up%d" % at)
        dz = mm(scr["df"][...], w["down"][at : at + tile, :], NT)
        du = (dz * got["dg"][:, at : at + tile].astype(F32)).astype(BF16)
        scr["du"][:, at : at + tile] = du
        keep("du", slice(None), pl.ds(at, tile))
        note(10 + at // tile, total(du.astype(F32)))
        term = mm(du, w["up"][:, at : at + tile], NT)
        dh2 = term if dh2 is None else dh2 + term
    for row in range(10 + hidden // tile, SUM_ROWS):
        sums[row : row + 1, :] = jnp.zeros((1, width), F32)

    wait("m")
    hat, inverse = unit_rows(got["m"][...])
    note(6, total(dh2 * hat))
    note(7, total(dh2))
    dm = g_scr[...].astype(F32) * kept + norm_back(dh2 * vec.n2_gain[...], hat, inverse)
    scr["dx"][...] = dm
    wait("br")
    note(5, total(dm * got["br"][...].astype(F32)))
    db = (dm * vec.attn_gain[...]).astype(BF16)
    scr["db"][...] = db
    keep("db")
    note(4, total(db.astype(F32)))

    wait("proj")
    do_scr[...] = mm(scr["db"][...], w["proj"][...], NT).astype(BF16)
    wait("p")
    wait("wt")
    first = ramp((length, pair), 1) < head_dim
    zero = jnp.zeros((length, pair), BF16)
    scale = head_dim ** (-0.5)
    p_scr, dp_scr = got["p"], scr["dp"]
    for head in range(heads):
        at = head // 2 * pair
        own = jnp.where(first == (head % 2 == 0), do_scr[:, at : at + pair], zero)
        dwt_scr[head] = mm(own, p_scr[:, 2 * width + at : 2 * width + at + pair], NT)
    for head in range(heads):
        for at in range(0, length, 64):
            dwt = dwt_scr[head, at : at + 64]
            probs = got["wt"][head, at : at + 64].astype(F32)
            inner = jnp.sum(probs * dwt, axis=-1, keepdims=True)
            scr["ds"][head, at : at + 64] = (probs * (dwt - inner)).astype(BF16)
    keep("ds")
    for head in range(0, heads, 2):
        at = head // 2 * pair
        queries = p_scr[:, at : at + pair]
        keys_all = p_scr[:, width + at : width + at + pair]
        dout = do_scr[:, at : at + pair]
        sides = (scr["ds"], keys_all, NN), (scr["ds"], queries, TN), (got["wt"], dout, TN)
        for part, (left, right, dims) in enumerate(sides):
            even, odd = jnp.where(first, right, zero), jnp.where(first, zero, right)
            merged = mm(left[head], even, dims) + mm(left[head + 1], odd, dims)
            if part == 0:
                merged = merged * scale
            dp_scr[:, part * width + at : part * width + at + pair] = merged.astype(BF16)
    keep("dp")

    wait("qkv")
    dh = mm(dp_scr[...], w["qkv"][...], NT)
    wait("x")
    hat, inverse = unit_rows(x_scr[...].astype(F32))
    dx = scr["dx"][...] + norm_back(dh * vec.n1_gain[...], hat, inverse)
    send_scr[...] = dx.astype(BF16)
    keep("send")
    scr["dx"][...] = dx
    keep("dx")
    note(0, total(dh * hat))
    note(1, total(dh))
    note(2, total(dp_scr[:, :width].astype(F32)))
    note(3, total(dp_scr[:, 2 * width :].astype(F32)))
    keep("sums")


def layer_kernel(section, mb, kind, adds, layout, *refs):
    groups = [dict() for _ in layout]
    for group, names in zip(groups, layout):
        group.update(zip(names, refs))
        refs = refs[len(names) :]
    given, outs, own = groups
    sec_ref, rows_ref, cols_ref = [given[name] for name in ("sec", "rows", "cols")]
    length, width = own["x"].shape

    @pl.when(sec_ref[0] == section)
    def _():
        loads, stores = {}, []

        def wait(name):
            if name in loads:
                loads.pop(name).wait()

        def keep(name, *piece):
            if name not in outs:
                return
            dst = outs[name]
            if name == "send":
                src = own["send"] if kind != FORWARD else own["act"]
            else:
                src = own[name]
                dst = dst if name == "sums" else dst.at[mb]
            if piece:
                src, dst = src.at[piece], dst.at[piece]
            store = pltpu.make_async_copy(src, dst, own["out_sem"].at[len(stores)])
            store.start()
            stores.append(store)

        order = []
        x_src = given["x"] if section else given["x"].at[mb]
        hidden = own["dg"].shape[1]
        if kind != BACKWARD:
            order += [("wide", given["wide"], own["wide"]), ("x", x_src, own["x"])]
            order += [(name, given[name].at[0], own[name]) for name in WEIGHTS]
        if kind != FORWARD:
            if adds:
                order.append(("sums", outs["sums"], own["sums"]))
            order.append(("g", given["g"].at[mb] if section else given["g"], own["g"]))
        if kind == BACKWARD:
            order.append(("fd", given["fd"].at[mb], own["fd"]))
            for at in range(0, hidden, width):
                strip, piece = pl.ds(at, width), (slice(None), pl.ds(at, width))
                order += [
                    ("down%d" % at, given["down"].at[0].at[strip], own["down"].at[strip]),
                    ("dg%d" % at, given["dg"].at[mb].at[piece], own["dg"].at[piece]),
                    ("up%d" % at, given["up"].at[0].at[piece], own["up"].at[piece]),
                ]
            order += [
                ("m", given["m"].at[mb], own["m"]),
                ("br", given["br"].at[mb], own["br"]),
                ("proj", given["proj"].at[0], own["proj"]),
                ("p", given["p"].at[mb], own["p"]),
                ("wt", given["wt"].at[mb], own["wt"]),
                ("qkv", given["qkv"].at[0], own["qkv"]),
                ("x", x_src, own["x"]),
            ]
        for place, (name, src, dst) in enumerate(order):
            loads[name] = pltpu.make_async_copy(src, dst, own["in_sem"].at[place])
            loads[name].start()
        if kind != BACKWARD:
            tools = (own["bias"], own["ladder"], own["score"])
            forward_body(
                mb, rows_ref, cols_ref, given, own["wide"], own["x"], own, own, tools, wait, keep
            )
        if kind != FORWARD:
            kept = 1.0
            if section:
                _, _, inside = pack_places(rows_ref, cols_ref, mb, (length, 1), 0)
                kept = jnp.where(inside, 1.0, 0.0)
            tools = (own["do"], own["score"], own["send"])
            backward_body(
                adds, kept, given, own["g"], own["x"], own, own, own, tools, wait, keep
            )
        for store in stores:
            store.wait()


def run_layer(section, mb, kind, adds, inputs, vectors, weights, prior):
    smem = pl.BlockSpec(memory_space=pltpu.SMEM)
    vmem = pl.BlockSpec(memory_space=pltpu.VMEM)
    hbm = pl.BlockSpec(memory_space=pl.ANY)
    length, width = inputs["x"].shape[-2:]
    micro_count = inputs["rows"].shape[0]
    hidden = weights["up"].shape[2]
    heads = inputs["heads"]
    inputs = {name: array for name, array in inputs.items() if name != "heads"}
    shapes = layer_shapes(micro_count, length, width, hidden, heads)
    results = []
    if kind != BACKWARD:
        results += SIDES
    if kind == FORWARD:
        results += HELD
    if kind != FORWARD:
        results += GRADS
    out_shape = [jax.ShapeDtypeStruct(*shapes[name]) for name in results]
    sends = kind == FORWARD or section == 1
    if sends:
        results.append("send")
        out_shape.append(jax.ShapeDtypeStruct((length, width), BF16))
    operands = {**inputs, **vectors, **weights}
    specs = []
    for name in operands:
        specs.append(smem if name in ("sec", "rows", "cols") else vmem if name in VECTORS else hbm)
    held = [name for name in results if name in prior]
    operands_all = {**operands, **{"prior " + name: prior[name] for name in held}}
    block = lambda name: pltpu.VMEM(shapes[name][0][1:], shapes[name][1])
    scratch = {"x": pltpu.VMEM((length, width), BF16)}
    for name in WEIGHTS:
        scratch[name] = pltpu.VMEM(weights[name].shape[1:], BF16)
    for name in HELD:
        scratch[name] = block(name)
    scratch["score"] = pltpu.VMEM((heads, length, length), F32)
    if kind != BACKWARD:
        for name in SIDES:
            scratch[name] = block(name)
        scratch["wide"] = pltpu.VMEM(inputs["wide"].shape, BF16)
        scratch["bias"] = pltpu.VMEM((heads, 512, length), BF16)
        scratch["ladder"] = pltpu.VMEM((CODE * (GRID - 1) + WIDE, length), BF16)
    if kind != FORWARD:
        for name in GRADS[:-1]:
            scratch[name] = block(name)
        scratch["sums"] = pltpu.VMEM((SUM_ROWS, width), F32)
        for name in ("g", "do", "send"):
            scratch[name] = pltpu.VMEM((length, width), BF16)
    scratch["in_sem"] = pltpu.SemaphoreType.DMA((10 + 3 * (hidden // width),))
    scratch["out_sem"] = pltpu.SemaphoreType.DMA((len(results) + 2 * (hidden // width),))
    layout = (list(operands_all), results, list(scratch))
    made = pl.pallas_call(
        functools.partial(layer_kernel, section, mb, kind, adds, layout),
        out_shape=out_shape,
        in_specs=specs + [hbm] * len(held),
        out_specs=[hbm] * len(results),
        scratch_shapes=list(scratch.values()),
        input_output_aliases={
            len(operands) + at: results.index(name) for at, name in enumerate(held)
        },
        compiler_params=pltpu.CompilerParams(vmem_limit_bytes=VMEM_BYTES),
        cost_estimate=BRIEF,
        name="layer_" + kind,
    )(*operands_all.values())
    return dict(zip(results, made))


def turn_kernel(chunk_count, *refs):
    count = len(refs) // 4
    sources, outs, refs = refs[:count], refs[count : 2 * count], refs[2 * count :]
    lefts, turned, refs = refs[:count], refs[count : 2 * count], refs[2 * count :]
    in_sem, out_sem = refs
    loads = [
        pltpu.make_async_copy(src, dst, in_sem.at[at])
        for at, (src, dst) in enumerate(zip(sources, lefts))
    ]
    stores = [
        pltpu.make_async_copy(src, dst, out_sem.at[at])
        for at, (src, dst) in enumerate(zip(turned, outs))
    ]
    for load in loads:
        load.start()
    for left, out, load, store in zip(lefts, turned, loads, stores):
        load.wait()
        micro_count, length, width = left.shape
        step = width // chunk_count
        strip = 256 if width % 256 == 0 else width
        for mb in range(micro_count):
            flipped = jnp.concatenate(
                [left[mb, :, at : at + strip].T for at in range(0, width, strip)], axis=0
            )
            for chunk in range(chunk_count):
                core_of, to = chunk % 2, chunk // 2 * step
                out[core_of, to : to + step, mb * length : (mb + 1) * length] = flipped[
                    chunk * step : (chunk + 1) * step, :
                ]
        store.start()
    for store in stores:
        store.wait()


def turn_lefts(chunk_count, lefts):
    hbm = pl.BlockSpec(memory_space=pl.ANY)
    shapes = [(2, left.shape[2] // 2, left.shape[0] * left.shape[1]) for left in lefts]
    return pl.pallas_call(
        functools.partial(turn_kernel, chunk_count),
        out_shape=[jax.ShapeDtypeStruct(shape, BF16) for shape in shapes],
        in_specs=[hbm] * len(lefts),
        out_specs=[hbm] * len(lefts),
        scratch_shapes=[pltpu.VMEM(left.shape, BF16) for left in lefts]
        + [pltpu.VMEM(shape, BF16) for shape in shapes]
        + [pltpu.SemaphoreType.DMA((len(lefts),))] * 2,
        compiler_params=pltpu.CompilerParams(vmem_limit_bytes=VMEM_BYTES),
        cost_estimate=BRIEF,
        name="turn_lefts",
    )(*lefts)


def placed(chunk, order):
    place = 0
    for bit in order:
        place = 2 * place + (chunk >> (bit - 1) & 1)
    return place


def weight_kernel(parts, fresh, orders, sides, sec_ref, *refs):
    operands, refs = refs[: 2 * parts], refs[2 * parts :]
    if fresh:
        (grad_hbm, gain_ref), refs = refs[:2], refs[2:]
    count = len(sides)
    outs, refs = refs[:count], refs[count:]
    lefts, rights, refs = refs[:parts], refs[parts : 2 * parts], refs[2 * parts :]
    scrs, (in_sem, out_sem), refs = refs[:count], refs[count : count + 2], refs[count + 2 :]
    halves = [sec_ref[1] if side else 1 - sec_ref[1] for side in sides]
    strip = 384
    loads = []
    for part in range(parts):
        pairs = [(operands[2 * part + 1], rights[part])]
        for which, half in enumerate(halves):
            for low in range(0, lefts[part].shape[1], strip):
                rows = pl.ds(low, strip)
                pairs.append(
                    (operands[2 * part].at[half].at[rows], lefts[part].at[which].at[rows])
                )
        loads.append([])
        for kind, (src, dst) in enumerate(pairs):
            load = pltpu.make_async_copy(src, dst, in_sem.at[part, kind])
            load.start()
            loads[part].append(load)
    if fresh:
        grad_scr = refs[0]
        grad_copy = pltpu.make_async_copy(grad_hbm, grad_scr, in_sem.at[parts, 0])
        grad_copy.start()
        grad_copy.wait()
        loads[0][0].wait()

        @pl.when(sec_ref[0] == 0)
        def _():
            rights[0][rights[0].shape[0] - 1] = (grad_scr[...].astype(F32) * gain_ref[...]).astype(BF16)

    stores = []
    unit = scrs[0].shape[2]
    tile = min(768, unit)
    for which in range(count):
        at_col = 0
        for part in range(parts):
            if which == 0 and not fresh:
                loads[part][0].wait()
            micro_count, length, cols = rights[part].shape
            height = lefts[part].shape[1]
            pieces = height // strip
            for at in range(0, cols, tile):
                right = rights[part][:, :, at : at + tile].reshape(micro_count * length, tile)
                cut, place = divmod(at_col + at, unit)
                step = height >> len(orders[cut])
                for low in range(0, height, strip):
                    if at == 0:
                        loads[part][1 + which * pieces + low // strip].wait()
                    block = mm(lefts[part][which, low : low + strip], right).astype(BF16)
                    for top in range(0, strip, step):
                        to = step * placed((low + top) // step, orders[cut])
                        scrs[which][cut, to : to + step, place : place + tile] = block[
                            top : top + step
                        ]
                piece = (slice(None), pl.ds(place, tile))
                store = pltpu.make_async_copy(
                    scrs[which].at[cut].at[piece],
                    outs[which].at[cut].at[piece],
                    out_sem.at[len(stores)],
                )
                store.start()
                stores.append(store)
            at_col += cols
    for store in stores:
        store.wait()


def weight_terms(orders, sides, sec, pairs, fresh=()):
    hbm = pl.BlockSpec(memory_space=pl.ANY)
    vmem = pl.BlockSpec(memory_space=pltpu.VMEM)
    smem = pl.BlockSpec(memory_space=pltpu.SMEM)
    height = pairs[0][0].shape[1]
    cuts = len(orders)
    unit = sum(right.shape[2] for _, right in pairs) // cuts
    tiles = -(-unit // min(768, unit)) * cuts * len(sides)
    operands = [side for pair in pairs for side in pair]
    scratch = [pltpu.VMEM((len(sides), *left.shape[1:]), BF16) for left, _ in pairs]
    scratch += [pltpu.VMEM(right.shape, BF16) for _, right in pairs]
    scratch += [pltpu.VMEM((cuts, height, unit), BF16) for _ in sides]
    scratch += [
        pltpu.SemaphoreType.DMA((len(pairs) + 1, 1 + 2 * (height // 384))),
        pltpu.SemaphoreType.DMA((tiles,)),
    ]
    if fresh:
        scratch.append(pltpu.VMEM(fresh[0].shape, BF16))
    return pl.pallas_call(
        functools.partial(weight_kernel, len(pairs), bool(fresh), orders, sides),
        out_shape=[jax.ShapeDtypeStruct((cuts, height, unit), BF16) for _ in sides],
        in_specs=[smem] + [hbm] * len(operands) + ([hbm, vmem] if fresh else []),
        out_specs=[hbm] * len(sides),
        scratch_shapes=scratch,
        compiler_params=pltpu.CompilerParams(vmem_limit_bytes=VMEM_BYTES),
        cost_estimate=BRIEF,
        name="weight_terms",
    )(sec, *operands, *fresh)


def swap(block, bit):
    devices = range(lax.axis_size("dp"))
    return lax.ppermute(block, "dp", [(i, i ^ bit) for i in devices])


def after(value, *others):
    return lax.optimization_barrier((value, *others))[0]


def half_of(block, side):
    block = block.reshape(2, block.shape[0] // 2, block.shape[1])
    return lax.dynamic_index_in_dim(block, side, 0, keepdims=False)


def total_of(blocks):
    return functools.reduce(jnp.add, [block.astype(F32) for block in blocks])


def next_sum(mine, come, order, rank):
    side = (rank >> order[0]) & 1
    sent = total_of([half_of(mine, 1 - side), half_of(come, 1 - side)]).astype(BF16)
    kept = total_of([half_of(mine, side), half_of(come, side)]).astype(BF16)
    come = swap(sent, 1 << order[0])
    return lax.optimization_barrier(kept), come, order[1:], sent


def full_sum(values):
    size = lax.axis_size("dp")
    if size & (size - 1):
        return lax.psum(values, "dp")
    bit = 1
    while bit < size:
        values = values + swap(values, bit)
        bit *= 2
    return values


def shards(
    patches_in,
    grid_rows,
    grid_cols,
    norm1_gain,
    norm1_bias,
    qkv_weight,
    q_bias,
    v_bias,
    rel_table,
    proj_weight,
    proj_bias,
    attn_scale,
    norm2_gain,
    norm2_bias,
    fc1_weight,
    fc1_bias,
    fc2_weight,
    fc2_bias,
    mlp_scale,
    cotangent,
):
    rank = lax.axis_index("dp")
    dp_size = lax.axis_size("dp")
    micro_count, length, width = patches_in.shape
    hidden = fc1_bias.shape[1]
    rel, heads = rel_table.shape[1:]
    sec = jnp.stack([lax.axis_index("section"), rank % 2]).astype(jnp.int32)
    weights = dict(zip(WEIGHTS, (qkv_weight, proj_weight, fc1_weight, fc2_weight)))
    vectors = dict(
        zip(
            VECTORS,
            (
                norm1_gain,
                norm1_bias,
                q_bias,
                v_bias,
                proj_bias,
                attn_scale,
                norm2_gain,
                norm2_bias,
                fc1_bias,
                fc2_bias,
                mlp_scale,
            ),
        )
    )
    common = {"sec": sec, "rows": grid_rows, "cols": grid_cols, "heads": heads}
    wide = table_spread(rel_table)

    cache, grads = {}, {}
    moved, returned = [], []
    for mb in range(micro_count):
        inputs = {**common, "x": patches_in, "wide": wide}
        cache = run_layer(0, mb, FORWARD, False, inputs, vectors, weights, cache)
        moved.append(lax.ppermute(cache.pop("send"), "section", [(0, 1)]))
    for mb in range(micro_count):
        inputs = {**common, "x": moved[mb], "wide": wide, "g": cotangent}
        made = run_layer(1, mb, BOTH, mb > 0, inputs, vectors, weights, {**cache, **grads})
        returned.append(lax.ppermute(made.pop("send"), "section", [(1, 0)]))
        cache.update({name: made[name] for name in SIDES})
        grads = {name: made[name] for name in GRADS}

    def backward(mb, grad, prior):
        inputs = {**common, "x": patches_in, "g": grad}
        inputs.update({name: cache[name] for name in HELD})
        return run_layer(0, mb, BACKWARD, mb > 0, inputs, vectors, weights, prior)

    spread_out = dp_size == 16 and width % (16 * dp_size) == 0
    if spread_out:
        lefts = [after(cache[name], grads["dx"]) for name in ("z", "h2", "o", "h")]
        z_turned, h2_turned, o_turned, h_turned = turn_lefts(dp_size, lefts)
    for mb in range(micro_count - 1):
        grads = backward(mb, returned[mb], grads)
    last = returned[-1]
    if spread_out:
        one, two = (1, 2, 3), (2, 1, 3)

        def paired(send, keep, orders):
            got = swap(send, 1)
            return [(keep[cut], got[cut], order, None) for cut, order in enumerate(orders)]

        def follow(units, *before):
            done = []
            for mine, come, order, _ in units:
                done.append(next_sum(mine, after(come, *before), order, rank))
            return done

        def moving(units):
            return [sent for _, _, _, sent in units]

        def ended(units, *before):
            return jnp.concatenate(
                [total_of([mine, after(come, *before)]) for mine, come, _, _ in units], axis=1
            )

        down_orders, attn_orders, up_orders = ((one, two), (one, two), (one, two))
        operands = ([(z_turned, grads["df"])], (last, mlp_scale))
        (send,) = weight_terms(down_orders, (0,), sec, *operands)
        (keep,) = weight_terms(down_orders, (1,), after(sec, send), *operands)
        down = follow(paired(send, keep, down_orders))
        grads = backward(micro_count - 1, after(last, *moving(down)), grads)
        down = follow(down, grads["sums"])
        send, keep = weight_terms(
            attn_orders,
            (0, 1),
            sec,
            [(after(o_turned, *moving(down)), grads["db"]), (h_turned, grads["dp"])],
        )
        attn = paired(send, keep, attn_orders)
        send, keep = weight_terms(
            up_orders, (0, 1), sec, [(after(h2_turned, send), grads["du"])]
        )
        up = paired(send, keep, up_orders)
        attn = follow(attn, send)
        down = follow(down, *moving(attn))
        up = follow(up, *moving(down))
        rev = table_grad(grid_rows, grid_cols, after(grads["ds"], *moving(up)), rel)
        small = jnp.concatenate([grads["sums"], rev], axis=0)
        small = small + swap(small, 1)
        attn = follow(attn, small)
        small = small + swap(after(small, *moving(attn)), 2)
        down_grad = ended(down, small)
        up = follow(up, down_grad)
        small = small + swap(after(small, *moving(up)), 4)
        attn = follow(attn, small)
        small = small + swap(after(small, *moving(attn)), 8)
        up = follow(up, small)
        attn_grad = ended(attn, *moving(up))
        up_grad = ended(up, attn_grad)
        proj_grad, qkv_grad = attn_grad[:, :width], attn_grad[:, width:]
        sums, rev = small[:SUM_ROWS], small[SUM_ROWS:]
    else:
        grads = backward(micro_count - 1, last, grads)

        def plain(left, right):
            term = jnp.einsum("mrk,mrn->kn", left, right, preferred_element_type=F32)
            return lax.psum_scatter(term, "dp", scatter_dimension=0, tiled=True)

        down_grad = plain(cache["z"], grads["df"])
        up_grad = plain(cache["h2"], grads["du"])
        proj_grad = plain(cache["o"], grads["db"])
        qkv_grad = plain(cache["h"], grads["dp"])
        rev = full_sum(table_grad(grid_rows, grid_cols, grads["ds"], rel))
        sums = full_sum(grads["sums"])
    rel_grad = jnp.flip(rev[:heads, :rel].T, 0)
    up_shift_grad = sums[10 : 10 + hidden // width].reshape(1, hidden)
    small = [sums[row : row + 1] for row in range(10)]
    return (
        cache["act"][None],
        grads["dx"][None],
        small[0],
        small[1],
        qkv_grad[None],
        small[2],
        small[3],
        rel_grad[None],
        proj_grad[None],
        small[4],
        small[5],
        small[6],
        small[7],
        up_grad[None],
        up_shift_grad,
        down_grad[None],
        small[8],
        small[9],
    )


def solution(mesh):
    layer_row = P("section", None)
    layer_matrix = P("section", None, None)
    packs = P(None, "dp", None)
    scattered = P("section", "dp", None)
    in_specs = (
        packs,
        packs,
        packs,
        layer_row,
        layer_row,
        layer_matrix,
        layer_row,
        layer_row,
        layer_matrix,
        layer_matrix,
        layer_row,
        layer_row,
        layer_row,
        layer_row,
        layer_matrix,
        layer_row,
        layer_matrix,
        layer_row,
        layer_row,
        packs,
    )
    out_specs = (
        P("section", None, "dp", None),
        P("section", None, "dp", None),
        layer_row,
        layer_row,
        scattered,
        layer_row,
        layer_row,
        layer_matrix,
        scattered,
        layer_row,
        layer_row,
        layer_row,
        layer_row,
        scattered,
        layer_row,
        scattered,
        layer_row,
        layer_row,
    )
    return jax.shard_map(
        shards, mesh=mesh, in_specs=in_specs, out_specs=out_specs, check_vma=False
    )
```
